128 devices in a mesh: lon: 16 (over z, y_lo, core), lat: 8 (over x, y_hi).
Axes of the slice: x: 4, y: 4 (y_hi: 2, y_lo: 2; y = y_hi * 2 + y_lo), z: 4, core: 2. Of those that a mesh axis runs over, the one named last changes fastest.
Arguments:
- tokens: bfloat16 [288, 384, 1024], P('lat', 'lon'), may hold values from -6 to 6
- cotangent: bfloat16 [288, 384, 1024], P('lat', 'lon'), may hold values from -6 to 6
- w_qkv: bfloat16 [1024, 3072], replicated, may hold values from -0.1875 to 0.1875
- w_out: bfloat16 [1024, 1024], replicated, may hold values from -0.1875 to 0.1875
- row_valid: int32 [288], replicated, may hold values from 0 to 1, as said below
Outputs:
- d_tokens: bfloat16 [288, 384, 1024], P('lat', 'lon')
- grad_qkv: float32 [1024, 3072], P(('lon', 'lat'))
- grad_out_t: float32 [1024, 1024], P(('lon', 'lat'))
The draws below stay inside these ranges and needn't reach their ends.
Inputs may be any that keep to these rules, and one draw needn't show every extreme that they name: row_valid is 0 on the first 1 to 3 rows and on the last 1 to 3 rows, and 1 on all other rows.
All inputs are finite; a program needn't handle non-finite values.
Results may differ from the reference program's by a relative error of at most 0.015.
Values may be sent and summed in bfloat16 or wider, within the bound.
A program may use at most 128 MiB of HBM per device.

```python
import math
import jax
import jax.numpy as jnp
from jax import lax

D = 1024
HEADS = 16
WIN = 6
HEAD_DIM = 64
HALF = 3
LAT_TOK = 288
LON_TOK = 384
TOKENS = 110592


def draw_row_valid(key, part):
    key = jax.random.fold_in(key, 7)
    top_key, bottom_key = jax.random.split(key)
    top_rows = jax.random.randint(top_key, (), 1, HALF + 1)
    bottom_rows = jax.random.randint(bottom_key, (), 1, HALF + 1)
    row_index = jnp.arange(LAT_TOK, dtype=jnp.int32)
    return ((row_index >= top_rows) & (row_index < LAT_TOK - bottom_rows)).astype(jnp.int32)


def spiked(values, key, source, target, shards_of, factor):
    owner, partner = [(jnp.arange(values.shape[axis_at]) // (values.shape[axis_at] // shards_of)).reshape([-1 if axis == axis_at else 1 for axis in range(values.ndim)]) for axis_at in (source, target)]
    chosen = jax.random.permutation(key, shards_of)[partner]
    strong = (owner == chosen) | (owner == (partner + shards_of // 2) % shards_of)
    return jnp.where(strong, factor * values, values)


def steps_of(rng, extent, cuts, low, largest):
    def one(axis_at, blocks):
        heights = jax.random.uniform(jax.random.fold_in(jax.random.fold_in(rng, 6), axis_at), (blocks,), jnp.float32, low / len(cuts), largest / len(cuts))
        return jnp.repeat(jnp.exp(heights), extent[axis_at] // blocks).reshape((-1,) + (1,) * (len(extent) - axis_at - 1))

    level = one(*cuts[0])
    for cut in cuts[1:]:
        level = level * one(*cut)
    return level


def bell_draw(rng, shape, spread, limit, cuts=(), kind=jnp.bfloat16):
    array = spread * jax.random.normal(rng, shape, jnp.float32)
    if cuts:
        array = array * steps_of(rng, shape, cuts, -0.22, 0.18)
    return jnp.clip(array, -limit, limit).astype(kind)


def heavy_noise(rng, shape, scale, bound, cuts, heavy, kind=jnp.bfloat16):
    entries = scale * jax.random.normal(rng, shape, jnp.float32)
    if cuts:
        entries = entries * steps_of(rng, shape, cuts, -0.22, 0.18)
    return jnp.clip(spiked(entries, jax.random.fold_in(rng, 3), *heavy), -bound, bound).astype(kind)


def setup_inputs(seed: int = 0) -> dict:
    splits = jax.random.split(jax.random.key(seed), 6)
    tokens = heavy_noise(splits[0], (LAT_TOK, LON_TOK, D), 1.0, 6.0, ((0, 8), (1, 16)), (0, 2, 8, 2.0))
    cotangent = heavy_noise(splits[1], (LAT_TOK, LON_TOK, D), 1.0, 6.0, ((0, 8), (1, 16)), (1, 2, 16, 2.0))
    w_qkv = bell_draw(splits[2], (D, 3 * D), D ** -0.5, 0.1875)
    w_out = bell_draw(splits[3], (D, D), D ** -0.5, 0.1875)
    row_valid = draw_row_valid(jax.random.fold_in(splits[5], 71), 0)
    return {"tokens": tokens, "cotangent": cotangent, "w_qkv": w_qkv, "w_out": w_out, "row_valid": row_valid}


COSINE_SHARPNESS = 10.0
EPSILON = 1e-06

def window_core(x_win, dy_win, wrap_win, valid_win, w_qkv, w_out):
    win_count, win_area, feature_dim = x_win.shape
    x_float = x_win.reshape(win_count * win_area, feature_dim).astype(jnp.float32)
    inv_rms = lax.rsqrt(lax.optimization_barrier(jnp.mean(x_float * x_float, axis=-1, keepdims=True)) + EPSILON)
    normed = (x_float * inv_rms).astype(jnp.bfloat16)
    qkv_all = jnp.dot(normed, w_qkv, preferred_element_type=jnp.float32).astype(jnp.bfloat16)
    split_heads = qkv_all.reshape(win_count, win_area, 3, HEADS, HEAD_DIM)
    queries = split_heads[:, :, 0].astype(jnp.float32)
    keys_raw = split_heads[:, :, 1].astype(jnp.float32)
    values = split_heads[:, :, 2].astype(jnp.float32)
    inv_q = lax.rsqrt(lax.optimization_barrier(jnp.sum(queries * queries, axis=-1, keepdims=True)) + EPSILON)
    inv_k = lax.rsqrt(lax.optimization_barrier(jnp.sum(keys_raw * keys_raw, axis=-1, keepdims=True)) + EPSILON)
    q_unit = queries * inv_q
    k_unit = keys_raw * inv_k
    query_lowprec = q_unit.astype(jnp.bfloat16).astype(jnp.float32)
    key_lowprec = k_unit.astype(jnp.bfloat16).astype(jnp.float32)
    position = jnp.arange(win_area, dtype=jnp.int32)
    itself = position[:, None] == position[None, :]
    permitted_pairs = (wrap_win[:, :, None] == wrap_win[:, None, :]) & (valid_win[:, None, :] | itself[None])
    similarity_scores = COSINE_SHARPNESS * jnp.einsum('sfxe,sqxe->sxfq', query_lowprec, key_lowprec)
    unmasked_weights = jnp.where(permitted_pairs[:, None], jnp.exp(similarity_scores - COSINE_SHARPNESS), 0.0)
    probabilities = unmasked_weights / lax.optimization_barrier(jnp.sum(unmasked_weights, axis=-1, keepdims=True))
    prob_round = probabilities.astype(jnp.bfloat16).astype(jnp.float32)
    attended = jnp.einsum('mxon,mnxq->moxq', prob_round, values).astype(jnp.bfloat16)
    attended = attended.reshape(win_count * win_area, feature_dim)
    dy_flat = dy_win.reshape(win_count * win_area, feature_dim)
    d_att = jnp.dot(dy_flat, w_out.T, preferred_element_type=jnp.float32).astype(jnp.bfloat16)
    d_heads = d_att.reshape(win_count, win_area, HEADS, HEAD_DIM).astype(jnp.float32)
    d_probs = jnp.einsum('sfxe,sqxe->sxfq', d_heads, values)
    d_values = jnp.einsum('vfns,vnfp->vsfp', prob_round, d_heads).astype(jnp.bfloat16)
    d_scores = probabilities * (d_probs - lax.optimization_barrier(jnp.sum(probabilities * d_probs, axis=-1, keepdims=True)))
    grad_scores_lowprec = d_scores.astype(jnp.bfloat16).astype(jnp.float32)
    grad_query_direction = COSINE_SHARPNESS * jnp.einsum('mxon,mnxq->moxq', grad_scores_lowprec, key_lowprec)
    grad_key_direction = COSINE_SHARPNESS * jnp.einsum('vfns,vnfp->vsfp', grad_scores_lowprec, query_lowprec)
    d_queries = (inv_q * (grad_query_direction - q_unit * lax.optimization_barrier(jnp.sum(q_unit * grad_query_direction, axis=-1, keepdims=True)))).astype(jnp.bfloat16)
    d_keys = (inv_k * (grad_key_direction - k_unit * lax.optimization_barrier(jnp.sum(k_unit * grad_key_direction, axis=-1, keepdims=True)))).astype(jnp.bfloat16)
    d_qkv = jnp.stack([d_queries, d_keys, d_values], axis=2).reshape(win_count * win_area, 3 * feature_dim)
    d_normed = jnp.dot(d_qkv, w_qkv.T, preferred_element_type=jnp.float32)
    cubed = inv_rms * inv_rms * inv_rms
    d_input = inv_rms * d_normed - x_float * cubed * lax.optimization_barrier(jnp.mean(d_normed * x_float, axis=-1, keepdims=True))
    d_input = d_input.astype(jnp.bfloat16).reshape(win_count, win_area, feature_dim)
    return (d_input, normed, d_qkv, attended, dy_flat)

def to_windows(field_grid):
    groups = LAT_TOK // WIN
    columns = LON_TOK // WIN
    reshaped = field_grid.reshape((groups, WIN, columns, WIN) + field_grid.shape[2:])
    reordered = jnp.moveaxis(reshaped, 2, 1)
    return reordered.reshape((groups, columns, WIN * WIN) + field_grid.shape[2:])

def reference(tokens, cotangent, w_qkv, w_out, row_valid):
    rolled_x = jnp.roll(tokens, (-HALF, -HALF), axis=(0, 1))
    rolled_dy = jnp.roll(cotangent, (-HALF, -HALF), axis=(0, 1))
    row_index = jnp.arange(LAT_TOK, dtype=jnp.int32)
    anchor = (row_index + HALF) % LAT_TOK
    wrap_rows = anchor < HALF
    valid_rows = jnp.roll(row_valid, -HALF) == 1
    wrap_grid = jnp.broadcast_to(wrap_rows[:, None], (LAT_TOK, LON_TOK))
    valid_grid = jnp.broadcast_to(valid_rows[:, None], (LAT_TOK, LON_TOK))

    def group_step(totals, pieces):
        x_win, dy_win, wrap_win, valid_win = pieces
        d_win, normed, d_qkv, attended, dy_flat = window_core(x_win, dy_win, wrap_win, valid_win, w_qkv, w_out)
        grad_q = totals[0] + jnp.dot(normed.T, d_qkv, preferred_element_type=jnp.float32)
        grad_o = totals[1] + jnp.dot(dy_flat.T, attended, preferred_element_type=jnp.float32)
        return ((grad_q, grad_o), d_win)
    start_totals = (jnp.zeros((D, 3 * D), jnp.float32), jnp.zeros((D, D), jnp.float32))
    sums, d_wins = lax.scan(group_step, start_totals, (to_windows(rolled_x), to_windows(rolled_dy), to_windows(wrap_grid), to_windows(valid_grid)))
    groups = LAT_TOK // WIN
    columns = LON_TOK // WIN
    d_grid = d_wins.reshape(groups, columns, WIN, WIN, D)
    d_grid = jnp.moveaxis(d_grid, 1, 2).reshape(LAT_TOK, LON_TOK, D)
    d_tokens = jnp.roll(d_grid, (HALF, HALF), axis=(0, 1))
    grad_scale = 1.0 / math.sqrt(TOKENS)
    return (d_tokens, sums[0] * grad_scale, sums[1] * grad_scale)
```

```python
import functools
import math

import jax
import jax.numpy as jnp
from jax import lax
from jax.experimental import pallas as pl
from jax.experimental.pallas import tpu as pltpu
from jax.sharding import PartitionSpec as P

D = 1024
HEADS = 16
WIN = 6
HEAD_DIM = 64
HALF = 3
ROWS = 36
COLS = 24
LOCAL = ROWS * COLS
STRIPS = ROWS // WIN
STRIP = WIN * COLS
GROUP = 256
CHUNKS = D // GROUP
GROUP_HEADS = GROUP // HEAD_DIM
STACK = GROUP_HEADS * STRIP

SHARP = 10.0
LOG2E = math.log2(math.e)
EPSILON = 1e-06
BLOCKED = -1e30

F32 = jnp.float32
BF16 = jnp.bfloat16
MESH = pl.DeviceIdType.MESH
NN = (((1,), (0,)), ((), ()))
NT = (((1,), (1,)), ((), ()))
TN = (((0,), (0,)), ((), ()))


def dot(a, b, dims=NN):
    return lax.dot_general(a, b, dims, preferred_element_type=F32)


def head_sums(t, ones):
    hi = t.astype(BF16)
    lo = (t - hi.astype(F32)).astype(BF16)
    return dot(hi, ones) + dot(lo, ones)


def by_head(t):
    lane = lax.broadcasted_iota(jnp.int32, t.shape, 1) // HEAD_DIM
    zero = jnp.zeros_like(t)
    return jnp.concatenate([jnp.where(lane == h, t, zero) for h in range(GROUP_HEADS)], axis=0)


def pick_heads(t):
    lane = lax.broadcasted_iota(jnp.int32, (STRIP, GROUP), 1) // HEAD_DIM
    out = t[:STRIP]
    for h in range(1, GROUP_HEADS):
        out = jnp.where(lane == h, t[h * STRIP : (h + 1) * STRIP], out)
    return out


def prologue(x, cot, normed, normed_t, cot_t, inv_rms):
    def norm_strip(s, _):
        rows = pl.ds(pl.multiple_of(s * STRIP, 16), STRIP)
        xf = x[rows, :].astype(F32)
        inv = lax.rsqrt(jnp.mean(xf * xf, axis=-1, keepdims=True) + EPSILON)
        inv_rms[rows, :] = inv
        normed[rows, :] = (xf * inv).astype(BF16)
        return 0

    lax.fori_loop(0, STRIPS, norm_strip, 0)
    for at in range(0, LOCAL, 128):
        width = min(128, LOCAL - at)
        normed_t[:, at : at + width] = normed[at : at + width, :].T
        cot_t[:, at : at + width] = cot[at : at + width, :].T


def project(p, cot, w_qkv, w_out, normed, qb, kb, vb, dab):
    def part(i, _):
        rows = pl.ds(pl.multiple_of(i * 432, 16), 432)
        base = pl.multiple_of(p * GROUP, GROUP)
        n = normed[rows, :]
        qb[rows, :] = dot(n, w_qkv[:, pl.ds(base, GROUP)]).astype(BF16)
        kb[rows, :] = dot(n, w_qkv[:, pl.ds(base + D, GROUP)]).astype(BF16)
        vb[rows, :] = dot(n, w_qkv[:, pl.ds(base + 2 * D, GROUP)]).astype(BF16)
        dab[rows, :] = dot(cot[rows, :], w_out[pl.ds(base, GROUP), :], NT).astype(BF16)
        return 0

    lax.fori_loop(0, 2, part, 0)


def attend(p, bias, qb, kb, vb, dab, ob, d_qkv):
    row_head = lax.broadcasted_iota(jnp.int32, (GROUP, GROUP), 0) // HEAD_DIM
    col_head = lax.broadcasted_iota(jnp.int32, (GROUP, GROUP), 1) // HEAD_DIM
    ones = jnp.where(row_head == col_head, 1.0, 0.0).astype(BF16)

    def strip(s, _):
        rows = pl.ds(pl.multiple_of(s * STRIP, 16), STRIP)
        base = pl.multiple_of(p * GROUP, GROUP)
        q = qb[rows, :].astype(F32)
        k = kb[rows, :].astype(F32)
        inv_q = lax.rsqrt(head_sums(q * q, ones) + EPSILON)
        inv_k = lax.rsqrt(head_sums(k * k, ones) + EPSILON)
        q_unit = q * inv_q
        k_unit = k * inv_k
        q_heads = by_head(q_unit.astype(BF16))
        k_round = k_unit.astype(BF16)
        v = vb[rows, :]
        da_heads = by_head(dab[rows, :])
        scores = dot(q_heads, k_round, NT).reshape(GROUP_HEADS, STRIP, STRIP)
        weights = jnp.exp2(scores * (SHARP * LOG2E) + bias[s][None])
        total = jnp.sum(weights, axis=-1, keepdims=True)
        probs = weights * (1.0 / total)
        prob_round = probs.astype(BF16).reshape(STACK, STRIP)
        d_probs = dot(da_heads, v, NT).reshape(GROUP_HEADS, STRIP, STRIP)
        mixed = jnp.sum(probs * d_probs, axis=-1, keepdims=True)
        ds_round = (probs * (d_probs - mixed)).astype(BF16).reshape(STACK, STRIP)
        ob[rows, :] = pick_heads(dot(prob_round, v)).astype(BF16)
        d_qkv[rows, pl.ds(base + 2 * D, GROUP)] = dot(prob_round, da_heads, TN).astype(BF16)
        dq_unit = SHARP * pick_heads(dot(ds_round, k_round))
        dk_unit = SHARP * dot(ds_round, q_heads, TN)
        d_q = inv_q * (dq_unit - q_unit * head_sums(q_unit * dq_unit, ones))
        d_k = inv_k * (dk_unit - k_unit * head_sums(k_unit * dk_unit, ones))
        d_qkv[rows, pl.ds(base, GROUP)] = d_q.astype(BF16)
        d_qkv[rows, pl.ds(base + D, GROUP)] = d_k.astype(BF16)
        return 0

    lax.fori_loop(0, STRIPS, strip, 0)


def weight_terms(p, normed_t, cot_t, d_qkv, ob, terms):
    def plane(z, _):
        rows = pl.ds(pl.multiple_of(z * 256, 256), 256)
        base = pl.multiple_of(p * GROUP, GROUP)
        n = normed_t[rows, :]
        g_q = dot(n, d_qkv[:, pl.ds(base, GROUP)])
        g_k = dot(n, d_qkv[:, pl.ds(base + D, GROUP)])
        g_v = dot(n, d_qkv[:, pl.ds(base + 2 * D, GROUP)])
        g_o = dot(cot_t[rows, :], ob[...])
        for unit in range(32):
            y_lo, core, x, y_hi = unit // 16, unit // 8 % 2, unit // 2 % 4, unit % 2
            y = y_hi * 2 + y_lo
            part = slice(unit * 8, unit * 8 + 8)
            first = jnp.concatenate([g_q[part], g_k[part]], axis=0)
            second = jnp.concatenate([g_v[part], g_o[part]], axis=0)
            terms[p, core, 0, x, y, z] = first.astype(BF16)
            terms[p, core, 1, z, y, x] = second.astype(BF16)
        return 0

    lax.fori_loop(0, 4, plane, 0)


def token_grad(x, w_qkv, d_qkv, inv_rms, d_normed, d_x):
    def columns(n, _):
        cols = pl.ds(pl.multiple_of(n * 256, 256), 256)
        d_normed[:, cols] = dot(d_qkv[...], w_qkv[cols, :], NT)
        return 0

    lax.fori_loop(0, D // 256, columns, 0)

    def strip(s, _):
        rows = pl.ds(pl.multiple_of(s * STRIP, 16), STRIP)
        xf = x[rows, :].astype(F32)
        dn = d_normed[rows, :]
        inv = inv_rms[rows, :]
        pull = jnp.mean(dn * xf, axis=-1, keepdims=True) * (inv * inv * inv)
        d_x[rows, :] = (inv * dn - xf * pull).astype(BF16)
        return 0

    lax.fori_loop(0, STRIPS, strip, 0)


def window_kernel(x, cot, w_qkv, w_out, bias, d_x, terms, normed, normed_t, cot_t, inv_rms, qb, kb, vb, dab, ob, d_qkv, d_normed):
    prologue(x, cot, normed, normed_t, cot_t, inv_rms)

    def chunk(p, _):
        project(p, cot, w_qkv, w_out, normed, qb, kb, vb, dab)
        attend(p, bias, qb, kb, vb, dab, ob, d_qkv)
        weight_terms(p, normed_t, cot_t, d_qkv, ob, terms)
        return 0

    lax.fori_loop(0, CHUNKS, chunk, 0)
    token_grad(x, w_qkv, d_qkv, inv_rms, d_normed, d_x)


TERMS = (CHUNKS, 2, 2, 4, 4, 4, 16, GROUP)


def window_call(x, cot, w_qkv, w_out, bias):
    vmem = pl.BlockSpec(memory_space=pltpu.VMEM)
    return pl.pallas_call(
        window_kernel,
        out_shape=(jax.ShapeDtypeStruct((LOCAL, D), BF16), jax.ShapeDtypeStruct(TERMS, BF16)),
        in_specs=[vmem] * 5,
        out_specs=(vmem, vmem),
        scratch_shapes=[
            pltpu.VMEM((LOCAL, D), BF16),
            pltpu.VMEM((D, LOCAL), BF16),
            pltpu.VMEM((D, LOCAL), BF16),
            pltpu.VMEM((LOCAL, 1), F32),
            pltpu.VMEM((LOCAL, GROUP), BF16),
            pltpu.VMEM((LOCAL, GROUP), BF16),
            pltpu.VMEM((LOCAL, GROUP), BF16),
            pltpu.VMEM((LOCAL, GROUP), BF16),
            pltpu.VMEM((LOCAL, GROUP), BF16),
            pltpu.VMEM((LOCAL, 3 * D), BF16),
            pltpu.VMEM((LOCAL, D), F32),
        ],
        compiler_params=pltpu.CompilerParams(vmem_limit_bytes=60 * 1024 * 1024),
        name="windows",
    )(x, cot, w_qkv, w_out, bias)


def place():
    lon, lat = lax.axis_index("lon"), lax.axis_index("lat")
    z, y_lo, core = lon // 4, lon // 2 % 2, lon % 2
    x, y_hi = lat // 2, lat % 2
    return x, y_hi * 2 + y_lo, z, core


def device(x, y, z, core):
    return {"lon": z * 4 + y % 2 * 2 + core, "lat": x * 2 + y // 2}


def axis_peer(axis, step):
    x, y, z, core = place()
    if axis == "x":
        at = (x + step) % 4
        return at, device(at, y, z, core)
    if axis == "y":
        at = (y + step) % 4
        return at, device(x, at, z, core)
    at = (z + step) % 4
    return at, device(x, y, at, core)


ORDERS = (("x", "y", "z"), ("z", "y", "x"))


def greet():
    x, y, z, core = place()
    barrier = pltpu.get_barrier_semaphore()
    pl.semaphore_signal(barrier, inc=1, device_id=device(x, y, z, 1 - core), device_id_type=MESH)
    for axis in "xyz":
        for step in (1, 2, 3):
            _, peer = axis_peer(axis, step)
            pl.semaphore_signal(barrier, inc=1, device_id=peer, device_id_type=MESH)
    pl.semaphore_wait(barrier, 10)


def core_copy(p, terms, got_0, send, recv):
    x, y, z, core = place()
    return pltpu.make_async_remote_copy(
        src_ref=terms.at[p, 1 - core],
        dst_ref=got_0.at[p],
        send_sem=send.at[p, 0, 0],
        recv_sem=recv.at[p, 0, 0],
        device_id=device(x, y, z, 1 - core),
        device_id_type=MESH,
    )


def stage_copy(p, stage, half, step, source, target, send, recv):
    at, peer = axis_peer(ORDERS[half][stage], step)
    slot = 3 * half + step - 1
    return pltpu.make_async_remote_copy(
        src_ref=source.at[p, half, at],
        dst_ref=target.at[p, half, step - 1],
        send_sem=send.at[p, 1 + stage, slot],
        recv_sem=recv.at[p, 1 + stage, slot],
        device_id=peer,
        device_id_type=MESH,
    )


STEPS = [(half, step) for half in (0, 1) for step in (1, 2, 3)]


def my_index(stage, half):
    x, y, z, _ = place()
    return {"x": x, "y": y, "z": z}[ORDERS[half][stage]]


def rs_start(p, terms, got_0, send, recv):
    core_copy(p, terms, got_0, send, recv).start()


def rs_first(p, terms, got_0, sum_0, got_1, send, recv):
    core = place()[3]
    core_copy(p, terms, got_0, send, recv).wait_recv()
    for half in (0, 1):
        for a in range(4):
            sum_0[p, half, a] = terms[p, core, half, a] + got_0[p, half, a]
    for half, step in STEPS:
        stage_copy(p, 0, half, step, sum_0, got_1, send, recv).start()


def rs_next(p, stage, source, got, total, after, send, recv):
    for half, step in STEPS:
        stage_copy(p, stage, half, step, source, got, send, recv).wait_recv()
    for half in (0, 1):
        mine = source[p, half, my_index(stage, half)].astype(F32)
        for i in range(3):
            mine = mine + got[p, half, i].astype(F32)
        total[p, half] = mine.astype(total.dtype)
    if after is not None:
        for half, step in STEPS:
            stage_copy(p, stage + 1, half, step, total, after, send, recv).start()


def rs_finish(terms, got_0, sums, gots, send, recv):
    def one(p, _):
        core_copy(p, terms, got_0, send, recv).wait_send()
        for stage in range(3):
            for half, step in STEPS:
                stage_copy(p, stage, half, step, sums[stage], gots[stage], send, recv).wait_send()
        return 0

    lax.fori_loop(0, CHUNKS, one, 0)


def write_grads(sum_3, grad_qkv, grad_out):
    scale = 1.0 / math.sqrt(LOCAL * 128)
    for p in range(CHUNKS):
        at = p * GROUP
        grad_qkv[:, at : at + GROUP] = sum_3[p, 0, :8, :] * scale
        grad_qkv[:, D + at : D + at + GROUP] = sum_3[p, 0, 8:, :] * scale
        grad_qkv[:, 2 * D + at : 2 * D + at + GROUP] = sum_3[p, 1, :8, :] * scale
        grad_out[:, at : at + GROUP] = sum_3[p, 1, 8:, :] * scale


def scatter_kernel(terms, grad_qkv, grad_out, got_0, sum_0, got_1, sum_1, got_2, sum_2, got_3, sum_3, send, recv):
    greet()

    def loop(body):
        lax.fori_loop(0, CHUNKS, lambda p, _: (body(p), 0)[1], 0)

    loop(lambda p: rs_start(p, terms, got_0, send, recv))
    loop(lambda p: rs_first(p, terms, got_0, sum_0, got_1, send, recv))
    loop(lambda p: rs_next(p, 0, sum_0, got_1, sum_1, got_2, send, recv))
    loop(lambda p: rs_next(p, 1, sum_1, got_2, sum_2, got_3, send, recv))
    loop(lambda p: rs_next(p, 2, sum_2, got_3, sum_3, None, send, recv))
    write_grads(sum_3, grad_qkv, grad_out)
    rs_finish(terms, got_0, (sum_0, sum_1, sum_2), (got_1, got_2, got_3), send, recv)


def scatter_scratch():
    unit = (16, GROUP)
    return [
        pltpu.VMEM((CHUNKS, 2, 4, 4, 4) + unit, BF16),
        pltpu.VMEM((CHUNKS, 2, 4, 4, 4) + unit, BF16),
        pltpu.VMEM((CHUNKS, 2, 3, 4, 4) + unit, BF16),
        pltpu.VMEM((CHUNKS, 2, 4, 4) + unit, BF16),
        pltpu.VMEM((CHUNKS, 2, 3, 4) + unit, BF16),
        pltpu.VMEM((CHUNKS, 2, 4) + unit, BF16),
        pltpu.VMEM((CHUNKS, 2, 3) + unit, BF16),
        pltpu.VMEM((CHUNKS, 2) + unit, F32),
        pltpu.SemaphoreType.DMA((CHUNKS, 4, 6)),
        pltpu.SemaphoreType.DMA((CHUNKS, 4, 6)),
    ]


def scatter_call(terms):
    vmem = pl.BlockSpec(memory_space=pltpu.VMEM)
    return pl.pallas_call(
        scatter_kernel,
        out_shape=(jax.ShapeDtypeStruct((8, 3 * D), F32), jax.ShapeDtypeStruct((8, D), F32)),
        in_specs=[vmem],
        out_specs=(vmem, vmem),
        scratch_shapes=scatter_scratch(),
        compiler_params=pltpu.CompilerParams(
            collective_id=0, has_side_effects=True, vmem_limit_bytes=48 * 1024 * 1024
        ),
        name="scatter",
    )(terms)


def passed_along(value, axes, steps):
    sizes = [lax.axis_size(axis) for axis in axes]
    total = math.prod(sizes)
    pairs = []
    for source in range(total):
        if len(axes) == 1:
            pairs.append((source, (source + steps) % total))
        else:
            first, second = source // sizes[1], source % sizes[1]
            pairs.append((source, (first + steps) % sizes[0] * sizes[1] + (second + steps) % sizes[1]))
    return lax.ppermute(value, axes if len(axes) > 1 else axes[0], pairs)


def pair_bias(row_valid):
    lat_total = row_valid.shape[0]
    lat_band = lax.axis_index("lat")
    row = (lat_band * ROWS + jnp.arange(ROWS, dtype=jnp.int32) + HALF) % lat_total
    wrap = row < HALF
    valid = lax.dynamic_slice_in_dim(jnp.roll(row_valid, -HALF), lat_band * ROWS, ROWS) == 1
    wrap = wrap.reshape(STRIPS, WIN)
    valid = valid.reshape(STRIPS, WIN)
    place_in_row = jnp.arange(COLS, dtype=jnp.int32)
    window = (place_in_row - HALF) % COLS // WIN
    token_row = jnp.repeat(jnp.arange(WIN), COLS)
    token_window = jnp.tile(window, WIN)
    token_wrap = wrap[:, token_row]
    token_valid = valid[:, token_row]
    itself = jnp.eye(STRIP, dtype=bool)
    allowed = (
        (token_window[:, None] == token_window[None, :])[None]
        & (token_wrap[:, :, None] == token_wrap[:, None, :])
        & (token_valid[:, None, :] | itself[None])
    )
    return jnp.where(allowed, -SHARP * LOG2E, BLOCKED).astype(F32)


def on_device(tokens, cotangent, w_qkv, w_out, row_valid):
    paired = jnp.stack([tokens, cotangent])
    below = passed_along(paired[:, :HALF], ("lat",), -1)
    beside = passed_along(paired[:, HALF:, :HALF], ("lon",), -1)
    corner = passed_along(paired[:, :HALF, :HALF], ("lon", "lat"), -1)
    side = jnp.concatenate([beside, corner], axis=1)
    body = jnp.concatenate([paired[:, HALF:, HALF:], below[:, :, HALF:]], axis=1)
    rolled = jnp.concatenate([side, body], axis=2).reshape(2, LOCAL, D)
    d_x, terms = window_call(rolled[0], rolled[1], w_qkv, w_out, pair_bias(row_valid))
    grad_qkv, grad_out = scatter_call(terms)
    d_grid = d_x.reshape(ROWS, COLS, D)
    side = d_grid[:, :HALF]
    from_left = passed_along(side[:-HALF], ("lon",), 1)
    from_above = passed_along(d_grid[-HALF:], ("lat",), 1)
    from_corner = passed_along(side[-HALF:], ("lon", "lat"), 1)
    side = jnp.concatenate([from_corner, from_left], axis=0)
    body = jnp.concatenate([from_above[:, HALF:], d_grid[:-HALF, HALF:]], axis=0)
    d_tokens = jnp.concatenate([side, body], axis=1)
    return (d_tokens, grad_qkv, grad_out)


def solution(mesh):
    placed = (P("lat", "lon", None), P("lat", "lon", None), P(), P(), P())
    return jax.shard_map(
        on_device,
        mesh=mesh,
        in_specs=placed,
        out_specs=(P("lat", "lon", None), P(("lon", "lat"), None), P(("lon", "lat"), None)),
        check_vma=False,
    )
```

```python
import functools
import math

import jax
import jax.numpy as jnp
from jax import lax
from jax.experimental import pallas as pl
from jax.experimental.pallas import tpu as pltpu
from jax.sharding import PartitionSpec as P

D = 1024
HEADS = 16
WIN = 6
HEAD_DIM = 64
HALF = 3
ROWS = 36
COLS = 24
LOCAL = ROWS * COLS
STRIPS = ROWS // WIN
STRIP = WIN * COLS
GROUP = 256
CHUNKS = D // GROUP
GROUP_HEADS = GROUP // HEAD_DIM
STACK = GROUP_HEADS * STRIP

SHARP = 10.0
LOG2E = math.log2(math.e)
EPSILON = 1e-06
BLOCKED = -1e30

F32 = jnp.float32
BF16 = jnp.bfloat16
MESH = pl.DeviceIdType.MESH
NN = (((1,), (0,)), ((), ()))
NT = (((1,), (1,)), ((), ()))
TN = (((0,), (0,)), ((), ()))


def dot(a, b, dims=NN):
    return lax.dot_general(a, b, dims, preferred_element_type=F32)


def head_sums(t, ones):
    hi = t.astype(BF16)
    lo = (t - hi.astype(F32)).astype(BF16)
    return dot(hi, ones) + dot(lo, ones)


def by_head(t):
    lane = lax.broadcasted_iota(jnp.int32, t.shape, 1) // HEAD_DIM
    zero = jnp.zeros_like(t)
    return jnp.concatenate([jnp.where(lane == h, t, zero) for h in range(GROUP_HEADS)], axis=0)


def pick_heads(t):
    lane = lax.broadcasted_iota(jnp.int32, (STRIP, GROUP), 1) // HEAD_DIM
    out = t[:STRIP]
    for h in range(1, GROUP_HEADS):
        out = jnp.where(lane == h, t[h * STRIP : (h + 1) * STRIP], out)
    return out


def prologue(x, cot, normed, normed_t, cot_t, inv_rms):
    def norm_strip(s, _):
        rows = pl.ds(pl.multiple_of(s * STRIP, 16), STRIP)
        xf = x[rows, :].astype(F32)
        inv = lax.rsqrt(jnp.mean(xf * xf, axis=-1, keepdims=True) + EPSILON)
        inv_rms[rows, :] = inv
        normed[rows, :] = (xf * inv).astype(BF16)
        return 0

    lax.fori_loop(0, STRIPS, norm_strip, 0)
    for at in range(0, LOCAL, 128):
        width = min(128, LOCAL - at)
        normed_t[:, at : at + width] = normed[at : at + width, :].T
        cot_t[:, at : at + width] = cot[at : at + width, :].T


def project(p, cot, w_qkv, w_out, normed, qb, kb, vb, dab):
    def part(i, _):
        rows = pl.ds(pl.multiple_of(i * 432, 16), 432)
        base = pl.multiple_of(p * GROUP, GROUP)
        n = normed[rows, :]
        qb[rows, :] = dot(n, w_qkv[:, pl.ds(base, GROUP)]).astype(BF16)
        kb[rows, :] = dot(n, w_qkv[:, pl.ds(base + D, GROUP)]).astype(BF16)
        vb[rows, :] = dot(n, w_qkv[:, pl.ds(base + 2 * D, GROUP)]).astype(BF16)
        dab[rows, :] = dot(cot[rows, :], w_out[pl.ds(base, GROUP), :], NT).astype(BF16)
        return 0

    lax.fori_loop(0, 2, part, 0)


def attend(p, bias, qb, kb, vb, dab, ob, d_qkv):
    row_head = lax.broadcasted_iota(jnp.int32, (GROUP, GROUP), 0) // HEAD_DIM
    col_head = lax.broadcasted_iota(jnp.int32, (GROUP, GROUP), 1) // HEAD_DIM
    ones = jnp.where(row_head == col_head, 1.0, 0.0).astype(BF16)

    def strip(s, _):
        rows = pl.ds(pl.multiple_of(s * STRIP, 16), STRIP)
        base = pl.multiple_of(p * GROUP, GROUP)
        q = qb[rows, :].astype(F32)
        k = kb[rows, :].astype(F32)
        inv_q = lax.rsqrt(head_sums(q * q, ones) + EPSILON)
        inv_k = lax.rsqrt(head_sums(k * k, ones) + EPSILON)
        q_unit = q * inv_q
        k_unit = k * inv_k
        q_heads = by_head(q_unit.astype(BF16))
        k_round = k_unit.astype(BF16)
        v = vb[rows, :]
        da_heads = by_head(dab[rows, :])
        scores = dot(q_heads, k_round, NT).reshape(GROUP_HEADS, STRIP, STRIP)
        weights = jnp.exp2(scores * (SHARP * LOG2E) + bias[s][None])
        total = jnp.sum(weights, axis=-1, keepdims=True)
        probs = weights * (1.0 / total)
        prob_round = probs.astype(BF16).reshape(STACK, STRIP)
        d_probs = dot(da_heads, v, NT).reshape(GROUP_HEADS, STRIP, STRIP)
        mixed = jnp.sum(probs * d_probs, axis=-1, keepdims=True)
        ds_round = (probs * (d_probs - mixed)).astype(BF16).reshape(STACK, STRIP)
        ob[rows, :] = pick_heads(dot(prob_round, v)).astype(BF16)
        d_qkv[rows, pl.ds(base + 2 * D, GROUP)] = dot(prob_round, da_heads, TN).astype(BF16)
        dq_unit = SHARP * pick_heads(dot(ds_round, k_round))
        dk_unit = SHARP * dot(ds_round, q_heads, TN)
        d_q = inv_q * (dq_unit - q_unit * head_sums(q_unit * dq_unit, ones))
        d_k = inv_k * (dk_unit - k_unit * head_sums(k_unit * dk_unit, ones))
        d_qkv[rows, pl.ds(base, GROUP)] = d_q.astype(BF16)
        d_qkv[rows, pl.ds(base + D, GROUP)] = d_k.astype(BF16)
        return 0

    lax.fori_loop(0, STRIPS, strip, 0)


def weight_terms(p, normed_t, cot_t, d_qkv, ob, terms):
    def plane(z, _):
        rows = pl.ds(pl.multiple_of(z * 256, 256), 256)
        base = pl.multiple_of(p * GROUP, GROUP)
        n = normed_t[rows, :]
        g_q = dot(n, d_qkv[:, pl.ds(base, GROUP)])
        g_k = dot(n, d_qkv[:, pl.ds(base + D, GROUP)])
        g_v = dot(n, d_qkv[:, pl.ds(base + 2 * D, GROUP)])
        g_o = dot(cot_t[rows, :], ob[...])
        for unit in range(32):
            y_lo, core, x, y_hi = unit // 16, unit // 8 % 2, unit // 2 % 4, unit % 2
            y = y_hi * 2 + y_lo
            part = slice(unit * 8, unit * 8 + 8)
            first = jnp.concatenate([g_q[part], g_k[part]], axis=0)
            second = jnp.concatenate([g_v[part], g_o[part]], axis=0)
            terms[p, core, 0, x, y, z] = first.astype(BF16)
            terms[p, core, 1, z, y, x] = second.astype(BF16)
        return 0

    lax.fori_loop(0, 4, plane, 0)


def normed_grad(n, w_qkv, d_qkv, d_normed):
    cols = pl.ds(pl.multiple_of(n * 256, 256), 256)
    d_normed[:, cols] = dot(d_qkv[...], w_qkv[cols, :], NT)


def token_grad(x, inv_rms, d_normed, d_x):
    def strip(s, _):
        rows = pl.ds(pl.multiple_of(s * STRIP, 16), STRIP)
        xf = x[rows, :].astype(F32)
        dn = d_normed[rows, :]
        inv = inv_rms[rows, :]
        pull = jnp.mean(dn * xf, axis=-1, keepdims=True) * (inv * inv * inv)
        d_x[rows, :] = (inv * dn - xf * pull).astype(BF16)
        return 0

    lax.fori_loop(0, STRIPS, strip, 0)


def pair_bias(invalid, bias):
    query = lax.broadcasted_iota(jnp.int32, (STRIP, STRIP), 0)
    key = lax.broadcasted_iota(jnp.int32, (STRIP, STRIP), 1)
    window = lambda t: (t % COLS + COLS - HALF) % COLS // WIN
    half = lambda t: t // (HALF * COLS)
    same_window = window(query) == window(key)
    same_half = half(query) == half(key)
    seam = lax.axis_index("lat") == lax.axis_size("lat") - 1
    open_bias = jnp.where(same_window, -SHARP * LOG2E, BLOCKED)
    seam_bias = jnp.where(same_window & same_half, -SHARP * LOG2E, BLOCKED)
    others = jnp.where(query == key, 0.0, BLOCKED)
    for s in range(STRIPS):
        base = open_bias if s < STRIPS - 1 else jnp.where(seam, seam_bias, open_bias)
        bias[s] = base + others * invalid[s : s + 1, :]


def window_kernel(
    x, cot, w_qkv, w_out, invalid, d_x, grad_qkv, grad_out,
    bias, normed, normed_t, cot_t, inv_rms, qb, kb, vb, dab, ob, d_qkv, d_normed, terms,
    got_0, sum_0, got_1, sum_1, got_2, sum_2, got_3, sum_3, send, recv,
):
    greet()
    pair_bias(invalid, bias)
    prologue(x, cot, normed, normed_t, cot_t, inv_rms)
    first = lambda p: rs_first(p, terms, got_0, sum_0, got_1, send, recv)
    second = lambda p: rs_next(p, 0, sum_0, got_1, sum_1, got_2, send, recv)
    third = lambda p: rs_next(p, 1, sum_1, got_2, sum_2, got_3, send, recv)
    last = lambda p: rs_next(p, 2, sum_2, got_3, sum_3, None, send, recv)

    def chunk(p, _):
        project(p, cot, w_qkv, w_out, normed, qb, kb, vb, dab)
        pl.when(p > 0)(lambda: first(p - 1))
        attend(p, bias, qb, kb, vb, dab, ob, d_qkv)
        pl.when(p > 0)(lambda: second(p - 1))
        weight_terms(p, normed_t, cot_t, d_qkv, ob, terms)
        rs_start(p, terms, got_0, send, recv)
        pl.when(p > 0)(lambda: third(p - 1))
        return 0

    lax.fori_loop(0, CHUNKS, chunk, 0)

    def tail(n, _):
        normed_grad(n, w_qkv, d_qkv, d_normed)
        pl.when(n == 0)(lambda: first(CHUNKS - 1))
        pl.when(n == 3)(lambda: second(CHUNKS - 1))
        return 0

    lax.fori_loop(0, D // 256, tail, 0)
    token_grad(x, inv_rms, d_normed, d_x)
    third(CHUNKS - 1)
    lax.fori_loop(0, CHUNKS, lambda p, _: (last(p), 0)[1], 0)
    write_grads(sum_3, grad_qkv, grad_out)
    rs_finish(terms, got_0, (sum_0, sum_1, sum_2), (got_1, got_2, got_3), send, recv)


TERMS = (CHUNKS, 2, 2, 4, 4, 4, 16, GROUP)


def window_call(x, cot, w_qkv, w_out, invalid):
    vmem = pl.BlockSpec(memory_space=pltpu.VMEM)
    return pl.pallas_call(
        window_kernel,
        out_shape=(
            jax.ShapeDtypeStruct((LOCAL, D), BF16),
            jax.ShapeDtypeStruct((8, 3 * D), F32),
            jax.ShapeDtypeStruct((8, D), F32),
        ),
        in_specs=[vmem] * 5,
        out_specs=(vmem, vmem, vmem),
        scratch_shapes=[
            pltpu.VMEM((STRIPS, STRIP, STRIP), F32),
            pltpu.VMEM((LOCAL, D), BF16),
            pltpu.VMEM((D, LOCAL), BF16),
            pltpu.VMEM((D, LOCAL), BF16),
            pltpu.VMEM((LOCAL, 1), F32),
            pltpu.VMEM((LOCAL, GROUP), BF16),
            pltpu.VMEM((LOCAL, GROUP), BF16),
            pltpu.VMEM((LOCAL, GROUP), BF16),
            pltpu.VMEM((LOCAL, GROUP), BF16),
            pltpu.VMEM((LOCAL, GROUP), BF16),
            pltpu.VMEM((LOCAL, 3 * D), BF16),
            pltpu.VMEM((LOCAL, D), F32),
            pltpu.VMEM(TERMS, BF16),
        ]
        + scatter_scratch(),
        compiler_params=pltpu.CompilerParams(
            collective_id=0, has_side_effects=True, vmem_limit_bytes=60 * 1024 * 1024
        ),
        name="windows",
    )(x, cot, w_qkv, w_out, invalid)


def place():
    lon, lat = lax.axis_index("lon"), lax.axis_index("lat")
    z, y_lo, core = lon // 4, lon // 2 % 2, lon % 2
    x, y_hi = lat // 2, lat % 2
    return x, y_hi * 2 + y_lo, z, core


def device(x, y, z, core):
    return {"lon": z * 4 + y % 2 * 2 + core, "lat": x * 2 + y // 2}


def axis_peer(axis, step):
    x, y, z, core = place()
    if axis == "x":
        at = (x + step) % 4
        return at, device(at, y, z, core)
    if axis == "y":
        at = (y + step) % 4
        return at, device(x, at, z, core)
    at = (z + step) % 4
    return at, device(x, y, at, core)


ORDERS = (("x", "y", "z"), ("z", "y", "x"))


def greet():
    x, y, z, core = place()
    barrier = pltpu.get_barrier_semaphore()
    pl.semaphore_signal(barrier, inc=1, device_id=device(x, y, z, 1 - core), device_id_type=MESH)
    for axis in "xyz":
        for step in (1, 2, 3):
            _, peer = axis_peer(axis, step)
            pl.semaphore_signal(barrier, inc=1, device_id=peer, device_id_type=MESH)
    pl.semaphore_wait(barrier, 10)


def core_copy(p, terms, got_0, send, recv):
    x, y, z, core = place()
    return pltpu.make_async_remote_copy(
        src_ref=terms.at[p, 1 - core],
        dst_ref=got_0.at[p],
        send_sem=send.at[p, 0, 0],
        recv_sem=recv.at[p, 0, 0],
        device_id=device(x, y, z, 1 - core),
        device_id_type=MESH,
    )


def stage_copy(p, stage, half, step, source, target, send, recv):
    at, peer = axis_peer(ORDERS[half][stage], step)
    slot = 3 * half + step - 1
    return pltpu.make_async_remote_copy(
        src_ref=source.at[p, half, at],
        dst_ref=target.at[p, half, step - 1],
        send_sem=send.at[p, 1 + stage, slot],
        recv_sem=recv.at[p, 1 + stage, slot],
        device_id=peer,
        device_id_type=MESH,
    )


STEPS = [(half, step) for half in (0, 1) for step in (1, 2, 3)]


def my_index(stage, half):
    x, y, z, _ = place()
    return {"x": x, "y": y, "z": z}[ORDERS[half][stage]]


def rs_start(p, terms, got_0, send, recv):
    core_copy(p, terms, got_0, send, recv).start()


def rs_first(p, terms, got_0, sum_0, got_1, send, recv):
    core = place()[3]
    core_copy(p, terms, got_0, send, recv).wait_recv()
    for half in (0, 1):
        for a in range(4):
            sum_0[p, half, a] = terms[p, core, half, a] + got_0[p, half, a]
    for half, step in STEPS:
        stage_copy(p, 0, half, step, sum_0, got_1, send, recv).start()


def rs_next(p, stage, source, got, total, after, send, recv):
    for half, step in STEPS:
        stage_copy(p, stage, half, step, source, got, send, recv).wait_recv()
    for half in (0, 1):
        mine = source[p, half, my_index(stage, half)].astype(F32)
        for i in range(3):
            mine = mine + got[p, half, i].astype(F32)
        total[p, half] = mine.astype(total.dtype)
    if after is not None:
        for half, step in STEPS:
            stage_copy(p, stage + 1, half, step, total, after, send, recv).start()


def rs_finish(terms, got_0, sums, gots, send, recv):
    def one(p, _):
        core_copy(p, terms, got_0, send, recv).wait_send()
        for stage in range(3):
            for half, step in STEPS:
                stage_copy(p, stage, half, step, sums[stage], gots[stage], send, recv).wait_send()
        return 0

    lax.fori_loop(0, CHUNKS, one, 0)


def write_grads(sum_3, grad_qkv, grad_out):
    scale = 1.0 / math.sqrt(LOCAL * 128)
    for p in range(CHUNKS):
        at = p * GROUP
        grad_qkv[:, at : at + GROUP] = sum_3[p, 0, :8, :] * scale
        grad_qkv[:, D + at : D + at + GROUP] = sum_3[p, 0, 8:, :] * scale
        grad_qkv[:, 2 * D + at : 2 * D + at + GROUP] = sum_3[p, 1, :8, :] * scale
        grad_out[:, at : at + GROUP] = sum_3[p, 1, 8:, :] * scale


def scatter_scratch():
    unit = (16, GROUP)
    return [
        pltpu.VMEM((CHUNKS, 2, 4, 4, 4) + unit, BF16),
        pltpu.VMEM((CHUNKS, 2, 4, 4, 4) + unit, BF16),
        pltpu.VMEM((CHUNKS, 2, 3, 4, 4) + unit, BF16),
        pltpu.VMEM((CHUNKS, 2, 4, 4) + unit, BF16),
        pltpu.VMEM((CHUNKS, 2, 3, 4) + unit, BF16),
        pltpu.VMEM((CHUNKS, 2, 4) + unit, BF16),
        pltpu.VMEM((CHUNKS, 2, 3) + unit, BF16),
        pltpu.VMEM((CHUNKS, 2) + unit, F32),
        pltpu.SemaphoreType.DMA((CHUNKS, 4, 6)),
        pltpu.SemaphoreType.DMA((CHUNKS, 4, 6)),
    ]


def passed_along(value, axes, steps):
    sizes = [lax.axis_size(axis) for axis in axes]
    total = math.prod(sizes)
    pairs = []
    for source in range(total):
        if len(axes) == 1:
            pairs.append((source, (source + steps) % total))
        else:
            first, second = source // sizes[1], source % sizes[1]
            pairs.append((source, (first + steps) % sizes[0] * sizes[1] + (second + steps) % sizes[1]))
    return lax.ppermute(value, axes if len(axes) > 1 else axes[0], pairs)


def invalid_keys(row_valid):
    rows = lax.dynamic_slice_in_dim(jnp.roll(row_valid, -HALF), lax.axis_index("lat") * ROWS, ROWS)
    return jnp.repeat(1.0 - rows.astype(F32), COLS).reshape(STRIPS, STRIP)


def on_device(tokens, cotangent, w_qkv, w_out, row_valid):
    paired = jnp.stack([tokens, cotangent])
    below = passed_along(paired[:, :HALF], ("lat",), -1)
    beside = passed_along(paired[:, HALF:, :HALF], ("lon",), -1)
    corner = passed_along(paired[:, :HALF, :HALF], ("lon", "lat"), -1)
    side = jnp.concatenate([beside, corner], axis=1)
    body = jnp.concatenate([paired[:, HALF:, HALF:], below[:, :, HALF:]], axis=1)
    rolled = jnp.concatenate([side, body], axis=2).reshape(2, LOCAL, D)
    d_x, grad_qkv, grad_out = window_call(rolled[0], rolled[1], w_qkv, w_out, invalid_keys(row_valid))
    d_grid = d_x.reshape(ROWS, COLS, D)
    side = d_grid[:, :HALF]
    from_left = passed_along(side[:-HALF], ("lon",), 1)
    from_above = passed_along(d_grid[-HALF:], ("lat",), 1)
    from_corner = passed_along(side[-HALF:], ("lon", "lat"), 1)
    side = jnp.concatenate([from_corner, from_left], axis=0)
    body = jnp.concatenate([from_above[:, HALF:], d_grid[:-HALF, HALF:]], axis=0)
    d_tokens = jnp.concatenate([side, body], axis=1)
    return (d_tokens, grad_qkv, grad_out)


def solution(mesh):
    placed = (P("lat", "lon", None), P("lat", "lon", None), P(), P(), P())
    return jax.shard_map(
        on_device,
        mesh=mesh,
        in_specs=placed,
        out_specs=(P("lat", "lon", None), P(("lon", "lat"), None), P(("lon", "lat"), None)),
        check_vma=False,
    )
```

```python
import math

import jax
import jax.numpy as jnp
from jax import lax
from jax.experimental import pallas as pl
from jax.experimental.pallas import tpu as pltpu
from jax.sharding import PartitionSpec as P

D = 1024
HEADS = 16
WIN = 6
HEAD_DIM = 64
HALF = 3
ROWS = 36
COLS = 24
LOCAL = ROWS * COLS
STRIPS = ROWS // WIN
STRIP = WIN * COLS
GROUP = 256
CHUNKS = D // GROUP
GROUP_HEADS = GROUP // HEAD_DIM
STACK = GROUP_HEADS * STRIP
EDGE = 112
EDGES = 128
BAND = 80

SHARP = 10.0
LOG2E = math.log2(math.e)
EPSILON = 1e-06
BLOCKED = -1e30

F32 = jnp.float32
BF16 = jnp.bfloat16
MESH = pl.DeviceIdType.MESH
NN = (((1,), (0,)), ((), ()))
NT = (((1,), (1,)), ((), ()))
TN = (((0,), (0,)), ((), ()))


def dot(a, b, dims=NN):
    return lax.dot_general(a, b, dims, preferred_element_type=F32)


def head_sums(t, ones):
    hi = t.astype(BF16)
    lo = (t - hi.astype(F32)).astype(BF16)
    return dot(hi, ones) + dot(lo, ones)


def by_head(t):
    lane = lax.broadcasted_iota(jnp.int32, t.shape, 1) // HEAD_DIM
    zero = jnp.zeros_like(t)
    return jnp.concatenate([jnp.where(lane == h, t, zero) for h in range(GROUP_HEADS)], axis=0)


def pick_heads(t):
    lane = lax.broadcasted_iota(jnp.int32, (STRIP, GROUP), 1) // HEAD_DIM
    out = t[:STRIP]
    for h in range(1, GROUP_HEADS):
        out = jnp.where(lane == h, t[h * STRIP : (h + 1) * STRIP], out)
    return out


def shift_rows(ext, s):
    return ext[pl.ds(pl.multiple_of(s * STRIP + 64, 16), STRIP + 16), :].astype(F32)[8 : 8 + STRIP]


def edge_pick():
    at = lax.broadcasted_iota(jnp.int32, (EDGE, LOCAL), 0)
    token = lax.broadcasted_iota(jnp.int32, (EDGE, LOCAL), 1)
    return jnp.where(token == at // HALF * COLS + at % HALF, 1.0, 0.0).astype(BF16)


def edge_spread(s, near, far):
    token = lax.broadcasted_iota(jnp.int32, (STRIP, EDGES), 0)
    at = lax.broadcasted_iota(jnp.int32, (STRIP, EDGES), 1)
    row, col = s * WIN + token // COLS, token % COLS
    source = jnp.where(near(row), far[0] + HALF * row + col, far[1] + HALF * row + col)
    return jnp.where((col < HALF) & (at == source), 1.0, 0.0).astype(BF16)


def prologue(x_ext, cot_ext, edges, x, cot, normed, normed_t, cot_t, inv_rms):
    is_edge = lax.broadcasted_iota(jnp.int32, (STRIP, 1), 0) % COLS < HALF

    def norm_strip(s, _):
        rows = pl.ds(pl.multiple_of(s * STRIP, 16), STRIP)
        spread = edge_spread(s, lambda row: row < ROWS - HALF, (HALF * HALF, EDGE - HALF * (ROWS - HALF)))
        cot[rows, :] = jnp.where(is_edge, dot(spread, edges[1]), shift_rows(cot_ext, s)).astype(BF16)
        xf = jnp.where(is_edge, dot(spread, edges[0]), shift_rows(x_ext, s))
        x[rows, :] = xf.astype(BF16)
        inv = lax.rsqrt(jnp.mean(xf * xf, axis=-1, keepdims=True) + EPSILON)
        inv_rms[rows, :] = inv
        normed[rows, :] = (xf * inv).astype(BF16)
        return 0

    lax.fori_loop(0, STRIPS, norm_strip, 0)
    for at in range(0, LOCAL, 128):
        width = min(128, LOCAL - at)
        normed_t[:, at : at + width] = normed[at : at + width, :].T
        cot_t[:, at : at + width] = cot[at : at + width, :].T


def project(p, cot, w_qkv, w_out, normed, qb, kb, vb, dab):
    def part(i, _):
        rows = pl.ds(pl.multiple_of(i * 432, 16), 432)
        base = pl.multiple_of(p * GROUP, GROUP)
        n = normed[rows, :]
        qb[rows, :] = dot(n, w_qkv[:, pl.ds(base, GROUP)]).astype(BF16)
        kb[rows, :] = dot(n, w_qkv[:, pl.ds(base + D, GROUP)]).astype(BF16)
        vb[rows, :] = dot(n, w_qkv[:, pl.ds(base + 2 * D, GROUP)]).astype(BF16)
        dab[rows, :] = dot(cot[rows, :], w_out[pl.ds(base, GROUP), :], NT).astype(BF16)
        return 0

    lax.fori_loop(0, 2, part, 0)


def attend(p, bias, qb, kb, vb, dab, ob, d_qkv):
    row_head = lax.broadcasted_iota(jnp.int32, (GROUP, GROUP), 0) // HEAD_DIM
    col_head = lax.broadcasted_iota(jnp.int32, (GROUP, GROUP), 1) // HEAD_DIM
    ones = jnp.where(row_head == col_head, 1.0, 0.0).astype(BF16)

    def strip(s, _):
        rows = pl.ds(pl.multiple_of(s * STRIP, 16), STRIP)
        base = pl.multiple_of(p * GROUP, GROUP)
        q = qb[rows, :].astype(F32)
        k = kb[rows, :].astype(F32)
        inv_q = lax.rsqrt(head_sums(q * q, ones) + EPSILON)
        inv_k = lax.rsqrt(head_sums(k * k, ones) + EPSILON)
        q_unit = q * inv_q
        k_unit = k * inv_k
        q_heads = by_head(q_unit.astype(BF16))
        k_round = k_unit.astype(BF16)
        v = vb[rows, :]
        da_heads = by_head(dab[rows, :])
        scores = dot(q_heads, k_round, NT).reshape(GROUP_HEADS, STRIP, STRIP)
        weights = jnp.exp2(scores * (SHARP * LOG2E) + bias[s][None])
        total = jnp.sum(weights, axis=-1, keepdims=True)
        probs = weights * (1.0 / total)
        prob_round = probs.astype(BF16).reshape(STACK, STRIP)
        d_probs = dot(da_heads, v, NT).reshape(GROUP_HEADS, STRIP, STRIP)
        mixed = jnp.sum(probs * d_probs, axis=-1, keepdims=True)
        ds_round = (probs * (d_probs - mixed)).astype(BF16).reshape(STACK, STRIP)
        ob[rows, :] = pick_heads(dot(prob_round, v)).astype(BF16)
        d_qkv[rows, pl.ds(base + 2 * D, GROUP)] = dot(prob_round, da_heads, TN).astype(BF16)
        dq_unit = SHARP * pick_heads(dot(ds_round, k_round))
        dk_unit = SHARP * dot(ds_round, q_heads, TN)
        d_q = inv_q * (dq_unit - q_unit * head_sums(q_unit * dq_unit, ones))
        d_k = inv_k * (dk_unit - k_unit * head_sums(k_unit * dk_unit, ones))
        d_qkv[rows, pl.ds(base, GROUP)] = d_q.astype(BF16)
        d_qkv[rows, pl.ds(base + D, GROUP)] = d_k.astype(BF16)
        return 0

    lax.fori_loop(0, STRIPS, strip, 0)


def weight_terms(p, normed_t, cot_t, d_qkv, ob, terms):
    def plane(z, _):
        rows = pl.ds(pl.multiple_of(z * 256, 256), 256)
        base = pl.multiple_of(p * GROUP, GROUP)
        n = normed_t[rows, :]
        g_q = dot(n, d_qkv[:, pl.ds(base, GROUP)])
        g_k = dot(n, d_qkv[:, pl.ds(base + D, GROUP)])
        g_v = dot(n, d_qkv[:, pl.ds(base + 2 * D, GROUP)])
        g_o = dot(cot_t[rows, :], ob[...])
        for unit in range(32):
            y_lo, core, x, y_hi = unit // 16, unit // 8 % 2, unit // 2 % 4, unit % 2
            y = y_hi * 2 + y_lo
            part = slice(unit * 8, unit * 8 + 8)
            first = jnp.concatenate([g_q[part], g_k[part]], axis=0)
            second = jnp.concatenate([g_v[part], g_o[part]], axis=0)
            terms[p, core, 0, x, y, z] = first.astype(BF16)
            terms[p, core, 1, z, y, x] = second.astype(BF16)
        return 0

    lax.fori_loop(0, 4, plane, 0)


def normed_grad(n, w_qkv, d_qkv, d_normed):
    cols = pl.ds(pl.multiple_of(n * 256, 256), 256)
    d_normed[:, cols] = dot(d_qkv[...], w_qkv[cols, :], NT)


def token_grad(x, inv_rms, d_normed, d_ext):
    def strip(s, _):
        rows = pl.ds(pl.multiple_of(s * STRIP, 16), STRIP)
        xf = x[rows, :].astype(F32)
        dn = d_normed[rows, :]
        inv = inv_rms[rows, :]
        pull = jnp.mean(dn * xf, axis=-1, keepdims=True) * (inv * inv * inv)
        d_ext[pl.ds(pl.multiple_of(s * STRIP + BAND, 16), STRIP), :] = (inv * dn - xf * pull).astype(BF16)
        return 0

    lax.fori_loop(0, STRIPS, strip, 0)


def assemble(d_ext, d_edges, d_tokens):
    is_edge = lax.broadcasted_iota(jnp.int32, (STRIP, 1), 0) % COLS < HALF

    def strip(s, _):
        start = pl.multiple_of(s * STRIP, 16)
        own = d_ext[pl.ds(start, STRIP + 16), :].astype(F32)[8 : 8 + STRIP]
        spread = edge_spread(s, lambda row: row >= HALF, (-HALF * HALF, EDGE + HALF))
        d_tokens[pl.ds(start, STRIP), :] = jnp.where(is_edge, dot(spread, d_edges[...]), own).astype(BF16)
        return 0

    lax.fori_loop(0, STRIPS, strip, 0)


def pair_bias(row_valid, bias):
    query = lax.broadcasted_iota(jnp.int32, (STRIP, STRIP), 0)
    key = lax.broadcasted_iota(jnp.int32, (STRIP, STRIP), 1)
    window = lambda t: (t % COLS + COLS - HALF) % COLS // WIN
    half = lambda t: t // (HALF * COLS)
    same_window = window(query) == window(key)
    same_half = half(query) == half(key)
    lat, bands = lax.axis_index("lat"), lax.axis_size("lat")
    open_bias = jnp.where(same_window, -SHARP * LOG2E, BLOCKED)
    seam_bias = jnp.where(same_window & same_half, -SHARP * LOG2E, BLOCKED)
    others = jnp.where(query == key, 0.0, BLOCKED)
    key_row = lax.broadcasted_iota(jnp.int32, (1, STRIP), 1) // COLS
    for s in range(STRIPS):
        base = open_bias if s < STRIPS - 1 else jnp.where(lat == bands - 1, seam_bias, open_bias)
        invalid = jnp.zeros((1, STRIP), F32)
        for i in range(WIN):
            flag = 1.0 - row_valid[(lat * ROWS + s * WIN + i + HALF) % (ROWS * bands)].astype(F32)
            invalid = jnp.where(key_row == i, flag, invalid)
        bias[s] = base + others * invalid


def neighbour(lat_step, lon_step):
    lon, lons = lax.axis_index("lon"), lax.axis_size("lon")
    lat, lats = lax.axis_index("lat"), lax.axis_size("lat")
    return {"lon": (lon + lon_step + lons) % lons, "lat": (lat + lat_step + lats) % lats}


def remote(source, target, send, recv, slot, peer):
    return pltpu.make_async_remote_copy(
        src_ref=source, dst_ref=target, send_sem=send.at[slot], recv_sem=recv.at[slot], device_id=peer, device_id_type=MESH
    )


def window_kernel(
    tokens, cotangent, w_qkv_hbm, w_out_hbm, row_valid, d_tokens, grad_qkv, grad_out,
    x_ext, cot_ext, w_qkv, w_out, edge_out, edges, d_ext, d_edge_out, d_edges,
    bias, x, cot, normed, normed_t, cot_t, inv_rms, qb, kb, vb, dab, ob, d_qkv, d_normed, terms,
    got_0, got_1, sum_1, got_2, sum_2, got_3, sum_3, send, recv, halo_send, halo_recv, load,
):
    greet()
    loads = [
        pltpu.make_async_copy(tokens, x_ext.at[0:LOCAL], load.at[0]),
        pltpu.make_async_copy(cotangent, cot_ext.at[0:LOCAL], load.at[1]),
        pltpu.make_async_copy(w_qkv_hbm, w_qkv, load.at[2]),
        pltpu.make_async_copy(w_out_hbm, w_out, load.at[3]),
    ]
    for copy in loads:
        copy.start()
    pair_bias(row_valid, bias)
    pick = edge_pick()
    for copy in loads[:2]:
        copy.wait()
    met()
    up, left, corner = neighbour(-1, 0), neighbour(0, -1), neighbour(-1, -1)
    halos = [
        remote(x_ext.at[0:BAND], x_ext.at[LOCAL : LOCAL + BAND], halo_send, halo_recv, 0, up),
        remote(cot_ext.at[0:BAND], cot_ext.at[LOCAL : LOCAL + BAND], halo_send, halo_recv, 1, up),
        remote(edge_out, edges.at[:, 0:EDGE], halo_send, halo_recv, 2, left),
        remote(edge_out.at[:, 0:16], edges.at[:, EDGE:EDGES], halo_send, halo_recv, 3, corner),
    ]
    halos[0].start()
    halos[1].start()
    edge_out[0] = dot(pick, x_ext[0:LOCAL, :]).astype(BF16)
    edge_out[1] = dot(pick, cot_ext[0:LOCAL, :]).astype(BF16)
    halos[2].start()
    halos[3].start()
    for copy in halos:
        copy.wait_recv()
    prologue(x_ext, cot_ext, edges, x, cot, normed, normed_t, cot_t, inv_rms)
    for copy in loads[2:]:
        copy.wait()
    first = lambda p: rs_first(p, terms, got_0, got_1, send, recv)
    second = lambda p: rs_next(p, 0, terms, got_1, sum_1, got_2, send, recv)
    third = lambda p: rs_next(p, 1, sum_1, got_2, sum_2, got_3, send, recv)
    last = lambda p: rs_next(p, 2, sum_2, got_3, sum_3, None, send, recv)

    def chunk(p, _):
        project(p, cot, w_qkv, w_out, normed, qb, kb, vb, dab)
        pl.when(p > 0)(lambda: first(p - 1))
        attend(p, bias, qb, kb, vb, dab, ob, d_qkv)
        pl.when(p > 1)(lambda: third(p - 2))
        weight_terms(p, normed_t, cot_t, d_qkv, ob, terms)
        rs_start(p, terms, got_0, send, recv)
        pl.when(p > 0)(lambda: second(p - 1))
        return 0

    lax.fori_loop(0, CHUNKS, chunk, 0)

    def tail(n, _):
        normed_grad(n, w_qkv, d_qkv, d_normed)
        pl.when(n == 0)(lambda: first(CHUNKS - 1))
        pl.when(n == 1)(lambda: third(CHUNKS - 2))
        return 0

    lax.fori_loop(0, D // 256, tail, 0)
    token_grad(x, inv_rms, d_normed, d_ext)
    down, right, far_corner = neighbour(1, 0), neighbour(0, 1), neighbour(1, 1)
    returns = [
        remote(d_ext.at[LOCAL : LOCAL + BAND], d_ext.at[0:BAND], halo_send, halo_recv, 4, down),
        remote(d_edge_out, d_edges.at[0:EDGE], halo_send, halo_recv, 5, right),
        remote(d_edge_out.at[EDGE - 16 : EDGE], d_edges.at[EDGE:EDGES], halo_send, halo_recv, 6, far_corner),
    ]
    returns[0].start()
    d_edge_out[...] = dot(edge_pick(), d_ext[BAND : BAND + LOCAL, :]).astype(BF16)
    returns[1].start()
    returns[2].start()
    second(CHUNKS - 1)
    for copy in returns:
        copy.wait_recv()
    assemble(d_ext, d_edges, d_tokens)
    third(CHUNKS - 1)
    lax.fori_loop(0, CHUNKS, lambda p, _: (last(p), 0)[1], 0)
    write_grads(sum_3, grad_qkv, grad_out)
    rs_finish(terms, got_0, (terms, sum_1, sum_2), (got_1, got_2, got_3), send, recv)
    for copy in halos + returns:
        copy.wait_send()


TERMS = (CHUNKS, 2, 2, 4, 4, 4, 16, GROUP)


def window_call(tokens, cotangent, w_qkv, w_out, row_valid):
    vmem = pl.BlockSpec(memory_space=pltpu.VMEM)
    anywhere = pl.BlockSpec(memory_space=pl.ANY)
    return pl.pallas_call(
        window_kernel,
        out_shape=(
            jax.ShapeDtypeStruct((LOCAL, D), BF16),
            jax.ShapeDtypeStruct((8, 3 * D), F32),
            jax.ShapeDtypeStruct((8, D), F32),
        ),
        in_specs=[anywhere] * 4 + [pl.BlockSpec(memory_space=pltpu.SMEM)],
        out_specs=(vmem, vmem, vmem),
        scratch_shapes=[
            pltpu.VMEM((LOCAL + BAND, D), BF16),
            pltpu.VMEM((LOCAL + BAND, D), BF16),
            pltpu.VMEM((D, 3 * D), BF16),
            pltpu.VMEM((D, D), BF16),
            pltpu.VMEM((2, EDGE, D), BF16),
            pltpu.VMEM((2, EDGES, D), BF16),
            pltpu.VMEM((BAND + LOCAL, D), BF16),
            pltpu.VMEM((EDGE, D), BF16),
            pltpu.VMEM((EDGES, D), BF16),
            pltpu.VMEM((STRIPS, STRIP, STRIP), F32),
            pltpu.VMEM((LOCAL, D), BF16),
            pltpu.VMEM((LOCAL, D), BF16),
            pltpu.VMEM((LOCAL, D), BF16),
            pltpu.VMEM((D, LOCAL), BF16),
            pltpu.VMEM((D, LOCAL), BF16),
            pltpu.VMEM((LOCAL, 1), F32),
            pltpu.VMEM((LOCAL, GROUP), BF16),
            pltpu.VMEM((LOCAL, GROUP), BF16),
            pltpu.VMEM((LOCAL, GROUP), BF16),
            pltpu.VMEM((LOCAL, GROUP), BF16),
            pltpu.VMEM((LOCAL, GROUP), BF16),
            pltpu.VMEM((LOCAL, 3 * D), BF16),
            pltpu.VMEM((LOCAL, D), F32),
            pltpu.VMEM(TERMS, BF16),
        ]
        + scatter_scratch()
        + [pltpu.SemaphoreType.DMA((7,)), pltpu.SemaphoreType.DMA((7,)), pltpu.SemaphoreType.DMA((4,))],
        compiler_params=pltpu.CompilerParams(
            collective_id=0, has_side_effects=True, vmem_limit_bytes=62 * 1024 * 1024
        ),
        name="windows",
    )(tokens, cotangent, w_qkv, w_out, row_valid)


def place():
    lon, lat = lax.axis_index("lon"), lax.axis_index("lat")
    z, y_lo, core = lon // 4, lon // 2 % 2, lon % 2
    x, y_hi = lat // 2, lat % 2
    return x, y_hi * 2 + y_lo, z, core


def device(x, y, z, core):
    return {"lon": z * 4 + y % 2 * 2 + core, "lat": x * 2 + y // 2}


def axis_peer(axis, step):
    x, y, z, core = place()
    if axis == "x":
        at = (x + step) % 4
        return at, device(at, y, z, core)
    if axis == "y":
        at = (y + step) % 4
        return at, device(x, at, z, core)
    at = (z + step) % 4
    return at, device(x, y, at, core)


ORDERS = (("x", "y", "z"), ("z", "y", "x"))


AROUND = ((-1, 0), (0, -1), (-1, -1), (1, 0), (0, 1), (1, 1))


def greet():
    x, y, z, core = place()
    peers = [device(x, y, z, 1 - core)]
    peers += [axis_peer(axis, step)[1] for axis in "xyz" for step in (1, 2, 3)]
    peers += [neighbour(*step) for step in AROUND]
    for peer in peers:
        pl.semaphore_signal(pltpu.get_barrier_semaphore(), inc=1, device_id=peer, device_id_type=MESH)


def met():
    pl.semaphore_wait(pltpu.get_barrier_semaphore(), 10 + len(AROUND))


def core_copy(p, terms, got_0, send, recv):
    x, y, z, core = place()
    return pltpu.make_async_remote_copy(
        src_ref=terms.at[p, 1 - core],
        dst_ref=got_0.at[p],
        send_sem=send.at[p, 0, 0],
        recv_sem=recv.at[p, 0, 0],
        device_id=device(x, y, z, 1 - core),
        device_id_type=MESH,
    )


def stage_copy(p, stage, half, step, source, target, send, recv):
    at, peer = axis_peer(ORDERS[half][stage], step)
    slot = 3 * half + step - 1
    return pltpu.make_async_remote_copy(
        src_ref=source.at[p, place()[3], half, at] if stage == 0 else source.at[p, half, at],
        dst_ref=target.at[p, half, step - 1],
        send_sem=send.at[p, 1 + stage, slot],
        recv_sem=recv.at[p, 1 + stage, slot],
        device_id=peer,
        device_id_type=MESH,
    )


STEPS = [(half, step) for half in (0, 1) for step in (1, 2, 3)]


def my_index(stage, half):
    x, y, z, _ = place()
    return {"x": x, "y": y, "z": z}[ORDERS[half][stage]]


def rs_start(p, terms, got_0, send, recv):
    core_copy(p, terms, got_0, send, recv).start()


def rs_first(p, terms, got_0, got_1, send, recv):
    core = place()[3]
    core_copy(p, terms, got_0, send, recv).wait_recv()
    for half in (0, 1):
        for a in range(4):
            terms[p, core, half, a] = terms[p, core, half, a] + got_0[p, half, a]
    for half, step in STEPS:
        stage_copy(p, 0, half, step, terms, got_1, send, recv).start()


def rs_next(p, stage, source, got, total, after, send, recv):
    for half, step in STEPS:
        stage_copy(p, stage, half, step, source, got, send, recv).wait_recv()
    for half in (0, 1):
        index = (half, my_index(stage, half))
        mine = source[(p, place()[3]) + index if stage == 0 else (p,) + index].astype(F32)
        for i in range(3):
            mine = mine + got[p, half, i].astype(F32)
        total[p, half] = mine.astype(total.dtype)
    if after is not None:
        for half, step in STEPS:
            stage_copy(p, stage + 1, half, step, total, after, send, recv).start()


def rs_finish(terms, got_0, sums, gots, send, recv):
    def one(p, _):
        core_copy(p, terms, got_0, send, recv).wait_send()
        for stage in range(3):
            for half, step in STEPS:
                stage_copy(p, stage, half, step, sums[stage], gots[stage], send, recv).wait_send()
        return 0

    lax.fori_loop(0, CHUNKS, one, 0)


def write_grads(sum_3, grad_qkv, grad_out):
    scale = 1.0 / math.sqrt(LOCAL * 128)
    for p in range(CHUNKS):
        at = p * GROUP
        grad_qkv[:, at : at + GROUP] = sum_3[p, 0, :8, :] * scale
        grad_qkv[:, D + at : D + at + GROUP] = sum_3[p, 0, 8:, :] * scale
        grad_qkv[:, 2 * D + at : 2 * D + at + GROUP] = sum_3[p, 1, :8, :] * scale
        grad_out[:, at : at + GROUP] = sum_3[p, 1, 8:, :] * scale


def scatter_scratch():
    unit = (16, GROUP)
    return [
        pltpu.VMEM((CHUNKS, 2, 4, 4, 4) + unit, BF16),
        pltpu.VMEM((CHUNKS, 2, 3, 4, 4) + unit, BF16),
        pltpu.VMEM((CHUNKS, 2, 4, 4) + unit, BF16),
        pltpu.VMEM((CHUNKS, 2, 3, 4) + unit, BF16),
        pltpu.VMEM((CHUNKS, 2, 4) + unit, BF16),
        pltpu.VMEM((CHUNKS, 2, 3) + unit, BF16),
        pltpu.VMEM((CHUNKS, 2) + unit, F32),
        pltpu.SemaphoreType.DMA((CHUNKS, 4, 6)),
        pltpu.SemaphoreType.DMA((CHUNKS, 4, 6)),
    ]


def on_device(tokens, cotangent, w_qkv, w_out, row_valid):
    flat = (LOCAL, D)
    d_tokens, grad_qkv, grad_out = window_call(tokens.reshape(flat), cotangent.reshape(flat), w_qkv, w_out, row_valid)
    return (d_tokens.reshape(tokens.shape), grad_qkv, grad_out)


def solution(mesh):
    placed = (P("lat", "lon", None), P("lat", "lon", None), P(), P(), P())
    return jax.shard_map(
        on_device,
        mesh=mesh,
        in_specs=placed,
        out_specs=(P("lat", "lon", None), P(("lon", "lat"), None), P(("lon", "lat"), None)),
        check_vma=False,
    )
```

```python
import math

import jax
import jax.numpy as jnp
from jax import lax
from jax.experimental import pallas as pl
from jax.experimental.pallas import tpu as pltpu
from jax.sharding import PartitionSpec as P

D = 1024
HEADS = 16
WIN = 6
HEAD_DIM = 64
HALF = 3
ROWS = 36
COLS = 24
LOCAL = ROWS * COLS
STRIPS = ROWS // WIN
STRIP = WIN * COLS
GROUP = 256
CHUNKS = D // GROUP
GROUP_HEADS = GROUP // HEAD_DIM
STACK = GROUP_HEADS * STRIP
EDGE = 112
EDGES = 128
BAND = 80
EARLY = STRIP * (STRIPS - 1)

SHARP = 10.0
LOG2E = math.log2(math.e)
EPSILON = 1e-06
BLOCKED = -1e30

F32 = jnp.float32
BF16 = jnp.bfloat16
MESH = pl.DeviceIdType.MESH
NN = (((1,), (0,)), ((), ()))
NT = (((1,), (1,)), ((), ()))
TN = (((0,), (0,)), ((), ()))


def dot(a, b, dims=NN):
    return lax.dot_general(a, b, dims, preferred_element_type=F32)


def head_sums(a, b, ones):
    both = dot(jnp.concatenate([a, b], axis=0), ones)
    return both[:STRIP], both[STRIP:]


def by_head(t):
    lane = lax.broadcasted_iota(jnp.int32, t.shape, 1) // HEAD_DIM
    zero = jnp.zeros_like(t)
    return jnp.concatenate([jnp.where(lane == h, t, zero) for h in range(GROUP_HEADS)], axis=0)


def pick_heads(t):
    lane = lax.broadcasted_iota(jnp.int32, (STRIP, GROUP), 1) // HEAD_DIM
    out = t[:STRIP]
    for h in range(1, GROUP_HEADS):
        out = jnp.where(lane == h, t[h * STRIP : (h + 1) * STRIP], out)
    return out


def shift_rows(ext, s):
    return ext[pl.ds(pl.multiple_of(s * STRIP + 64, 16), STRIP + 16), :].astype(F32)[8 : 8 + STRIP]


def edge_pick():
    at = lax.broadcasted_iota(jnp.int32, (EDGE, LOCAL), 0)
    token = lax.broadcasted_iota(jnp.int32, (EDGE, LOCAL), 1)
    return jnp.where(token == at // HALF * COLS + at % HALF, 1.0, 0.0).astype(BF16)


def edge_spread(s, near, far):
    token = lax.broadcasted_iota(jnp.int32, (STRIP, EDGES), 0)
    at = lax.broadcasted_iota(jnp.int32, (STRIP, EDGES), 1)
    row, col = s * WIN + token // COLS, token % COLS
    source = jnp.where(near(row), far[0] + HALF * row + col, far[1] + HALF * row + col)
    return jnp.where((col < HALF) & (at == source), 1.0, 0.0).astype(BF16)


def normalize(strips, x_ext, cot_ext, edges, x, cot, normed, inv_rms):
    is_edge = lax.broadcasted_iota(jnp.int32, (STRIP, 1), 0) % COLS < HALF

    def norm_strip(s, _):
        rows = pl.ds(pl.multiple_of(s * STRIP, 16), STRIP)
        spread = edge_spread(s, lambda row: row < ROWS - HALF, (HALF * HALF, EDGE - HALF * (ROWS - HALF)))
        cot[rows, :] = jnp.where(is_edge, dot(spread, edges[1]), shift_rows(cot_ext, s)).astype(BF16)
        xf = jnp.where(is_edge, dot(spread, edges[0]), shift_rows(x_ext, s))
        x[rows, :] = xf.astype(BF16)
        inv = lax.rsqrt(jnp.mean(xf * xf, axis=-1, keepdims=True) + EPSILON)
        inv_rms[rows, :] = inv
        normed[rows, :] = (xf * inv).astype(BF16)
        return 0

    lax.fori_loop(*strips, norm_strip, 0)


def turn(blocks, cot, normed, normed_t, cot_t):
    for block in blocks:
        at = block * 128
        end = min(at + 128, LOCAL)
        normed_t[:, at:end] = normed[at:end, :].T
        cot_t[:, at:end] = cot[at:end, :].T


def project(p, start, size, cot, w_qkv, w_out, normed, qb, kb, vb, dab):
    rows = pl.ds(start, size)
    base = pl.multiple_of(p * GROUP, GROUP)
    n = normed[rows, :]
    qb[rows, :] = dot(n, w_qkv[:, pl.ds(base, GROUP)]).astype(BF16)
    kb[rows, :] = dot(n, w_qkv[:, pl.ds(base + D, GROUP)]).astype(BF16)
    vb[rows, :] = dot(n, w_qkv[:, pl.ds(base + 2 * D, GROUP)]).astype(BF16)
    dab[rows, :] = dot(cot[rows, :], w_out[pl.ds(base, GROUP), :], NT).astype(BF16)


def attend(p, strips, bias, qb, kb, vb, dab, ob, d_qkv):
    row_head = lax.broadcasted_iota(jnp.int32, (GROUP, GROUP), 0) // HEAD_DIM
    col_head = lax.broadcasted_iota(jnp.int32, (GROUP, GROUP), 1) // HEAD_DIM
    ones = jnp.where(row_head == col_head, 1.0, 0.0).astype(BF16)

    def strip(s, _):
        rows = pl.ds(pl.multiple_of(s * STRIP, 16), STRIP)
        base = pl.multiple_of(p * GROUP, GROUP)
        q, k = qb[rows, :], kb[rows, :]
        q_squares, k_squares = head_sums(q * q, k * k, ones)
        inv_q = lax.rsqrt(q_squares + EPSILON)
        inv_k = lax.rsqrt(k_squares + EPSILON)
        q_unit = q * inv_q
        k_unit = k * inv_k
        q_heads = by_head(q_unit.astype(BF16))
        k_round = k_unit.astype(BF16)
        v = vb[rows, :]
        da_heads = by_head(dab[rows, :])
        scores = dot(q_heads, k_round, NT).reshape(GROUP_HEADS, STRIP, STRIP)
        weights = jnp.exp2(scores * (SHARP * LOG2E) + bias[s][None])
        total = jnp.sum(weights, axis=-1, keepdims=True)
        probs = weights * (1.0 / total)
        prob_round = probs.astype(BF16).reshape(STACK, STRIP)
        d_probs = dot(da_heads, v, NT).reshape(GROUP_HEADS, STRIP, STRIP)
        mixed = jnp.sum(probs * d_probs, axis=-1, keepdims=True)
        ds_round = (probs * (d_probs - mixed)).astype(BF16).reshape(STACK, STRIP)
        ob[rows, :] = pick_heads(dot(prob_round, v)).astype(BF16)
        d_qkv[rows, pl.ds(base + 2 * D, GROUP)] = dot(prob_round, da_heads, TN).astype(BF16)
        dq_unit = SHARP * pick_heads(dot(ds_round, k_round))
        dk_unit = SHARP * dot(ds_round, q_heads, TN)
        q_along, k_along = head_sums((q_unit * dq_unit).astype(BF16), (k_unit * dk_unit).astype(BF16), ones)
        d_q = inv_q * (dq_unit - q_unit * q_along)
        d_k = inv_k * (dk_unit - k_unit * k_along)
        d_qkv[rows, pl.ds(base, GROUP)] = d_q.astype(BF16)
        d_qkv[rows, pl.ds(base + D, GROUP)] = d_k.astype(BF16)
        return 0

    lax.fori_loop(*strips, strip, 0, unroll=strips[1] - strips[0])


def weight_terms(p, half, normed_t, cot_t, d_qkv, ob, terms):
    def plane(z, _):
        rows = pl.ds(pl.multiple_of(z * 256, 256), 256)
        base = pl.multiple_of(p * GROUP, GROUP)
        n = normed_t[rows, :]
        if half == 0:
            upper = dot(n, d_qkv[:, pl.ds(base, GROUP)])
            lower = dot(n, d_qkv[:, pl.ds(base + D, GROUP)])
        else:
            upper = dot(n, d_qkv[:, pl.ds(base + 2 * D, GROUP)])
            lower = dot(cot_t[rows, :], ob[...])
        for unit in range(32):
            y_lo, core, x, y_hi = unit // 16, unit // 8 % 2, unit // 2 % 4, unit % 2
            y = y_hi * 2 + y_lo
            part = slice(unit * 8, unit * 8 + 8)
            both = jnp.concatenate([upper[part], lower[part]], axis=0).astype(BF16)
            terms[(p, core, half) + ((x, y, z) if half == 0 else (z, y, x))] = both
        return 0

    lax.fori_loop(0, 4, plane, 0)


def normed_grad(start, size, n, w_qkv, d_qkv, d_normed):
    cols = pl.ds(pl.multiple_of(n * 256, 256), 256)
    d_normed[start : start + size, cols] = dot(d_qkv[start : start + size, :], w_qkv[cols, :], NT)


def token_grad(strips, x, inv_rms, d_normed, d_ext):
    def strip(s, _):
        rows = pl.ds(pl.multiple_of(s * STRIP, 16), STRIP)
        xf = x[rows, :].astype(F32)
        dn = d_normed[rows, :]
        inv = inv_rms[rows, :]
        pull = jnp.mean(dn * xf, axis=-1, keepdims=True) * (inv * inv * inv)
        d_ext[pl.ds(pl.multiple_of(s * STRIP + BAND, 16), STRIP), :] = (inv * dn - xf * pull).astype(BF16)
        return 0

    lax.fori_loop(*strips, strip, 0)


def assemble(d_ext, d_edges, d_tokens):
    is_edge = lax.broadcasted_iota(jnp.int32, (STRIP, 1), 0) % COLS < HALF

    def strip(s, _):
        start = pl.multiple_of(s * STRIP, 16)
        own = d_ext[pl.ds(start, STRIP + 16), :].astype(F32)[8 : 8 + STRIP]
        spread = edge_spread(s, lambda row: row >= HALF, (-HALF * HALF, EDGE + HALF))
        d_tokens[pl.ds(start, STRIP), :] = jnp.where(is_edge, dot(spread, d_edges[...]), own).astype(BF16)
        return 0

    lax.fori_loop(0, STRIPS, strip, 0)


def pair_bias(row_valid, bias):
    query = lax.broadcasted_iota(jnp.int32, (STRIP, STRIP), 0)
    key = lax.broadcasted_iota(jnp.int32, (STRIP, STRIP), 1)
    window = lambda t: (t % COLS + COLS - HALF) % COLS // WIN
    half = lambda t: t // (HALF * COLS)
    same_window = window(query) == window(key)
    same_half = half(query) == half(key)
    lat, bands = lax.axis_index("lat"), lax.axis_size("lat")
    open_bias = jnp.where(same_window, -SHARP * LOG2E, BLOCKED)
    seam_bias = jnp.where(same_window & same_half, -SHARP * LOG2E, BLOCKED)
    others = jnp.where(query == key, 0.0, BLOCKED)
    key_row = lax.broadcasted_iota(jnp.int32, (1, STRIP), 1) // COLS
    for s in range(STRIPS):
        base = open_bias if s < STRIPS - 1 else jnp.where(lat == bands - 1, seam_bias, open_bias)
        invalid = jnp.zeros((1, STRIP), F32)
        for i in range(WIN):
            flag = 1.0 - row_valid[(lat * ROWS + s * WIN + i + HALF) % (ROWS * bands)].astype(F32)
            invalid = jnp.where(key_row == i, flag, invalid)
        bias[s] = base + others * invalid


def neighbour(lat_step, lon_step):
    lon, lons = lax.axis_index("lon"), lax.axis_size("lon")
    lat, lats = lax.axis_index("lat"), lax.axis_size("lat")
    return {"lon": (lon + lon_step + lons) % lons, "lat": (lat + lat_step + lats) % lats}


def remote(source, target, send, recv, slot, peer):
    return pltpu.make_async_remote_copy(
        src_ref=source, dst_ref=target, send_sem=send.at[slot], recv_sem=recv.at[slot], device_id=peer, device_id_type=MESH
    )


def window_kernel(
    tokens, cotangent, w_qkv_hbm, w_out_hbm, row_valid, d_tokens, grad_qkv, grad_out,
    x_ext, cot_ext, w_qkv, w_out, edge_out, edges, d_ext, d_edge_out, d_edges,
    bias, x, cot, normed, normed_t, cot_t, inv_rms, qb, kb, vb, dab, ob, d_qkv, d_normed, terms,
    got_0, got_1, sum_1, got_2, sum_2, got_3, sum_3, send, recv, halo_send, halo_recv, load,
):
    greet()
    loads = [
        pltpu.make_async_copy(tokens, x_ext.at[0:LOCAL], load.at[0]),
        pltpu.make_async_copy(cotangent, cot_ext.at[0:LOCAL], load.at[1]),
        pltpu.make_async_copy(w_qkv_hbm, w_qkv, load.at[2]),
        pltpu.make_async_copy(w_out_hbm, w_out, load.at[3]),
    ]
    for copy in loads:
        copy.start()
    pair_bias(row_valid, bias)
    pick = edge_pick()
    for copy in loads[:2]:
        copy.wait()
    met()
    up, left, corner = neighbour(-1, 0), neighbour(0, -1), neighbour(-1, -1)
    halos = [
        remote(x_ext.at[0:BAND], x_ext.at[LOCAL : LOCAL + BAND], halo_send, halo_recv, 0, up),
        remote(cot_ext.at[0:BAND], cot_ext.at[LOCAL : LOCAL + BAND], halo_send, halo_recv, 1, up),
        remote(edge_out, edges.at[:, 0:EDGE], halo_send, halo_recv, 2, left),
        remote(edge_out.at[:, 0:16], edges.at[:, EDGE:EDGES], halo_send, halo_recv, 3, corner),
    ]
    edge_out[0] = dot(pick, x_ext[0:LOCAL, :]).astype(BF16)
    edge_out[1] = dot(pick, cot_ext[0:LOCAL, :]).astype(BF16)
    halos[2].start()
    halos[3].start()
    halos[0].start()
    halos[1].start()
    halos[2].wait_recv()
    halos[3].wait_recv()
    early, late = (0, STRIPS - 1), (STRIPS - 1, STRIPS)
    normalize(early, x_ext, cot_ext, edges, x, cot, normed, inv_rms)
    turn(range(5), cot, normed, normed_t, cot_t)
    for copy in loads[2:]:
        copy.wait()
    first = lambda p, half: rs_first(p, half, terms, got_0, got_1, send, recv)
    second = lambda p, half: rs_next(p, half, 0, terms, got_1, sum_1, got_2, send, recv)
    third = lambda p, half: rs_next(p, half, 1, sum_1, got_2, sum_2, got_3, send, recv)
    last = lambda p, half: rs_next(p, half, 2, sum_2, got_3, sum_3, None, send, recv)

    def finish_halo():
        halos[0].wait_recv()
        halos[1].wait_recv()
        normalize(late, x_ext, cot_ext, edges, x, cot, normed, inv_rms)
        turn(range(5, 7), cot, normed, normed_t, cot_t)

    def chunk(p, _):
        project(p, 0, EARLY, cot, w_qkv, w_out, normed, qb, kb, vb, dab)
        pl.when(p > 0)(lambda: first(p - 1, 0))
        attend(p, early, bias, qb, kb, vb, dab, ob, d_qkv)
        pl.when(p == 0)(finish_halo)
        pl.when(p > 0)(lambda: second(p - 1, 1))
        project(p, EARLY, STRIP, cot, w_qkv, w_out, normed, qb, kb, vb, dab)
        attend(p, late, bias, qb, kb, vb, dab, ob, d_qkv)
        pl.when(p > 0)(lambda: second(p - 1, 0))
        weight_terms(p, 1, normed_t, cot_t, d_qkv, ob, terms)
        core_copy(p, 1, terms, got_0, send, recv).start()
        pl.when(p > 0)(lambda: third(p - 1, 1))
        weight_terms(p, 0, normed_t, cot_t, d_qkv, ob, terms)
        core_copy(p, 0, terms, got_0, send, recv).start()
        pl.when(p > 0)(lambda: third(p - 1, 0))
        first(p, 1)
        return 0

    lax.fori_loop(0, CHUNKS, chunk, 0)
    end = CHUNKS - 1
    down, right, far_corner = neighbour(1, 0), neighbour(0, 1), neighbour(1, 1)
    returns = [
        remote(d_ext.at[LOCAL : LOCAL + BAND], d_ext.at[0:BAND], halo_send, halo_recv, 4, down),
        remote(d_edge_out, d_edges.at[0:EDGE], halo_send, halo_recv, 5, right),
        remote(d_edge_out.at[EDGE - 16 : EDGE], d_edges.at[EDGE:EDGES], halo_send, halo_recv, 6, far_corner),
    ]
    lax.fori_loop(0, D // 256, lambda n, _: (normed_grad(EARLY, STRIP, n, w_qkv, d_qkv, d_normed), 0)[1], 0)
    first(end, 0)
    token_grad(late, x, inv_rms, d_normed, d_ext)
    returns[0].start()
    lax.fori_loop(0, D // 256, lambda n, _: (normed_grad(0, EARLY, n, w_qkv, d_qkv, d_normed), 0)[1], 0)
    token_grad(early, x, inv_rms, d_normed, d_ext)
    d_edge_out[...] = dot(edge_pick(), d_ext[BAND : BAND + LOCAL, :]).astype(BF16)
    returns[1].start()
    returns[2].start()
    second(end, 1)
    second(end, 0)
    for copy in returns:
        copy.wait_recv()
    assemble(d_ext, d_edges, d_tokens)
    third(end, 1)
    third(end, 0)
    for half in (0, 1):
        lax.fori_loop(0, CHUNKS, lambda p, _: (last(p, half), 0)[1], 0)
    write_grads(sum_3, grad_qkv, grad_out)
    rs_finish(terms, got_0, (terms, sum_1, sum_2), (got_1, got_2, got_3), send, recv)
    for copy in halos + returns:
        copy.wait_send()


TERMS = (CHUNKS, 2, 2, 4, 4, 4, 16, GROUP)


def window_call(tokens, cotangent, w_qkv, w_out, row_valid):
    vmem = pl.BlockSpec(memory_space=pltpu.VMEM)
    anywhere = pl.BlockSpec(memory_space=pl.ANY)
    return pl.pallas_call(
        window_kernel,
        out_shape=(
            jax.ShapeDtypeStruct((LOCAL, D), BF16),
            jax.ShapeDtypeStruct((8, 3 * D), F32),
            jax.ShapeDtypeStruct((8, D), F32),
        ),
        in_specs=[anywhere] * 4 + [pl.BlockSpec(memory_space=pltpu.SMEM)],
        out_specs=(vmem, vmem, vmem),
        scratch_shapes=[
            pltpu.VMEM((LOCAL + BAND, D), BF16),
            pltpu.VMEM((LOCAL + BAND, D), BF16),
            pltpu.VMEM((D, 3 * D), BF16),
            pltpu.VMEM((D, D), BF16),
            pltpu.VMEM((2, EDGE, D), BF16),
            pltpu.VMEM((2, EDGES, D), BF16),
            pltpu.VMEM((BAND + LOCAL, D), BF16),
            pltpu.VMEM((EDGE, D), BF16),
            pltpu.VMEM((EDGES, D), BF16),
            pltpu.VMEM((STRIPS, STRIP, STRIP), F32),
            pltpu.VMEM((LOCAL, D), BF16),
            pltpu.VMEM((LOCAL, D), BF16),
            pltpu.VMEM((LOCAL, D), BF16),
            pltpu.VMEM((D, LOCAL), BF16),
            pltpu.VMEM((D, LOCAL), BF16),
            pltpu.VMEM((LOCAL, 1), F32),
            pltpu.VMEM((LOCAL, GROUP), BF16),
            pltpu.VMEM((LOCAL, GROUP), BF16),
            pltpu.VMEM((LOCAL, GROUP), BF16),
            pltpu.VMEM((LOCAL, GROUP), BF16),
            pltpu.VMEM((LOCAL, GROUP), BF16),
            pltpu.VMEM((LOCAL, 3 * D), BF16),
            pltpu.VMEM((LOCAL, D), F32),
            pltpu.VMEM(TERMS, BF16),
        ]
        + scatter_scratch()
        + [pltpu.SemaphoreType.DMA((7,)), pltpu.SemaphoreType.DMA((7,)), pltpu.SemaphoreType.DMA((4,))],
        compiler_params=pltpu.CompilerParams(
            collective_id=0, has_side_effects=True, vmem_limit_bytes=62 * 1024 * 1024
        ),
        name="windows",
    )(tokens, cotangent, w_qkv, w_out, row_valid)


def place():
    lon, lat = lax.axis_index("lon"), lax.axis_index("lat")
    z, y_lo, core = lon // 4, lon // 2 % 2, lon % 2
    x, y_hi = lat // 2, lat % 2
    return x, y_hi * 2 + y_lo, z, core


def device(x, y, z, core):
    return {"lon": z * 4 + y % 2 * 2 + core, "lat": x * 2 + y // 2}


def axis_peer(axis, step):
    x, y, z, core = place()
    if axis == "x":
        at = (x + step) % 4
        return at, device(at, y, z, core)
    if axis == "y":
        at = (y + step) % 4
        return at, device(x, at, z, core)
    at = (z + step) % 4
    return at, device(x, y, at, core)


ORDERS = (("x", "y", "z"), ("z", "y", "x"))


AROUND = ((-1, 0), (0, -1), (-1, -1), (1, 0), (0, 1), (1, 1))


def greet():
    x, y, z, core = place()
    peers = [device(x, y, z, 1 - core)]
    peers += [axis_peer(axis, step)[1] for axis in "xyz" for step in (1, 2, 3)]
    peers += [neighbour(*step) for step in AROUND]
    for peer in peers:
        pl.semaphore_signal(pltpu.get_barrier_semaphore(), inc=1, device_id=peer, device_id_type=MESH)


def met():
    pl.semaphore_wait(pltpu.get_barrier_semaphore(), 10 + len(AROUND))


def core_copy(p, half, terms, got_0, send, recv):
    x, y, z, core = place()
    return pltpu.make_async_remote_copy(
        src_ref=terms.at[p, 1 - core, half],
        dst_ref=got_0.at[p, half],
        send_sem=send.at[p, 0, half],
        recv_sem=recv.at[p, 0, half],
        device_id=device(x, y, z, 1 - core),
        device_id_type=MESH,
    )


def stage_copy(p, stage, half, step, source, target, send, recv):
    at, peer = axis_peer(ORDERS[half][stage], step)
    slot = 3 * half + step - 1
    return pltpu.make_async_remote_copy(
        src_ref=source.at[p, place()[3], half, at] if stage == 0 else source.at[p, half, at],
        dst_ref=target.at[p, half, step - 1],
        send_sem=send.at[p, 1 + stage, slot],
        recv_sem=recv.at[p, 1 + stage, slot],
        device_id=peer,
        device_id_type=MESH,
    )


STEPS = [(half, step) for half in (0, 1) for step in (1, 2, 3)]


def my_index(stage, half):
    x, y, z, _ = place()
    return {"x": x, "y": y, "z": z}[ORDERS[half][stage]]


def rs_first(p, half, terms, got_0, got_1, send, recv):
    core = place()[3]
    core_copy(p, half, terms, got_0, send, recv).wait_recv()
    for a in range(4):
        terms[p, core, half, a] = terms[p, core, half, a] + got_0[p, half, a]
    for step in (2, 1, 3):
        stage_copy(p, 0, half, step, terms, got_1, send, recv).start()


def rs_next(p, half, stage, source, got, total, after, send, recv):
    for step in (1, 2, 3):
        stage_copy(p, stage, half, step, source, got, send, recv).wait_recv()
    index = (half, my_index(stage, half))
    mine = source[(p, place()[3]) + index if stage == 0 else (p,) + index].astype(F32)
    for i in range(3):
        mine = mine + got[p, half, i].astype(F32)
    total[p, half] = mine.astype(total.dtype)
    if after is not None:
        for step in (2, 1, 3):
            stage_copy(p, stage + 1, half, step, total, after, send, recv).start()


def rs_finish(terms, got_0, sums, gots, send, recv):
    def one(p, _):
        for half in (0, 1):
            core_copy(p, half, terms, got_0, send, recv).wait_send()
        for stage in range(3):
            for half, step in STEPS:
                stage_copy(p, stage, half, step, sums[stage], gots[stage], send, recv).wait_send()
        return 0

    lax.fori_loop(0, CHUNKS, one, 0)


def write_grads(sum_3, grad_qkv, grad_out):
    scale = 1.0 / math.sqrt(LOCAL * 128)
    for p in range(CHUNKS):
        at = p * GROUP
        grad_qkv[:, at : at + GROUP] = sum_3[p, 0, :8, :] * scale
        grad_qkv[:, D + at : D + at + GROUP] = sum_3[p, 0, 8:, :] * scale
        grad_qkv[:, 2 * D + at : 2 * D + at + GROUP] = sum_3[p, 1, :8, :] * scale
        grad_out[:, at : at + GROUP] = sum_3[p, 1, 8:, :] * scale


def scatter_scratch():
    unit = (16, GROUP)
    return [
        pltpu.VMEM((CHUNKS, 2, 4, 4, 4) + unit, BF16),
        pltpu.VMEM((CHUNKS, 2, 3, 4, 4) + unit, BF16),
        pltpu.VMEM((CHUNKS, 2, 4, 4) + unit, BF16),
        pltpu.VMEM((CHUNKS, 2, 3, 4) + unit, BF16),
        pltpu.VMEM((CHUNKS, 2, 4) + unit, BF16),
        pltpu.VMEM((CHUNKS, 2, 3) + unit, BF16),
        pltpu.VMEM((CHUNKS, 2) + unit, F32),
        pltpu.SemaphoreType.DMA((CHUNKS, 4, 6)),
        pltpu.SemaphoreType.DMA((CHUNKS, 4, 6)),
    ]


def on_device(tokens, cotangent, w_qkv, w_out, row_valid):
    flat = (LOCAL, D)
    d_tokens, grad_qkv, grad_out = window_call(tokens.reshape(flat), cotangent.reshape(flat), w_qkv, w_out, row_valid)
    return (d_tokens.reshape(tokens.shape), grad_qkv, grad_out)


def solution(mesh):
    placed = (P("lat", "lon", None), P("lat", "lon", None), P(), P(), P())
    return jax.shard_map(
        on_device,
        mesh=mesh,
        in_specs=placed,
        out_specs=(P("lat", "lon", None), P(("lon", "lat"), None), P(("lon", "lat"), None)),
        check_vma=False,
    )
```

```python
import math

import jax
import jax.numpy as jnp
from jax import lax
from jax.experimental import pallas as pl
from jax.experimental.pallas import tpu as pltpu
from jax.sharding import PartitionSpec as P

D = 1024
HEADS = 16
WIN = 6
HEAD_DIM = 64
HALF = 3
ROWS = 36
COLS = 24
LOCAL = ROWS * COLS
STRIPS = ROWS // WIN
STRIP = WIN * COLS
GROUP = 256
CHUNKS = D // GROUP
GROUP_HEADS = GROUP // HEAD_DIM
STACK = GROUP_HEADS * STRIP
EDGE = 112
EDGES = 128
BAND = 80
EARLY = STRIP * (STRIPS - 1)

SHARP = 10.0
LOG2E = math.log2(math.e)
EPSILON = 1e-06
BLOCKED = -1e30

F32 = jnp.float32
BF16 = jnp.bfloat16
MESH = pl.DeviceIdType.MESH
NN = (((1,), (0,)), ((), ()))
NT = (((1,), (1,)), ((), ()))
TN = (((0,), (0,)), ((), ()))


def dot(a, b, dims=NN):
    return lax.dot_general(a, b, dims, preferred_element_type=F32)


def head_sums(a, b, ones):
    both = dot(jnp.concatenate([a, b], axis=0), ones)
    return both[:STRIP], both[STRIP:]


def by_head(t):
    lane = lax.broadcasted_iota(jnp.int32, t.shape, 1) // HEAD_DIM
    zero = jnp.zeros_like(t)
    return jnp.concatenate([jnp.where(lane == h, t, zero) for h in range(GROUP_HEADS)], axis=0)


def pick_heads(t):
    lane = lax.broadcasted_iota(jnp.int32, (STRIP, GROUP), 1) // HEAD_DIM
    out = t[:STRIP]
    for h in range(1, GROUP_HEADS):
        out = jnp.where(lane == h, t[h * STRIP : (h + 1) * STRIP], out)
    return out


def shift_rows(ext, s):
    return ext[pl.ds(pl.multiple_of(s * STRIP + 64, 16), STRIP + 16), :].astype(F32)[8 : 8 + STRIP]


def edge_pick():
    at = lax.broadcasted_iota(jnp.int32, (EDGE, LOCAL), 0)
    token = lax.broadcasted_iota(jnp.int32, (EDGE, LOCAL), 1)
    return jnp.where(token == at // HALF * COLS + at % HALF, 1.0, 0.0).astype(BF16)


def corner_pick():
    at = lax.broadcasted_iota(jnp.int32, (16, STRIP), 0) - HALF
    token = lax.broadcasted_iota(jnp.int32, (16, STRIP), 1)
    source = (HALF + (at + HALF) // HALF - 1) * COLS + (at + HALF) % HALF
    return jnp.where((at >= 0) & (at < HALF * HALF) & (token == source), 1.0, 0.0).astype(BF16)


def edge_spread(s, near, far, width=EDGES):
    token = lax.broadcasted_iota(jnp.int32, (STRIP, width), 0)
    at = lax.broadcasted_iota(jnp.int32, (STRIP, width), 1)
    row, col = s * WIN + token // COLS, token % COLS
    source = jnp.where(near(row), far[0] + HALF * row + col, far[1] + HALF * row + col)
    return jnp.where((col < HALF) & (at == source), 1.0, 0.0).astype(BF16)


def normalize(strips, width, x_ext, cot_ext, edges, x, cot, normed, inv_rms):
    is_edge = lax.broadcasted_iota(jnp.int32, (STRIP, 1), 0) % COLS < HALF

    def norm_strip(s, _):
        rows = pl.ds(pl.multiple_of(s * STRIP, 16), STRIP)
        spread = edge_spread(s, lambda row: row < ROWS - HALF, (HALF * HALF, EDGE - HALF * (ROWS - HALF)), width)
        cot[rows, :] = jnp.where(is_edge, dot(spread, edges[1, 0:width, :]), shift_rows(cot_ext, s)).astype(BF16)
        xf = jnp.where(is_edge, dot(spread, edges[0, 0:width, :]), shift_rows(x_ext, s))
        x[rows, :] = xf.astype(BF16)
        inv = lax.rsqrt(jnp.mean(xf * xf, axis=-1, keepdims=True) + EPSILON)
        inv_rms[rows, :] = inv
        normed[rows, :] = (xf * inv).astype(BF16)
        return 0

    lax.fori_loop(*strips, norm_strip, 0)


def turn(blocks, cot, normed, normed_t, cot_t):
    for block in blocks:
        at = block * 128
        end = min(at + 128, LOCAL)
        normed_t[:, at:end] = normed[at:end, :].T
        cot_t[:, at:end] = cot[at:end, :].T


def project(p, start, size, cot, w_qkv, w_out, normed, qb, kb, vb, dab):
    rows = pl.ds(start, size)
    base = pl.multiple_of(p * GROUP, GROUP)
    n = normed[rows, :]
    qb[rows, :] = dot(n, w_qkv[:, pl.ds(base, GROUP)]).astype(BF16)
    kb[rows, :] = dot(n, w_qkv[:, pl.ds(base + D, GROUP)]).astype(BF16)
    vb[rows, :] = dot(n, w_qkv[:, pl.ds(base + 2 * D, GROUP)]).astype(BF16)
    dab[rows, :] = dot(cot[rows, :], w_out[pl.ds(base, GROUP), :], NT).astype(BF16)


def attend(p, strips, unroll, bias, qb, kb, vb, dab, ob, d_qkv):
    row_head = lax.broadcasted_iota(jnp.int32, (GROUP, GROUP), 0) // HEAD_DIM
    col_head = lax.broadcasted_iota(jnp.int32, (GROUP, GROUP), 1) // HEAD_DIM
    ones = jnp.where(row_head == col_head, 1.0, 0.0).astype(BF16)

    def strip(s, _):
        rows = pl.ds(pl.multiple_of(s * STRIP, 16), STRIP)
        base = pl.multiple_of(p * GROUP, GROUP)
        q, k = qb[rows, :], kb[rows, :]
        q_squares, k_squares = head_sums(q * q, k * k, ones)
        inv_q = lax.rsqrt(q_squares + EPSILON)
        inv_k = lax.rsqrt(k_squares + EPSILON)
        q_unit = q * inv_q
        k_unit = k * inv_k
        q_heads = by_head(q_unit.astype(BF16))
        k_round = k_unit.astype(BF16)
        v = vb[rows, :]
        da_heads = by_head(dab[rows, :])
        scores = dot(q_heads, k_round, NT).reshape(GROUP_HEADS, STRIP, STRIP)
        weights = jnp.exp2(scores * (SHARP * LOG2E) + bias[s][None])
        total = jnp.sum(weights, axis=-1, keepdims=True)
        probs = weights * (1.0 / total)
        prob_round = probs.astype(BF16).reshape(STACK, STRIP)
        d_probs = dot(da_heads, v, NT).reshape(GROUP_HEADS, STRIP, STRIP)
        mixed = jnp.sum(probs * d_probs, axis=-1, keepdims=True)
        ds_round = (probs * (d_probs - mixed)).astype(BF16).reshape(STACK, STRIP)
        ob[rows, :] = pick_heads(dot(prob_round, v)).astype(BF16)
        d_qkv[rows, pl.ds(base + 2 * D, GROUP)] = dot(prob_round, da_heads, TN).astype(BF16)
        dq_unit = SHARP * pick_heads(dot(ds_round, k_round))
        dk_unit = SHARP * dot(ds_round, q_heads, TN)
        q_along, k_along = head_sums((q_unit * dq_unit).astype(BF16), (k_unit * dk_unit).astype(BF16), ones)
        d_q = inv_q * (dq_unit - q_unit * q_along)
        d_k = inv_k * (dk_unit - k_unit * k_along)
        d_qkv[rows, pl.ds(base, GROUP)] = d_q.astype(BF16)
        d_qkv[rows, pl.ds(base + D, GROUP)] = d_k.astype(BF16)
        return 0

    lax.fori_loop(*strips, strip, 0, unroll=unroll)


def weight_terms(p, half, normed_t, cot_t, d_qkv, ob, terms):
    base = pl.multiple_of(p * GROUP, GROUP)
    for top in range(0, D, 512):
        n = normed_t[top : top + 512, :]
        if half == 0:
            upper = dot(n, d_qkv[:, pl.ds(base, GROUP)])
            lower = dot(n, d_qkv[:, pl.ds(base + D, GROUP)])
        else:
            upper = dot(n, d_qkv[:, pl.ds(base + 2 * D, GROUP)])
            lower = dot(cot_t[top : top + 512, :], ob[...])
        for at in range(0, 512, 8):
            unit = (top + at) // 8
            z, y_lo, core, x, y_hi = unit // 32, unit // 16 % 2, unit // 8 % 2, unit // 2 % 4, unit % 2
            y = y_hi * 2 + y_lo
            both = jnp.concatenate([upper[at : at + 8], lower[at : at + 8]], axis=0).astype(BF16)
            terms[(p, core, half) + ((x, y, z) if half == 0 else (z, y, x))] = both


def normed_grad(start, size, n, w_qkv, d_qkv, d_normed):
    cols = pl.ds(pl.multiple_of(n * 256, 256), 256)
    d_normed[start : start + size, cols] = dot(d_qkv[start : start + size, :], w_qkv[cols, :], NT)


def token_grad(strips, x, inv_rms, d_normed, d_ext):
    def strip(s, _):
        rows = pl.ds(pl.multiple_of(s * STRIP, 16), STRIP)
        xf = x[rows, :].astype(F32)
        dn = d_normed[rows, :]
        inv = inv_rms[rows, :]
        pull = jnp.mean(dn * xf, axis=-1, keepdims=True) * (inv * inv * inv)
        d_ext[pl.ds(pl.multiple_of(s * STRIP + BAND, 16), STRIP), :] = (inv * dn - xf * pull).astype(BF16)
        return 0

    lax.fori_loop(*strips, strip, 0)


def assemble(d_ext, d_edges, d_tokens):
    is_edge = lax.broadcasted_iota(jnp.int32, (STRIP, 1), 0) % COLS < HALF

    def strip(s, _):
        start = pl.multiple_of(s * STRIP, 16)
        own = d_ext[pl.ds(start, STRIP + 16), :].astype(F32)[8 : 8 + STRIP]
        spread = edge_spread(s, lambda row: row >= HALF, (-HALF * HALF, EDGE + HALF))
        d_tokens[pl.ds(start, STRIP), :] = jnp.where(is_edge, dot(spread, d_edges[...]), own).astype(BF16)
        return 0

    lax.fori_loop(0, STRIPS, strip, 0)


def pair_bias(row_valid, bias):
    query = lax.broadcasted_iota(jnp.int32, (STRIP, STRIP), 0)
    key = lax.broadcasted_iota(jnp.int32, (STRIP, STRIP), 1)
    window = lambda t: (t % COLS + COLS - HALF) % COLS // WIN
    half = lambda t: t // (HALF * COLS)
    same_window = window(query) == window(key)
    same_half = half(query) == half(key)
    lat, bands = lax.axis_index("lat"), lax.axis_size("lat")
    open_bias = jnp.where(same_window, -SHARP * LOG2E, BLOCKED)
    seam_bias = jnp.where(same_window & same_half, -SHARP * LOG2E, BLOCKED)
    others = jnp.where(query == key, 0.0, BLOCKED)
    key_row = lax.broadcasted_iota(jnp.int32, (1, STRIP), 1) // COLS
    for s in range(STRIPS):
        base = open_bias if s < STRIPS - 1 else jnp.where(lat == bands - 1, seam_bias, open_bias)
        invalid = jnp.zeros((1, STRIP), F32)
        for i in range(WIN):
            flag = 1.0 - row_valid[(lat * ROWS + s * WIN + i + HALF) % (ROWS * bands)].astype(F32)
            invalid = jnp.where(key_row == i, flag, invalid)
        bias[s] = base + others * invalid


def neighbour(lat_step, lon_step):
    lon, lons = lax.axis_index("lon"), lax.axis_size("lon")
    lat, lats = lax.axis_index("lat"), lax.axis_size("lat")
    return {"lon": (lon + lon_step + lons) % lons, "lat": (lat + lat_step + lats) % lats}


def remote(source, target, send, recv, slot, peer):
    return pltpu.make_async_remote_copy(
        src_ref=source, dst_ref=target, send_sem=send.at[slot], recv_sem=recv.at[slot], device_id=peer, device_id_type=MESH
    )


def window_kernel(
    tokens, cotangent, w_qkv_hbm, w_out_hbm, row_valid, d_tokens, grad_qkv, grad_out,
    x_ext, cot_ext, w_qkv, w_out, edge_out, edges, d_ext, d_edge_out, d_corner_out, d_edges,
    bias, x, cot, normed, normed_t, cot_t, inv_rms, qb, kb, vb, dab, ob, d_qkv, d_normed, terms,
    got_0, got_1, sum_1, got_2, sum_2, got_3, sum_3, send, recv, halo_send, halo_recv, load,
):
    greet()
    loads = [
        pltpu.make_async_copy(tokens, x_ext.at[0:LOCAL], load.at[0]),
        pltpu.make_async_copy(cotangent, cot_ext.at[0:LOCAL], load.at[1]),
        pltpu.make_async_copy(w_qkv_hbm, w_qkv, load.at[2]),
        pltpu.make_async_copy(w_out_hbm, w_out, load.at[3]),
    ]
    for copy in loads:
        copy.start()
    pair_bias(row_valid, bias)
    pick = edge_pick()
    for copy in loads[:2]:
        copy.wait()
    met()
    up, left, corner = neighbour(-1, 0), neighbour(0, -1), neighbour(-1, -1)
    halos = [
        remote(x_ext.at[0:BAND], x_ext.at[LOCAL : LOCAL + BAND], halo_send, halo_recv, 0, up),
        remote(cot_ext.at[0:BAND], cot_ext.at[LOCAL : LOCAL + BAND], halo_send, halo_recv, 1, up),
        remote(edge_out, edges.at[:, 0:EDGE], halo_send, halo_recv, 2, left),
        remote(edge_out.at[:, 0:16], edges.at[:, EDGE:EDGES], halo_send, halo_recv, 3, corner),
    ]
    edge_out[0] = dot(pick, x_ext[0:LOCAL, :]).astype(BF16)
    edge_out[1] = dot(pick, cot_ext[0:LOCAL, :]).astype(BF16)
    halos[2].start()
    halos[3].start()
    halos[0].start()
    halos[1].start()
    halos[2].wait_recv()
    early, late = (0, STRIPS - 1), (STRIPS - 1, STRIPS)
    normalize(early, EDGE, x_ext, cot_ext, edges, x, cot, normed, inv_rms)
    turn(range(5), cot, normed, normed_t, cot_t)
    for copy in loads[2:]:
        copy.wait()
    first = lambda p, half: rs_first(p, half, terms, got_0, got_1, send, recv)
    second = lambda p, half: rs_next(p, half, 0, terms, got_1, sum_1, got_2, send, recv)
    third = lambda p, half: rs_next(p, half, 1, sum_1, got_2, sum_2, got_3, send, recv)
    last = lambda p, half: rs_next(p, half, 2, sum_2, got_3, sum_3, None, send, recv)

    def finish_halo():
        for i in (0, 1, 3):
            halos[i].wait_recv()
        normalize(late, EDGES, x_ext, cot_ext, edges, x, cot, normed, inv_rms)
        turn(range(5, 7), cot, normed, normed_t, cot_t)

    def both_thirds(p):
        third(p, 1)
        third(p, 0)

    def parts(p):
        project(p, 0, EARLY, cot, w_qkv, w_out, normed, qb, kb, vb, dab)
        attend(p, early, 5, bias, qb, kb, vb, dab, ob, d_qkv)
        finish_halo()
        project(p, EARLY, STRIP, cot, w_qkv, w_out, normed, qb, kb, vb, dab)
        attend(p, late, 1, bias, qb, kb, vb, dab, ob, d_qkv)

    def whole(p):
        project(p, 0, LOCAL, cot, w_qkv, w_out, normed, qb, kb, vb, dab)
        first(p - 1, 0)
        attend(p, (0, STRIPS), 3, bias, qb, kb, vb, dab, ob, d_qkv)
        second(p - 1, 1)
        pl.when(p > 1)(lambda: both_thirds(p - 2))

    def chunk(p, _):
        pl.when(p == 0)(lambda: parts(p))
        pl.when(p > 0)(lambda: whole(p))
        weight_terms(p, 1, normed_t, cot_t, d_qkv, ob, terms)
        core_copy(p, 1, terms, got_0, send, recv).start()
        pl.when(p > 0)(lambda: second(p - 1, 0))
        weight_terms(p, 0, normed_t, cot_t, d_qkv, ob, terms)
        core_copy(p, 0, terms, got_0, send, recv).start()
        first(p, 1)
        return 0

    lax.fori_loop(0, CHUNKS, chunk, 0)
    end = CHUNKS - 1
    down, right, far_corner = neighbour(1, 0), neighbour(0, 1), neighbour(1, 1)
    returns = [
        remote(d_ext.at[LOCAL : LOCAL + BAND], d_ext.at[0:BAND], halo_send, halo_recv, 4, down),
        remote(d_edge_out, d_edges.at[0:EDGE], halo_send, halo_recv, 5, right),
        remote(d_corner_out, d_edges.at[EDGE:EDGES], halo_send, halo_recv, 6, far_corner),
    ]
    lax.fori_loop(0, D // 256, lambda n, _: (normed_grad(EARLY, STRIP, n, w_qkv, d_qkv, d_normed), 0)[1], 0)
    first(end, 0)
    both_thirds(end - 1)
    token_grad(late, x, inv_rms, d_normed, d_ext)
    d_corner_out[...] = dot(corner_pick(), d_ext[BAND + EARLY : BAND + LOCAL, :]).astype(BF16)
    returns[2].start()
    returns[0].start()
    lax.fori_loop(0, D // 256, lambda n, _: (normed_grad(0, EARLY, n, w_qkv, d_qkv, d_normed), 0)[1], 0)
    token_grad(early, x, inv_rms, d_normed, d_ext)
    d_edge_out[...] = dot(edge_pick(), d_ext[BAND : BAND + LOCAL, :]).astype(BF16)
    returns[1].start()
    second(end, 1)
    second(end, 0)
    for copy in returns:
        copy.wait_recv()
    assemble(d_ext, d_edges, d_tokens)
    third(end, 1)
    third(end, 0)
    for half in (0, 1):
        lax.fori_loop(0, CHUNKS, lambda p, _: (last(p, half), 0)[1], 0)
    write_grads(sum_3, grad_qkv, grad_out)
    rs_finish(terms, got_0, (terms, sum_1, sum_2), (got_1, got_2, got_3), send, recv)
    for copy in halos + returns:
        copy.wait_send()


TERMS = (CHUNKS, 2, 2, 4, 4, 4, 16, GROUP)


def window_call(tokens, cotangent, w_qkv, w_out, row_valid):
    vmem = pl.BlockSpec(memory_space=pltpu.VMEM)
    anywhere = pl.BlockSpec(memory_space=pl.ANY)
    return pl.pallas_call(
        window_kernel,
        out_shape=(
            jax.ShapeDtypeStruct((LOCAL, D), BF16),
            jax.ShapeDtypeStruct((8, 3 * D), F32),
            jax.ShapeDtypeStruct((8, D), F32),
        ),
        in_specs=[anywhere] * 4 + [pl.BlockSpec(memory_space=pltpu.SMEM)],
        out_specs=(vmem, vmem, vmem),
        scratch_shapes=[
            pltpu.VMEM((LOCAL + BAND, D), BF16),
            pltpu.VMEM((LOCAL + BAND, D), BF16),
            pltpu.VMEM((D, 3 * D), BF16),
            pltpu.VMEM((D, D), BF16),
            pltpu.VMEM((2, EDGE, D), BF16),
            pltpu.VMEM((2, EDGES, D), BF16),
            pltpu.VMEM((BAND + LOCAL, D), BF16),
            pltpu.VMEM((EDGE, D), BF16),
            pltpu.VMEM((16, D), BF16),
            pltpu.VMEM((EDGES, D), BF16),
            pltpu.VMEM((STRIPS, STRIP, STRIP), F32),
            pltpu.VMEM((LOCAL, D), BF16),
            pltpu.VMEM((LOCAL, D), BF16),
            pltpu.VMEM((LOCAL, D), BF16),
            pltpu.VMEM((D, LOCAL), BF16),
            pltpu.VMEM((D, LOCAL), BF16),
            pltpu.VMEM((LOCAL, 1), F32),
            pltpu.VMEM((LOCAL, GROUP), BF16),
            pltpu.VMEM((LOCAL, GROUP), BF16),
            pltpu.VMEM((LOCAL, GROUP), BF16),
            pltpu.VMEM((LOCAL, GROUP), BF16),
            pltpu.VMEM((LOCAL, GROUP), BF16),
            pltpu.VMEM((LOCAL, 3 * D), BF16),
            pltpu.VMEM((LOCAL, D), F32),
            pltpu.VMEM(TERMS, BF16),
        ]
        + scatter_scratch()
        + [pltpu.SemaphoreType.DMA((7,)), pltpu.SemaphoreType.DMA((7,)), pltpu.SemaphoreType.DMA((4,))],
        compiler_params=pltpu.CompilerParams(
            collective_id=0, has_side_effects=True, vmem_limit_bytes=62 * 1024 * 1024
        ),
        name="windows",
    )(tokens, cotangent, w_qkv, w_out, row_valid)


def place():
    lon, lat = lax.axis_index("lon"), lax.axis_index("lat")
    z, y_lo, core = lon // 4, lon // 2 % 2, lon % 2
    x, y_hi = lat // 2, lat % 2
    return x, y_hi * 2 + y_lo, z, core


def device(x, y, z, core):
    return {"lon": z * 4 + y % 2 * 2 + core, "lat": x * 2 + y // 2}


def axis_peer(axis, step):
    x, y, z, core = place()
    if axis == "x":
        at = (x + step) % 4
        return at, device(at, y, z, core)
    if axis == "y":
        at = (y + step) % 4
        return at, device(x, at, z, core)
    at = (z + step) % 4
    return at, device(x, y, at, core)


ORDERS = (("x", "y", "z"), ("z", "y", "x"))


AROUND = ((-1, 0), (0, -1), (-1, -1), (1, 0), (0, 1), (1, 1))


def greet():
    x, y, z, core = place()
    peers = [device(x, y, z, 1 - core)]
    peers += [axis_peer(axis, step)[1] for axis in "xyz" for step in (1, 2, 3)]
    peers += [neighbour(*step) for step in AROUND]
    for peer in peers:
        pl.semaphore_signal(pltpu.get_barrier_semaphore(), inc=1, device_id=peer, device_id_type=MESH)


def met():
    pl.semaphore_wait(pltpu.get_barrier_semaphore(), 10 + len(AROUND))


def core_copy(p, half, terms, got_0, send, recv):
    x, y, z, core = place()
    return pltpu.make_async_remote_copy(
        src_ref=terms.at[p, 1 - core, half],
        dst_ref=got_0.at[p, half],
        send_sem=send.at[p, 0, half],
        recv_sem=recv.at[p, 0, half],
        device_id=device(x, y, z, 1 - core),
        device_id_type=MESH,
    )


def stage_copy(p, stage, half, step, source, target, send, recv):
    at, peer = axis_peer(ORDERS[half][stage], step)
    slot = 3 * half + step - 1
    return pltpu.make_async_remote_copy(
        src_ref=source.at[p, place()[3], half, at] if stage == 0 else source.at[p, half, at],
        dst_ref=target.at[p, half, step - 1],
        send_sem=send.at[p, 1 + stage, slot],
        recv_sem=recv.at[p, 1 + stage, slot],
        device_id=peer,
        device_id_type=MESH,
    )


STEPS = [(half, step) for half in (0, 1) for step in (1, 2, 3)]


def my_index(stage, half):
    x, y, z, _ = place()
    return {"x": x, "y": y, "z": z}[ORDERS[half][stage]]


def rs_first(p, half, terms, got_0, got_1, send, recv):
    core = place()[3]
    core_copy(p, half, terms, got_0, send, recv).wait_recv()
    for a in range(4):
        terms[p, core, half, a] = terms[p, core, half, a] + got_0[p, half, a]
    for step in (2, 1, 3):
        stage_copy(p, 0, half, step, terms, got_1, send, recv).start()


def rs_next(p, half, stage, source, got, total, after, send, recv):
    for step in (1, 2, 3):
        stage_copy(p, stage, half, step, source, got, send, recv).wait_recv()
    index = (half, my_index(stage, half))
    mine = source[(p, place()[3]) + index if stage == 0 else (p,) + index].astype(F32)
    for i in range(3):
        mine = mine + got[p, half, i].astype(F32)
    total[p, half] = mine.astype(total.dtype)
    if after is not None:
        for step in (2, 1, 3):
            stage_copy(p, stage + 1, half, step, total, after, send, recv).start()


def rs_finish(terms, got_0, sums, gots, send, recv):
    def one(p, _):
        for half in (0, 1):
            core_copy(p, half, terms, got_0, send, recv).wait_send()
        for stage in range(3):
            for half, step in STEPS:
                stage_copy(p, stage, half, step, sums[stage], gots[stage], send, recv).wait_send()
        return 0

    lax.fori_loop(0, CHUNKS, one, 0)


def write_grads(sum_3, grad_qkv, grad_out):
    scale = 1.0 / math.sqrt(LOCAL * 128)
    for p in range(CHUNKS):
        at = p * GROUP
        grad_qkv[:, at : at + GROUP] = sum_3[p, 0, :8, :] * scale
        grad_qkv[:, D + at : D + at + GROUP] = sum_3[p, 0, 8:, :] * scale
        grad_qkv[:, 2 * D + at : 2 * D + at + GROUP] = sum_3[p, 1, :8, :] * scale
        grad_out[:, at : at + GROUP] = sum_3[p, 1, 8:, :] * scale


def scatter_scratch():
    unit = (16, GROUP)
    return [
        pltpu.VMEM((CHUNKS, 2, 4, 4, 4) + unit, BF16),
        pltpu.VMEM((CHUNKS, 2, 3, 4, 4) + unit, BF16),
        pltpu.VMEM((CHUNKS, 2, 4, 4) + unit, BF16),
        pltpu.VMEM((CHUNKS, 2, 3, 4) + unit, BF16),
        pltpu.VMEM((CHUNKS, 2, 4) + unit, BF16),
        pltpu.VMEM((CHUNKS, 2, 3) + unit, BF16),
        pltpu.VMEM((CHUNKS, 2) + unit, F32),
        pltpu.SemaphoreType.DMA((CHUNKS, 4, 6)),
        pltpu.SemaphoreType.DMA((CHUNKS, 4, 6)),
    ]


def on_device(tokens, cotangent, w_qkv, w_out, row_valid):
    flat = (LOCAL, D)
    d_tokens, grad_qkv, grad_out = window_call(tokens.reshape(flat), cotangent.reshape(flat), w_qkv, w_out, row_valid)
    return (d_tokens.reshape(tokens.shape), grad_qkv, grad_out)


def solution(mesh):
    placed = (P("lat", "lon", None), P("lat", "lon", None), P(), P(), P())
    return jax.shard_map(
        on_device,
        mesh=mesh,
        in_specs=placed,
        out_specs=(P("lat", "lon", None), P(("lon", "lat"), None), P(("lon", "lat"), None)),
        check_vma=False,
    )
```

```python
import math

import jax
import jax.numpy as jnp
from jax import lax
from jax.experimental import pallas as pl
from jax.experimental.pallas import tpu as pltpu
from jax.sharding import PartitionSpec as P

D = 1024
HEADS = 16
WIN = 6
HEAD_DIM = 64
HALF = 3
ROWS = 36
COLS = 24
LOCAL = ROWS * COLS
STRIPS = ROWS // WIN
STRIP = WIN * COLS
GROUP = 256
CHUNKS = D // GROUP
GROUP_HEADS = GROUP // HEAD_DIM
STACK = GROUP_HEADS * STRIP
EDGE = 112
EDGES = 128
BAND = 80
EARLY = STRIP * (STRIPS - 1)

SHARP = 10.0
LOG2E = math.log2(math.e)
EPSILON = 1e-06
BLOCKED = -1e30

F32 = jnp.float32
BF16 = jnp.bfloat16
MESH = pl.DeviceIdType.MESH
NN = (((1,), (0,)), ((), ()))
NT = (((1,), (1,)), ((), ()))
TN = (((0,), (0,)), ((), ()))


def dot(a, b, dims=NN):
    return lax.dot_general(a, b, dims, preferred_element_type=F32)


def head_sums(a, b, ones):
    both = dot(jnp.concatenate([a, b], axis=0), ones)
    return both[:STRIP], both[STRIP:]


def by_head(t):
    lane = lax.broadcasted_iota(jnp.int32, t.shape, 1) // HEAD_DIM
    zero = jnp.zeros_like(t)
    return jnp.concatenate([jnp.where(lane == h, t, zero) for h in range(GROUP_HEADS)], axis=0)


def pick_heads(t):
    lane = lax.broadcasted_iota(jnp.int32, (STRIP, GROUP), 1) // HEAD_DIM
    out = t[:STRIP]
    for h in range(1, GROUP_HEADS):
        out = jnp.where(lane == h, t[h * STRIP : (h + 1) * STRIP], out)
    return out


def shift_rows(ext, s):
    return ext[pl.ds(pl.multiple_of(s * STRIP + 64, 16), STRIP + 16), :].astype(F32)[8 : 8 + STRIP]


def edge_pick():
    at = lax.broadcasted_iota(jnp.int32, (EDGE, LOCAL), 0)
    token = lax.broadcasted_iota(jnp.int32, (EDGE, LOCAL), 1)
    return jnp.where(token == at // HALF * COLS + at % HALF, 1.0, 0.0).astype(BF16)


def corner_pick():
    at = lax.broadcasted_iota(jnp.int32, (16, STRIP), 0) - HALF
    token = lax.broadcasted_iota(jnp.int32, (16, STRIP), 1)
    source = (HALF + (at + HALF) // HALF - 1) * COLS + (at + HALF) % HALF
    return jnp.where((at >= 0) & (at < HALF * HALF) & (token == source), 1.0, 0.0).astype(BF16)


def edge_spread(s, near, far, width=EDGES):
    token = lax.broadcasted_iota(jnp.int32, (STRIP, width), 0)
    at = lax.broadcasted_iota(jnp.int32, (STRIP, width), 1)
    row, col = s * WIN + token // COLS, token % COLS
    source = jnp.where(near(row), far[0] + HALF * row + col, far[1] + HALF * row + col)
    return jnp.where((col < HALF) & (at == source), 1.0, 0.0).astype(BF16)


def normalize(strips, width, x_ext, cot_ext, edges, x, cot, normed, inv_rms):
    is_edge = lax.broadcasted_iota(jnp.int32, (STRIP, 1), 0) % COLS < HALF

    def norm_strip(s, _):
        rows = pl.ds(pl.multiple_of(s * STRIP, 16), STRIP)
        spread = edge_spread(s, lambda row: row < ROWS - HALF, (HALF * HALF, EDGE - HALF * (ROWS - HALF)), width)
        cot[rows, :] = jnp.where(is_edge, dot(spread, edges[1, 0:width, :]), shift_rows(cot_ext, s)).astype(BF16)
        xf = jnp.where(is_edge, dot(spread, edges[0, 0:width, :]), shift_rows(x_ext, s))
        x[rows, :] = xf.astype(BF16)
        inv = lax.rsqrt(jnp.mean(xf * xf, axis=-1, keepdims=True) + EPSILON)
        inv_rms[rows, :] = inv
        normed[rows, :] = (xf * inv).astype(BF16)
        return 0

    lax.fori_loop(*strips, norm_strip, 0)


def turn(blocks, cot, normed, normed_t, cot_t):
    for block in blocks:
        at = block * 128
        end = min(at + 128, LOCAL)
        normed_t[:, at:end] = normed[at:end, :].T
        cot_t[:, at:end] = cot[at:end, :].T


def project(p, start, size, cot, w_qkv, w_out, normed, qb, kb, vb, dab):
    rows = pl.ds(start, size)
    base = pl.multiple_of(p * GROUP, GROUP)
    n = normed[rows, :]
    qb[rows, :] = dot(n, w_qkv[:, pl.ds(base, GROUP)]).astype(BF16)
    kb[rows, :] = dot(n, w_qkv[:, pl.ds(base + D, GROUP)]).astype(BF16)
    vb[rows, :] = dot(n, w_qkv[:, pl.ds(base + 2 * D, GROUP)]).astype(BF16)
    dab[rows, :] = dot(cot[rows, :], w_out[pl.ds(base, GROUP), :], NT).astype(BF16)


def attend(p, strips, unroll, bias, qb, kb, vb, dab, ob, d_qkv):
    row_head = lax.broadcasted_iota(jnp.int32, (GROUP, GROUP), 0) // HEAD_DIM
    col_head = lax.broadcasted_iota(jnp.int32, (GROUP, GROUP), 1) // HEAD_DIM
    ones = jnp.where(row_head == col_head, 1.0, 0.0).astype(BF16)

    def strip(s, _):
        rows = pl.ds(pl.multiple_of(s * STRIP, 16), STRIP)
        base = pl.multiple_of(p * GROUP, GROUP)
        q, k = qb[rows, :], kb[rows, :]
        q_squares, k_squares = head_sums(q * q, k * k, ones)
        inv_q = lax.rsqrt(q_squares + EPSILON)
        inv_k = lax.rsqrt(k_squares + EPSILON)
        q_unit = q * inv_q
        k_unit = k * inv_k
        q_heads = by_head(q_unit.astype(BF16))
        k_round = k_unit.astype(BF16)
        v = vb[rows, :]
        da_heads = by_head(dab[rows, :])
        scores = dot(q_heads, k_round, NT).reshape(GROUP_HEADS, STRIP, STRIP)
        weights = jnp.exp2(scores * (SHARP * LOG2E) + bias[s][None])
        total = jnp.sum(weights, axis=-1, keepdims=True)
        probs = weights * (1.0 / total)
        prob_round = probs.astype(BF16).reshape(STACK, STRIP)
        d_probs = dot(da_heads, v, NT).reshape(GROUP_HEADS, STRIP, STRIP)
        mixed = jnp.sum(probs * d_probs, axis=-1, keepdims=True)
        ds_round = (probs * (d_probs - mixed)).astype(BF16).reshape(STACK, STRIP)
        ob[rows, :] = pick_heads(dot(prob_round, v)).astype(BF16)
        d_qkv[rows, pl.ds(base + 2 * D, GROUP)] = dot(prob_round, da_heads, TN).astype(BF16)
        dq_unit = SHARP * pick_heads(dot(ds_round, k_round))
        dk_unit = SHARP * dot(ds_round, q_heads, TN)
        q_along, k_along = head_sums((q_unit * dq_unit).astype(BF16), (k_unit * dk_unit).astype(BF16), ones)
        d_q = inv_q * (dq_unit - q_unit * q_along)
        d_k = inv_k * (dk_unit - k_unit * k_along)
        d_qkv[rows, pl.ds(base, GROUP)] = d_q.astype(BF16)
        d_qkv[rows, pl.ds(base + D, GROUP)] = d_k.astype(BF16)
        return 0

    lax.fori_loop(*strips, strip, 0, unroll=unroll)


def weight_terms(p, half, normed_t, cot_t, d_qkv, ob, terms):
    base = pl.multiple_of(p * GROUP, GROUP)
    for top in range(0, D, 512):
        n = normed_t[top : top + 512, :]
        if half == 0:
            upper = dot(n, d_qkv[:, pl.ds(base, GROUP)])
            lower = dot(n, d_qkv[:, pl.ds(base + D, GROUP)])
        else:
            upper = dot(n, d_qkv[:, pl.ds(base + 2 * D, GROUP)])
            lower = dot(cot_t[top : top + 512, :], ob[...])
        for at in range(0, 512, 8):
            unit = (top + at) // 8
            z, y_lo, core, x, y_hi = unit // 32, unit // 16 % 2, unit // 8 % 2, unit // 2 % 4, unit % 2
            y = y_hi * 2 + y_lo
            both = jnp.concatenate([upper[at : at + 8], lower[at : at + 8]], axis=0).astype(BF16)
            terms[(p, core, half) + ((x, y, z) if half == 0 else (z, y, x))] = both


def normed_grad(start, size, n, w_qkv, d_qkv, d_normed):
    cols = pl.ds(pl.multiple_of(n * 256, 256), 256)
    d_normed[start : start + size, cols] = dot(d_qkv[start : start + size, :], w_qkv[cols, :], NT)


def token_grad(strips, x, inv_rms, d_normed, d_ext):
    def strip(s, _):
        rows = pl.ds(pl.multiple_of(s * STRIP, 16), STRIP)
        xf = x[rows, :].astype(F32)
        dn = d_normed[rows, :]
        inv = inv_rms[rows, :]
        pull = jnp.mean(dn * xf, axis=-1, keepdims=True) * (inv * inv * inv)
        d_ext[pl.ds(pl.multiple_of(s * STRIP + BAND, 16), STRIP), :] = (inv * dn - xf * pull).astype(BF16)
        return 0

    lax.fori_loop(*strips, strip, 0)


def assemble(d_ext, d_edges, d_tokens):
    is_edge = lax.broadcasted_iota(jnp.int32, (STRIP, 1), 0) % COLS < HALF

    def strip(s, _):
        start = pl.multiple_of(s * STRIP, 16)
        own = d_ext[pl.ds(start, STRIP + 16), :].astype(F32)[8 : 8 + STRIP]
        spread = edge_spread(s, lambda row: row >= HALF, (-HALF * HALF, EDGE + HALF))
        d_tokens[pl.ds(start, STRIP), :] = jnp.where(is_edge, dot(spread, d_edges[...]), own).astype(BF16)
        return 0

    lax.fori_loop(0, STRIPS, strip, 0)


def pair_bias(row_valid, bias):
    query = lax.broadcasted_iota(jnp.int32, (STRIP, STRIP), 0)
    key = lax.broadcasted_iota(jnp.int32, (STRIP, STRIP), 1)
    window = lambda t: (t % COLS + COLS - HALF) % COLS // WIN
    half = lambda t: t // (HALF * COLS)
    same_window = window(query) == window(key)
    same_half = half(query) == half(key)
    lat, bands = lax.axis_index("lat"), lax.axis_size("lat")
    open_bias = jnp.where(same_window, -SHARP * LOG2E, BLOCKED)
    seam_bias = jnp.where(same_window & same_half, -SHARP * LOG2E, BLOCKED)
    others = jnp.where(query == key, 0.0, BLOCKED)
    key_row = lax.broadcasted_iota(jnp.int32, (1, STRIP), 1) // COLS
    for s in range(STRIPS):
        base = open_bias if s < STRIPS - 1 else jnp.where(lat == bands - 1, seam_bias, open_bias)
        invalid = jnp.zeros((1, STRIP), F32)
        for i in range(WIN):
            flag = 1.0 - row_valid[(lat * ROWS + s * WIN + i + HALF) % (ROWS * bands)].astype(F32)
            invalid = jnp.where(key_row == i, flag, invalid)
        bias[s] = base + others * invalid


def neighbour(lat_step, lon_step):
    lon, lons = lax.axis_index("lon"), lax.axis_size("lon")
    lat, lats = lax.axis_index("lat"), lax.axis_size("lat")
    return {"lon": (lon + lon_step + lons) % lons, "lat": (lat + lat_step + lats) % lats}


def remote(source, target, send, recv, slot, peer):
    return pltpu.make_async_remote_copy(
        src_ref=source, dst_ref=target, send_sem=send.at[slot], recv_sem=recv.at[slot], device_id=peer, device_id_type=MESH
    )


def window_kernel(
    tokens, cotangent, w_qkv_hbm, w_out_hbm, row_valid, d_ext_hbm, d_edges_hbm, sum_3,
    x_ext, cot_ext, w_qkv, w_out, edge_out, edges, d_ext, d_edge_out, d_corner_out, d_edges,
    bias, x, cot, normed, normed_t, cot_t, inv_rms, qb, kb, vb, dab, ob, d_qkv, d_normed, terms,
    got_0, got_1, sum_1, got_2, sum_2, got_3, send, recv, halo_send, halo_recv, load,
):
    greet()
    loads = [
        pltpu.make_async_copy(tokens, x_ext.at[0:LOCAL], load.at[0]),
        pltpu.make_async_copy(cotangent, cot_ext.at[0:LOCAL], load.at[1]),
        pltpu.make_async_copy(w_qkv_hbm, w_qkv, load.at[2]),
        pltpu.make_async_copy(w_out_hbm, w_out, load.at[3]),
    ]
    for copy in loads:
        copy.start()
    pair_bias(row_valid, bias)
    pick = edge_pick()
    for copy in loads[:2]:
        copy.wait()
    met()
    up, left, corner = neighbour(-1, 0), neighbour(0, -1), neighbour(-1, -1)
    halos = [
        remote(x_ext.at[0:BAND], x_ext.at[LOCAL : LOCAL + BAND], halo_send, halo_recv, 0, up),
        remote(cot_ext.at[0:BAND], cot_ext.at[LOCAL : LOCAL + BAND], halo_send, halo_recv, 1, up),
        remote(edge_out, edges.at[:, 0:EDGE], halo_send, halo_recv, 2, left),
        remote(edge_out.at[:, 0:16], edges.at[:, EDGE:EDGES], halo_send, halo_recv, 3, corner),
    ]
    edge_out[0] = dot(pick, x_ext[0:LOCAL, :]).astype(BF16)
    edge_out[1] = dot(pick, cot_ext[0:LOCAL, :]).astype(BF16)
    halos[2].start()
    halos[3].start()
    halos[0].start()
    halos[1].start()
    halos[2].wait_recv()
    early, late = (0, STRIPS - 1), (STRIPS - 1, STRIPS)
    normalize(early, EDGE, x_ext, cot_ext, edges, x, cot, normed, inv_rms)
    turn(range(5), cot, normed, normed_t, cot_t)
    for copy in loads[2:]:
        copy.wait()
    first = lambda p, half: rs_first(p, half, terms, got_0, got_1, send, recv)
    second = lambda p, half: rs_next(p, half, 0, terms, got_1, sum_1, got_2, send, recv)
    third = lambda p, half: rs_next(p, half, 1, sum_1, got_2, sum_2, got_3, send, recv)
    last = lambda p, half: rs_next(p, half, 2, sum_2, got_3, sum_3, None, send, recv)

    def finish_halo():
        for i in (0, 1, 3):
            halos[i].wait_recv()
        normalize(late, EDGES, x_ext, cot_ext, edges, x, cot, normed, inv_rms)
        turn(range(5, 7), cot, normed, normed_t, cot_t)

    def both_thirds(p):
        third(p, 1)
        third(p, 0)

    def parts(p):
        project(p, 0, EARLY, cot, w_qkv, w_out, normed, qb, kb, vb, dab)
        attend(p, early, 5, bias, qb, kb, vb, dab, ob, d_qkv)
        finish_halo()
        project(p, EARLY, STRIP, cot, w_qkv, w_out, normed, qb, kb, vb, dab)
        attend(p, late, 1, bias, qb, kb, vb, dab, ob, d_qkv)

    def whole(p):
        project(p, 0, LOCAL, cot, w_qkv, w_out, normed, qb, kb, vb, dab)
        first(p - 1, 0)
        attend(p, (0, STRIPS), 3, bias, qb, kb, vb, dab, ob, d_qkv)
        second(p - 1, 1)
        pl.when(p > 1)(lambda: both_thirds(p - 2))

    def chunk(p, _):
        pl.when(p == 0)(lambda: parts(p))
        pl.when(p > 0)(lambda: whole(p))
        weight_terms(p, 1, normed_t, cot_t, d_qkv, ob, terms)
        core_copy(p, 1, terms, got_0, send, recv).start()
        pl.when(p > 0)(lambda: second(p - 1, 0))
        weight_terms(p, 0, normed_t, cot_t, d_qkv, ob, terms)
        core_copy(p, 0, terms, got_0, send, recv).start()
        first(p, 1)
        return 0

    lax.fori_loop(0, CHUNKS, chunk, 0)
    end = CHUNKS - 1
    down, right, far_corner = neighbour(1, 0), neighbour(0, 1), neighbour(1, 1)
    returns = [
        remote(d_ext.at[LOCAL : LOCAL + BAND], d_ext.at[0:BAND], halo_send, halo_recv, 4, down),
        remote(d_edge_out, d_edges.at[0:EDGE], halo_send, halo_recv, 5, right),
        remote(d_corner_out, d_edges.at[EDGE:EDGES], halo_send, halo_recv, 6, far_corner),
    ]
    lax.fori_loop(0, D // 256, lambda n, _: (normed_grad(EARLY, STRIP, n, w_qkv, d_qkv, d_normed), 0)[1], 0)
    first(end, 0)
    both_thirds(end - 1)
    token_grad(late, x, inv_rms, d_normed, d_ext)
    d_corner_out[...] = dot(corner_pick(), d_ext[BAND + EARLY : BAND + LOCAL, :]).astype(BF16)
    returns[2].start()
    returns[0].start()
    lax.fori_loop(0, D // 256, lambda n, _: (normed_grad(0, EARLY, n, w_qkv, d_qkv, d_normed), 0)[1], 0)
    token_grad(early, x, inv_rms, d_normed, d_ext)
    second(end, 1)
    d_edge_out[...] = dot(edge_pick(), d_ext[BAND : BAND + LOCAL, :]).astype(BF16)
    returns[1].start()
    stores = [
        pltpu.make_async_copy(d_ext.at[BAND : BAND + LOCAL], d_ext_hbm.at[BAND : BAND + LOCAL], load.at[0]),
        pltpu.make_async_copy(d_ext.at[0:BAND], d_ext_hbm.at[0:BAND], load.at[1]),
        pltpu.make_async_copy(d_edges, d_edges_hbm, load.at[2]),
    ]
    stores[0].start()
    second(end, 0)

    def settle(p, _):
        last(p, 1)
        last(p, 0)
        rs_finish(p, terms, got_0, (terms, sum_1, sum_2), (got_1, got_2, got_3), send, recv)
        return 0

    lax.fori_loop(0, end, settle, 0)
    third(end, 1)
    for copy in returns:
        copy.wait_recv()
    stores[1].start()
    stores[2].start()
    third(end, 0)
    for copy in halos + returns:
        copy.wait_send()
    settle(end, 0)
    for copy in stores:
        copy.wait()


def place_kernel(d_ext, d_edges, sum_3, d_tokens, grad_qkv, grad_out):
    assemble(d_ext, d_edges, d_tokens)
    write_grads(sum_3, grad_qkv, grad_out)


def place_call(d_ext, d_edges, sum_3):
    vmem = pl.BlockSpec(memory_space=pltpu.VMEM)
    return pl.pallas_call(
        place_kernel,
        out_shape=(
            jax.ShapeDtypeStruct((LOCAL, D), BF16),
            jax.ShapeDtypeStruct((8, 3 * D), F32),
            jax.ShapeDtypeStruct((8, D), F32),
        ),
        in_specs=[vmem] * 3,
        out_specs=(vmem, vmem, vmem),
        compiler_params=pltpu.CompilerParams(vmem_limit_bytes=62 * 1024 * 1024),
        name="assembly",
    )(d_ext, d_edges, sum_3)


TERMS = (CHUNKS, 2, 2, 4, 4, 4, 16, GROUP)


def window_call(tokens, cotangent, w_qkv, w_out, row_valid):
    vmem = pl.BlockSpec(memory_space=pltpu.VMEM)
    anywhere = pl.BlockSpec(memory_space=pl.ANY)
    return pl.pallas_call(
        window_kernel,
        out_shape=(
            jax.ShapeDtypeStruct((BAND + LOCAL, D), BF16),
            jax.ShapeDtypeStruct((EDGES, D), BF16),
            jax.ShapeDtypeStruct((CHUNKS, 2, 16, GROUP), F32),
        ),
        in_specs=[anywhere] * 4 + [pl.BlockSpec(memory_space=pltpu.SMEM)],
        out_specs=(anywhere, anywhere, vmem),
        scratch_shapes=[
            pltpu.VMEM((LOCAL + BAND, D), BF16),
            pltpu.VMEM((LOCAL + BAND, D), BF16),
            pltpu.VMEM((D, 3 * D), BF16),
            pltpu.VMEM((D, D), BF16),
            pltpu.VMEM((2, EDGE, D), BF16),
            pltpu.VMEM((2, EDGES, D), BF16),
            pltpu.VMEM((BAND + LOCAL, D), BF16),
            pltpu.VMEM((EDGE, D), BF16),
            pltpu.VMEM((16, D), BF16),
            pltpu.VMEM((EDGES, D), BF16),
            pltpu.VMEM((STRIPS, STRIP, STRIP), F32),
            pltpu.VMEM((LOCAL, D), BF16),
            pltpu.VMEM((LOCAL, D), BF16),
            pltpu.VMEM((LOCAL, D), BF16),
            pltpu.VMEM((D, LOCAL), BF16),
            pltpu.VMEM((D, LOCAL), BF16),
            pltpu.VMEM((LOCAL, 1), F32),
            pltpu.VMEM((LOCAL, GROUP), BF16),
            pltpu.VMEM((LOCAL, GROUP), BF16),
            pltpu.VMEM((LOCAL, GROUP), BF16),
            pltpu.VMEM((LOCAL, GROUP), BF16),
            pltpu.VMEM((LOCAL, GROUP), BF16),
            pltpu.VMEM((LOCAL, 3 * D), BF16),
            pltpu.VMEM((LOCAL, D), F32),
            pltpu.VMEM(TERMS, BF16),
        ]
        + scatter_scratch()
        + [pltpu.SemaphoreType.DMA((7,)), pltpu.SemaphoreType.DMA((7,)), pltpu.SemaphoreType.DMA((4,))],
        compiler_params=pltpu.CompilerParams(
            collective_id=0, has_side_effects=True, vmem_limit_bytes=62 * 1024 * 1024
        ),
        name="windows",
    )(tokens, cotangent, w_qkv, w_out, row_valid)


def place():
    lon, lat = lax.axis_index("lon"), lax.axis_index("lat")
    z, y_lo, core = lon // 4, lon // 2 % 2, lon % 2
    x, y_hi = lat // 2, lat % 2
    return x, y_hi * 2 + y_lo, z, core


def device(x, y, z, core):
    return {"lon": z * 4 + y % 2 * 2 + core, "lat": x * 2 + y // 2}


def axis_peer(axis, step):
    x, y, z, core = place()
    if axis == "x":
        at = (x + step) % 4
        return at, device(at, y, z, core)
    if axis == "y":
        at = (y + step) % 4
        return at, device(x, at, z, core)
    at = (z + step) % 4
    return at, device(x, y, at, core)


ORDERS = (("x", "y", "z"), ("z", "y", "x"))


AROUND = ((-1, 0), (0, -1), (-1, -1), (1, 0), (0, 1), (1, 1))


def greet():
    x, y, z, core = place()
    peers = [device(x, y, z, 1 - core)]
    peers += [axis_peer(axis, step)[1] for axis in "xyz" for step in (1, 2, 3)]
    peers += [neighbour(*step) for step in AROUND]
    for peer in peers:
        pl.semaphore_signal(pltpu.get_barrier_semaphore(), inc=1, device_id=peer, device_id_type=MESH)


def met():
    pl.semaphore_wait(pltpu.get_barrier_semaphore(), 10 + len(AROUND))


def core_copy(p, half, terms, got_0, send, recv):
    x, y, z, core = place()
    return pltpu.make_async_remote_copy(
        src_ref=terms.at[p, 1 - core, half],
        dst_ref=got_0.at[p, half],
        send_sem=send.at[p, 0, half],
        recv_sem=recv.at[p, 0, half],
        device_id=device(x, y, z, 1 - core),
        device_id_type=MESH,
    )


def stage_copy(p, stage, half, step, source, target, send, recv):
    at, peer = axis_peer(ORDERS[half][stage], step)
    slot = 3 * half + step - 1
    return pltpu.make_async_remote_copy(
        src_ref=source.at[p, place()[3], half, at] if stage == 0 else source.at[p, half, at],
        dst_ref=target.at[p, half, step - 1],
        send_sem=send.at[p, 1 + stage, slot],
        recv_sem=recv.at[p, 1 + stage, slot],
        device_id=peer,
        device_id_type=MESH,
    )


STEPS = [(half, step) for half in (0, 1) for step in (1, 2, 3)]


def my_index(stage, half):
    x, y, z, _ = place()
    return {"x": x, "y": y, "z": z}[ORDERS[half][stage]]


def rs_first(p, half, terms, got_0, got_1, send, recv):
    core = place()[3]
    core_copy(p, half, terms, got_0, send, recv).wait_recv()
    for a in range(4):
        terms[p, core, half, a] = terms[p, core, half, a] + got_0[p, half, a]
    for step in (2, 1, 3):
        stage_copy(p, 0, half, step, terms, got_1, send, recv).start()


def rs_next(p, half, stage, source, got, total, after, send, recv):
    for step in (1, 2, 3):
        stage_copy(p, stage, half, step, source, got, send, recv).wait_recv()
    index = (half, my_index(stage, half))
    mine = source[(p, place()[3]) + index if stage == 0 else (p,) + index].astype(F32)
    for i in range(3):
        mine = mine + got[p, half, i].astype(F32)
    total[p, half] = mine.astype(total.dtype)
    if after is not None:
        for step in (2, 1, 3):
            stage_copy(p, stage + 1, half, step, total, after, send, recv).start()


def rs_finish(p, terms, got_0, sums, gots, send, recv):
    for half in (0, 1):
        core_copy(p, half, terms, got_0, send, recv).wait_send()
    for stage in range(3):
        for half, step in STEPS:
            stage_copy(p, stage, half, step, sums[stage], gots[stage], send, recv).wait_send()


def write_grads(sum_3, grad_qkv, grad_out):
    scale = 1.0 / math.sqrt(LOCAL * 128)
    for p in range(CHUNKS):
        at = p * GROUP
        grad_qkv[:, at : at + GROUP] = sum_3[p, 0, :8, :] * scale
        grad_qkv[:, D + at : D + at + GROUP] = sum_3[p, 0, 8:, :] * scale
        grad_qkv[:, 2 * D + at : 2 * D + at + GROUP] = sum_3[p, 1, :8, :] * scale
        grad_out[:, at : at + GROUP] = sum_3[p, 1, 8:, :] * scale


def scatter_scratch():
    unit = (16, GROUP)
    return [
        pltpu.VMEM((CHUNKS, 2, 4, 4, 4) + unit, BF16),
        pltpu.VMEM((CHUNKS, 2, 3, 4, 4) + unit, BF16),
        pltpu.VMEM((CHUNKS, 2, 4, 4) + unit, BF16),
        pltpu.VMEM((CHUNKS, 2, 3, 4) + unit, BF16),
        pltpu.VMEM((CHUNKS, 2, 4) + unit, BF16),
        pltpu.VMEM((CHUNKS, 2, 3) + unit, BF16),
        pltpu.SemaphoreType.DMA((CHUNKS, 4, 6)),
        pltpu.SemaphoreType.DMA((CHUNKS, 4, 6)),
    ]


def on_device(tokens, cotangent, w_qkv, w_out, row_valid):
    flat = (LOCAL, D)
    d_tokens, grad_qkv, grad_out = place_call(
        *window_call(tokens.reshape(flat), cotangent.reshape(flat), w_qkv, w_out, row_valid)
    )
    return (d_tokens.reshape(tokens.shape), grad_qkv, grad_out)


def solution(mesh):
    placed = (P("lat", "lon", None), P("lat", "lon", None), P(), P(), P())
    return jax.shard_map(
        on_device,
        mesh=mesh,
        in_specs=placed,
        out_specs=(P("lat", "lon", None), P(("lon", "lat"), None), P(("lon", "lat"), None)),
        check_vma=False,
    )
```

```python
import math

import jax
import jax.numpy as jnp
from jax import lax
from jax.experimental import pallas as pl
from jax.experimental.pallas import tpu as pltpu
from jax.sharding import PartitionSpec as P

D = 1024
HEADS = 16
WIN = 6
HEAD_DIM = 64
HALF = 3
ROWS = 36
COLS = 24
LOCAL = ROWS * COLS
STRIPS = ROWS // WIN
STRIP = WIN * COLS
GROUP = 256
CHUNKS = D // GROUP
GROUP_HEADS = GROUP // HEAD_DIM
STACK = GROUP_HEADS * STRIP
EDGE = 112
EDGES = 128
BAND = 80
PLACED = 2
EARLY = STRIP * (STRIPS - 1)

SHARP = 10.0
LOG2E = math.log2(math.e)
EPSILON = 1e-06
BLOCKED = -1e30

F32 = jnp.float32
BF16 = jnp.bfloat16
MESH = pl.DeviceIdType.MESH
NN = (((1,), (0,)), ((), ()))
NT = (((1,), (1,)), ((), ()))
TN = (((0,), (0,)), ((), ()))


def dot(a, b, dims=NN):
    return lax.dot_general(a, b, dims, preferred_element_type=F32)


def head_sums(a, b, ones):
    both = dot(jnp.concatenate([a, b], axis=0), ones)
    return both[:STRIP], both[STRIP:]


def by_head(t):
    lane = lax.broadcasted_iota(jnp.int32, t.shape, 1) // HEAD_DIM
    zero = jnp.zeros_like(t)
    return jnp.concatenate([jnp.where(lane == h, t, zero) for h in range(GROUP_HEADS)], axis=0)


def pick_heads(t):
    lane = lax.broadcasted_iota(jnp.int32, (STRIP, GROUP), 1) // HEAD_DIM
    out = t[:STRIP]
    for h in range(1, GROUP_HEADS):
        out = jnp.where(lane == h, t[h * STRIP : (h + 1) * STRIP], out)
    return out


def shift_rows(ext, s):
    return ext[pl.ds(pl.multiple_of(s * STRIP + 64, 16), STRIP + 16), :].astype(F32)[8 : 8 + STRIP]


def edge_pick():
    at = lax.broadcasted_iota(jnp.int32, (EDGE, LOCAL), 0)
    token = lax.broadcasted_iota(jnp.int32, (EDGE, LOCAL), 1)
    return jnp.where(token == at // HALF * COLS + at % HALF, 1.0, 0.0).astype(BF16)


def corner_pick():
    at = lax.broadcasted_iota(jnp.int32, (16, STRIP), 0) - HALF
    token = lax.broadcasted_iota(jnp.int32, (16, STRIP), 1)
    source = (HALF + (at + HALF) // HALF - 1) * COLS + (at + HALF) % HALF
    return jnp.where((at >= 0) & (at < HALF * HALF) & (token == source), 1.0, 0.0).astype(BF16)


def edge_spread(s, near, far, width=EDGES):
    token = lax.broadcasted_iota(jnp.int32, (STRIP, width), 0)
    at = lax.broadcasted_iota(jnp.int32, (STRIP, width), 1)
    row, col = s * WIN + token // COLS, token % COLS
    source = jnp.where(near(row), far[0] + HALF * row + col, far[1] + HALF * row + col)
    return jnp.where((col < HALF) & (at == source), 1.0, 0.0).astype(BF16)


def normalize(strips, width, x_ext, cot_ext, edges, x, cot, normed, inv_rms):
    is_edge = lax.broadcasted_iota(jnp.int32, (STRIP, 1), 0) % COLS < HALF

    def norm_strip(s, _):
        rows = pl.ds(pl.multiple_of(s * STRIP, 16), STRIP)
        spread = edge_spread(s, lambda row: row < ROWS - HALF, (HALF * HALF, EDGE - HALF * (ROWS - HALF)), width)
        cot[rows, :] = jnp.where(is_edge, dot(spread, edges[1, 0:width, :]), shift_rows(cot_ext, s)).astype(BF16)
        xf = jnp.where(is_edge, dot(spread, edges[0, 0:width, :]), shift_rows(x_ext, s))
        x[rows, :] = xf.astype(BF16)
        inv = lax.rsqrt(jnp.mean(xf * xf, axis=-1, keepdims=True) + EPSILON)
        inv_rms[rows, :] = inv
        normed[rows, :] = (xf * inv).astype(BF16)
        return 0

    lax.fori_loop(*strips, norm_strip, 0)


def turn(blocks, cot, normed, normed_t, cot_t):
    for block in blocks:
        at = block * 128
        end = min(at + 128, LOCAL)
        normed_t[:, at:end] = normed[at:end, :].T
        cot_t[:, at:end] = cot[at:end, :].T


def project(p, start, size, cot, w_qkv, w_out, normed, qb, kb, vb, dab):
    rows = pl.ds(start, size)
    base = pl.multiple_of(p * GROUP, GROUP)
    n = normed[rows, :]
    qb[rows, :] = dot(n, w_qkv[:, pl.ds(base, GROUP)]).astype(BF16)
    kb[rows, :] = dot(n, w_qkv[:, pl.ds(base + D, GROUP)]).astype(BF16)
    vb[rows, :] = dot(n, w_qkv[:, pl.ds(base + 2 * D, GROUP)]).astype(BF16)
    dab[rows, :] = dot(cot[rows, :], w_out[pl.ds(base, GROUP), :], NT).astype(BF16)


def attend(p, strips, unroll, bias, qb, kb, vb, dab, ob, d_qkv):
    row_head = lax.broadcasted_iota(jnp.int32, (GROUP, GROUP), 0) // HEAD_DIM
    col_head = lax.broadcasted_iota(jnp.int32, (GROUP, GROUP), 1) // HEAD_DIM
    ones = jnp.where(row_head == col_head, 1.0, 0.0).astype(BF16)

    def strip(s, _):
        rows = pl.ds(pl.multiple_of(s * STRIP, 16), STRIP)
        base = pl.multiple_of(p * GROUP, GROUP)
        q, k = qb[rows, :], kb[rows, :]
        q_squares, k_squares = head_sums(q * q, k * k, ones)
        inv_q = lax.rsqrt(q_squares + EPSILON)
        inv_k = lax.rsqrt(k_squares + EPSILON)
        q_unit = q * inv_q
        k_unit = k * inv_k
        q_heads = by_head(q_unit.astype(BF16))
        k_round = k_unit.astype(BF16)
        v = vb[rows, :]
        da_heads = by_head(dab[rows, :])
        scores = dot(q_heads, k_round, NT).reshape(GROUP_HEADS, STRIP, STRIP)
        weights = jnp.exp2(scores * (SHARP * LOG2E) + bias[s][None])
        total = jnp.sum(weights, axis=-1, keepdims=True)
        probs = weights * (1.0 / total)
        prob_round = probs.astype(BF16).reshape(STACK, STRIP)
        d_probs = dot(da_heads, v, NT).reshape(GROUP_HEADS, STRIP, STRIP)
        mixed = jnp.sum(probs * d_probs, axis=-1, keepdims=True)
        ds_round = (probs * (d_probs - mixed)).astype(BF16).reshape(STACK, STRIP)
        ob[rows, :] = pick_heads(dot(prob_round, v)).astype(BF16)
        d_qkv[rows, pl.ds(base + 2 * D, GROUP)] = dot(prob_round, da_heads, TN).astype(BF16)
        dq_unit = SHARP * pick_heads(dot(ds_round, k_round))
        dk_unit = SHARP * dot(ds_round, q_heads, TN)
        q_along, k_along = head_sums((q_unit * dq_unit).astype(BF16), (k_unit * dk_unit).astype(BF16), ones)
        d_q = inv_q * (dq_unit - q_unit * q_along)
        d_k = inv_k * (dk_unit - k_unit * k_along)
        d_qkv[rows, pl.ds(base, GROUP)] = d_q.astype(BF16)
        d_qkv[rows, pl.ds(base + D, GROUP)] = d_k.astype(BF16)
        return 0

    lax.fori_loop(*strips, strip, 0, unroll=unroll)


def weight_terms(p, half, normed_t, cot_t, d_qkv, ob, terms):
    base = pl.multiple_of(p * GROUP, GROUP)
    for top in range(0, D, 512):
        n = normed_t[top : top + 512, :]
        if half == 0:
            upper = dot(n, d_qkv[:, pl.ds(base, GROUP)])
            lower = dot(n, d_qkv[:, pl.ds(base + D, GROUP)])
        else:
            upper = dot(n, d_qkv[:, pl.ds(base + 2 * D, GROUP)])
            lower = dot(cot_t[top : top + 512, :], ob[...])
        for at in range(0, 512, 8):
            unit = (top + at) // 8
            z, y_lo, core, x, y_hi = unit // 32, unit // 16 % 2, unit // 8 % 2, unit // 2 % 4, unit % 2
            y = y_hi * 2 + y_lo
            both = jnp.concatenate([upper[at : at + 8], lower[at : at + 8]], axis=0).astype(BF16)
            terms[(p, core, half) + ((x, y, z) if half == 0 else (z, y, x))] = both


def normed_grad(start, size, n, w_qkv, d_qkv, d_normed):
    cols = pl.ds(pl.multiple_of(n * 256, 256), 256)
    d_normed[start : start + size, cols] = dot(d_qkv[start : start + size, :], w_qkv[cols, :], NT)


def token_grad(strips, x, inv_rms, d_normed, d_ext):
    def strip(s, _):
        rows = pl.ds(pl.multiple_of(s * STRIP, 16), STRIP)
        xf = x[rows, :].astype(F32)
        dn = d_normed[rows, :]
        inv = inv_rms[rows, :]
        pull = jnp.mean(dn * xf, axis=-1, keepdims=True) * (inv * inv * inv)
        d_ext[pl.ds(pl.multiple_of(s * STRIP + BAND, 16), STRIP), :] = (inv * dn - xf * pull).astype(BF16)
        return 0

    lax.fori_loop(*strips, strip, 0)


def assemble(d_ext, d_next, d_edges, d_tokens):
    is_edge = lax.broadcasted_iota(jnp.int32, (STRIP, 1), 0) % COLS < HALF
    held = jnp.concatenate([d_ext[...].astype(F32), d_next[...].astype(F32)], axis=0)
    for i in range(PLACED):
        s = pl.program_id(0) * PLACED + i
        spread = edge_spread(s, lambda row: row >= HALF, (-HALF * HALF, EDGE + HALF))
        own = held[i * STRIP + 8 : (i + 1) * STRIP + 8]
        d_tokens[i * STRIP : (i + 1) * STRIP, :] = jnp.where(is_edge, dot(spread, d_edges[...]), own).astype(BF16)


def pair_bias(row_valid, bias):
    query = lax.broadcasted_iota(jnp.int32, (STRIP, STRIP), 0)
    key = lax.broadcasted_iota(jnp.int32, (STRIP, STRIP), 1)
    window = lambda t: (t % COLS + COLS - HALF) % COLS // WIN
    half = lambda t: t // (HALF * COLS)
    same_window = window(query) == window(key)
    same_half = half(query) == half(key)
    lat, bands = lax.axis_index("lat"), lax.axis_size("lat")
    open_bias = jnp.where(same_window, -SHARP * LOG2E, BLOCKED)
    seam_bias = jnp.where(same_window & same_half, -SHARP * LOG2E, BLOCKED)
    others = jnp.where(query == key, 0.0, BLOCKED)
    key_row = lax.broadcasted_iota(jnp.int32, (1, STRIP), 1) // COLS
    for s in range(STRIPS):
        base = open_bias if s < STRIPS - 1 else jnp.where(lat == bands - 1, seam_bias, open_bias)
        invalid = jnp.zeros((1, STRIP), F32)
        for i in range(WIN):
            flag = 1.0 - row_valid[(lat * ROWS + s * WIN + i + HALF) % (ROWS * bands)].astype(F32)
            invalid = jnp.where(key_row == i, flag, invalid)
        bias[s] = base + others * invalid


def neighbour(lat_step, lon_step):
    lon, lons = lax.axis_index("lon"), lax.axis_size("lon")
    lat, lats = lax.axis_index("lat"), lax.axis_size("lat")
    return {"lon": (lon + lon_step + lons) % lons, "lat": (lat + lat_step + lats) % lats}


def remote(source, target, send, recv, slot, peer):
    return pltpu.make_async_remote_copy(
        src_ref=source, dst_ref=target, send_sem=send.at[slot], recv_sem=recv.at[slot], device_id=peer, device_id_type=MESH
    )


def window_kernel(
    tokens, cotangent, w_qkv_hbm, w_out_hbm, row_valid, d_ext_hbm, d_edges_hbm, sum_3,
    x_ext, cot_ext, w_qkv, w_out, edge_out, edges, d_ext, d_edge_out, d_corner_out, d_edges,
    bias, x, cot, normed, normed_t, cot_t, inv_rms, qb, kb, vb, dab, ob, d_qkv, d_normed, terms,
    got_0, got_1, sum_1, got_2, sum_2, got_3, send, recv, halo_send, halo_recv, load,
):
    greet()
    loads = [
        pltpu.make_async_copy(tokens, x_ext.at[0:LOCAL], load.at[0]),
        pltpu.make_async_copy(cotangent, cot_ext.at[0:LOCAL], load.at[1]),
        pltpu.make_async_copy(w_qkv_hbm, w_qkv, load.at[2]),
        pltpu.make_async_copy(w_out_hbm, w_out, load.at[3]),
    ]
    for copy in loads:
        copy.start()
    pair_bias(row_valid, bias)
    pick = edge_pick()
    for copy in loads[:2]:
        copy.wait()
    edge_out[0] = dot(pick, x_ext[0:LOCAL, :]).astype(BF16)
    edge_out[1] = dot(pick, cot_ext[0:LOCAL, :]).astype(BF16)
    met()
    up, left, corner = neighbour(-1, 0), neighbour(0, -1), neighbour(-1, -1)
    halos = [
        remote(x_ext.at[0:BAND], x_ext.at[LOCAL : LOCAL + BAND], halo_send, halo_recv, 0, up),
        remote(cot_ext.at[0:BAND], cot_ext.at[LOCAL : LOCAL + BAND], halo_send, halo_recv, 1, up),
        remote(edge_out, edges.at[:, 0:EDGE], halo_send, halo_recv, 2, left),
        remote(edge_out.at[:, 0:16], edges.at[:, EDGE:EDGES], halo_send, halo_recv, 3, corner),
    ]
    halos[2].start()
    halos[3].start()
    halos[0].start()
    halos[1].start()
    halos[2].wait_recv()
    early, late = (0, STRIPS - 1), (STRIPS - 1, STRIPS)
    normalize(early, EDGE, x_ext, cot_ext, edges, x, cot, normed, inv_rms)
    turn(range(5), cot, normed, normed_t, cot_t)
    for copy in loads[2:]:
        copy.wait()
    first = lambda p, half: rs_first(p, half, terms, got_0, got_1, send, recv)
    second = lambda p, half: rs_next(p, half, 0, terms, got_1, sum_1, got_2, send, recv)
    third = lambda p, half: rs_next(p, half, 1, sum_1, got_2, sum_2, got_3, send, recv)
    last = lambda p, half: rs_next(p, half, 2, sum_2, got_3, sum_3, None, send, recv)

    def finish_halo():
        for i in (0, 1, 3):
            halos[i].wait_recv()
        normalize(late, EDGES, x_ext, cot_ext, edges, x, cot, normed, inv_rms)
        turn(range(5, 7), cot, normed, normed_t, cot_t)

    def both_thirds(p):
        third(p, 1)
        third(p, 0)

    def parts(p):
        project(p, 0, EARLY, cot, w_qkv, w_out, normed, qb, kb, vb, dab)
        attend(p, early, 5, bias, qb, kb, vb, dab, ob, d_qkv)
        finish_halo()
        project(p, EARLY, STRIP, cot, w_qkv, w_out, normed, qb, kb, vb, dab)
        attend(p, late, 1, bias, qb, kb, vb, dab, ob, d_qkv)

    def whole(p):
        project(p, 0, LOCAL, cot, w_qkv, w_out, normed, qb, kb, vb, dab)
        first(p - 1, 0)
        attend(p, (0, STRIPS), 6, bias, qb, kb, vb, dab, ob, d_qkv)
        second(p - 1, 1)
        pl.when(p > 1)(lambda: both_thirds(p - 2))

    def chunk(p, _):
        pl.when(p == 0)(lambda: parts(p))
        pl.when(p > 0)(lambda: whole(p))
        weight_terms(p, 1, normed_t, cot_t, d_qkv, ob, terms)
        core_copy(p, 1, terms, got_0, send, recv).start()
        weight_terms(p, 0, normed_t, cot_t, d_qkv, ob, terms)
        core_copy(p, 0, terms, got_0, send, recv).start()
        pl.when(p > 0)(lambda: second(p - 1, 0))
        first(p, 1)
        return 0

    lax.fori_loop(0, CHUNKS, chunk, 0)
    end = CHUNKS - 1
    down, right, far_corner = neighbour(1, 0), neighbour(0, 1), neighbour(1, 1)
    returns = [
        remote(d_ext.at[LOCAL : LOCAL + BAND], d_ext.at[0:BAND], halo_send, halo_recv, 4, down),
        remote(d_edge_out, d_edges.at[0:EDGE], halo_send, halo_recv, 5, right),
        remote(d_corner_out, d_edges.at[EDGE:EDGES], halo_send, halo_recv, 6, far_corner),
    ]
    lax.fori_loop(0, D // 256, lambda n, _: (normed_grad(EARLY, STRIP, n, w_qkv, d_qkv, d_normed), 0)[1], 0)
    first(end, 0)
    both_thirds(end - 1)
    token_grad(late, x, inv_rms, d_normed, d_ext)
    d_corner_out[...] = dot(corner_pick(), d_ext[BAND + EARLY : BAND + LOCAL, :]).astype(BF16)
    returns[2].start()
    returns[0].start()
    lax.fori_loop(0, D // 256, lambda n, _: (normed_grad(0, EARLY, n, w_qkv, d_qkv, d_normed), 0)[1], 0)
    token_grad(early, x, inv_rms, d_normed, d_ext)
    second(end, 1)
    d_edge_out[...] = dot(edge_pick(), d_ext[BAND : BAND + LOCAL, :]).astype(BF16)
    returns[1].start()
    stores = [
        pltpu.make_async_copy(d_ext.at[BAND : BAND + LOCAL], d_ext_hbm.at[BAND : BAND + LOCAL], load.at[0]),
        pltpu.make_async_copy(d_ext.at[0:BAND], d_ext_hbm.at[0:BAND], load.at[1]),
        pltpu.make_async_copy(d_edges, d_edges_hbm, load.at[2]),
    ]
    stores[0].start()
    second(end, 0)

    def settle(p, _):
        last(p, 1)
        last(p, 0)
        rs_finish(p, terms, got_0, (terms, sum_1, sum_2), (got_1, got_2, got_3), send, recv)
        return 0

    lax.fori_loop(0, end, settle, 0)
    third(end, 1)
    for copy in returns:
        copy.wait_recv()
    stores[1].start()
    stores[2].start()
    third(end, 0)
    for copy in halos + returns:
        copy.wait_send()
    settle(end, 0)
    for copy in stores:
        copy.wait()


def place_kernel(d_ext, d_next, d_edges, sum_3, d_tokens, grad_qkv, grad_out):
    assemble(d_ext, d_next, d_edges, d_tokens)
    pl.when(pl.program_id(0) == 0)(lambda: write_grads(sum_3, grad_qkv, grad_out))


def place_call(d_ext, d_edges, sum_3):
    rows = PLACED * STRIP
    return pl.pallas_call(
        place_kernel,
        grid=(STRIPS // PLACED,),
        out_shape=(
            jax.ShapeDtypeStruct((LOCAL, D), BF16),
            jax.ShapeDtypeStruct((8, 3 * D), F32),
            jax.ShapeDtypeStruct((8, D), F32),
        ),
        in_specs=[
            pl.BlockSpec((rows, D), lambda k: (k, 0)),
            pl.BlockSpec((16, D), lambda k: ((k + 1) * (rows // 16), 0)),
            pl.BlockSpec((EDGES, D), lambda k: (0, 0)),
            pl.BlockSpec((CHUNKS, 2, 16, GROUP), lambda k: (0, 0, 0, 0)),
        ],
        out_specs=(
            pl.BlockSpec((rows, D), lambda k: (k, 0)),
            pl.BlockSpec((8, 3 * D), lambda k: (0, 0)),
            pl.BlockSpec((8, D), lambda k: (0, 0)),
        ),
        compiler_params=pltpu.CompilerParams(vmem_limit_bytes=62 * 1024 * 1024),
        name="assembly",
    )(d_ext, d_ext, d_edges, sum_3)


TERMS = (CHUNKS, 2, 2, 4, 4, 4, 16, GROUP)


def window_call(tokens, cotangent, w_qkv, w_out, row_valid):
    vmem = pl.BlockSpec(memory_space=pltpu.VMEM)
    anywhere = pl.BlockSpec(memory_space=pl.ANY)
    return pl.pallas_call(
        window_kernel,
        out_shape=(
            jax.ShapeDtypeStruct((BAND + LOCAL, D), BF16),
            jax.ShapeDtypeStruct((EDGES, D), BF16),
            jax.ShapeDtypeStruct((CHUNKS, 2, 16, GROUP), F32),
        ),
        in_specs=[anywhere] * 4 + [pl.BlockSpec(memory_space=pltpu.SMEM)],
        out_specs=(anywhere, anywhere, vmem),
        scratch_shapes=[
            pltpu.VMEM((LOCAL + BAND, D), BF16),
            pltpu.VMEM((LOCAL + BAND, D), BF16),
            pltpu.VMEM((D, 3 * D), BF16),
            pltpu.VMEM((D, D), BF16),
            pltpu.VMEM((2, EDGE, D), BF16),
            pltpu.VMEM((2, EDGES, D), BF16),
            pltpu.VMEM((BAND + LOCAL, D), BF16),
            pltpu.VMEM((EDGE, D), BF16),
            pltpu.VMEM((16, D), BF16),
            pltpu.VMEM((EDGES, D), BF16),
            pltpu.VMEM((STRIPS, STRIP, STRIP), F32),
            pltpu.VMEM((LOCAL, D), BF16),
            pltpu.VMEM((LOCAL, D), BF16),
            pltpu.VMEM((LOCAL, D), BF16),
            pltpu.VMEM((D, LOCAL), BF16),
            pltpu.VMEM((D, LOCAL), BF16),
            pltpu.VMEM((LOCAL, 1), F32),
            pltpu.VMEM((LOCAL, GROUP), BF16),
            pltpu.VMEM((LOCAL, GROUP), BF16),
            pltpu.VMEM((LOCAL, GROUP), BF16),
            pltpu.VMEM((LOCAL, GROUP), BF16),
            pltpu.VMEM((LOCAL, GROUP), BF16),
            pltpu.VMEM((LOCAL, 3 * D), BF16),
            pltpu.VMEM((LOCAL, D), F32),
            pltpu.VMEM(TERMS, BF16),
        ]
        + scatter_scratch()
        + [pltpu.SemaphoreType.DMA((7,)), pltpu.SemaphoreType.DMA((7,)), pltpu.SemaphoreType.DMA((4,))],
        compiler_params=pltpu.CompilerParams(
            collective_id=0, has_side_effects=True, vmem_limit_bytes=62 * 1024 * 1024
        ),
        name="windows",
    )(tokens, cotangent, w_qkv, w_out, row_valid)


def place():
    lon, lat = lax.axis_index("lon"), lax.axis_index("lat")
    z, y_lo, core = lon // 4, lon // 2 % 2, lon % 2
    x, y_hi = lat // 2, lat % 2
    return x, y_hi * 2 + y_lo, z, core


def device(x, y, z, core):
    return {"lon": z * 4 + y % 2 * 2 + core, "lat": x * 2 + y // 2}


def axis_peer(axis, step):
    x, y, z, core = place()
    if axis == "x":
        at = (x + step) % 4
        return at, device(at, y, z, core)
    if axis == "y":
        at = (y + step) % 4
        return at, device(x, at, z, core)
    at = (z + step) % 4
    return at, device(x, y, at, core)


ORDERS = (("x", "y", "z"), ("z", "y", "x"))


AROUND = ((-1, 0), (0, -1), (-1, -1), (1, 0), (0, 1), (1, 1))


def greet():
    x, y, z, core = place()
    peers = [device(x, y, z, 1 - core)]
    peers += [axis_peer(axis, step)[1] for axis in "xyz" for step in (1, 2, 3)]
    peers += [neighbour(*step) for step in AROUND]
    for peer in peers:
        pl.semaphore_signal(pltpu.get_barrier_semaphore(), inc=1, device_id=peer, device_id_type=MESH)


def met():
    pl.semaphore_wait(pltpu.get_barrier_semaphore(), 10 + len(AROUND))


def core_copy(p, half, terms, got_0, send, recv):
    x, y, z, core = place()
    return pltpu.make_async_remote_copy(
        src_ref=terms.at[p, 1 - core, half],
        dst_ref=got_0.at[p, half],
        send_sem=send.at[p, 0, half],
        recv_sem=recv.at[p, 0, half],
        device_id=device(x, y, z, 1 - core),
        device_id_type=MESH,
    )


def stage_copy(p, stage, half, step, source, target, send, recv):
    at, peer = axis_peer(ORDERS[half][stage], step)
    slot = 3 * half + step - 1
    return pltpu.make_async_remote_copy(
        src_ref=source.at[p, place()[3], half, at] if stage == 0 else source.at[p, half, at],
        dst_ref=target.at[p, half, step - 1],
        send_sem=send.at[p, 1 + stage, slot],
        recv_sem=recv.at[p, 1 + stage, slot],
        device_id=peer,
        device_id_type=MESH,
    )


STEPS = [(half, step) for half in (0, 1) for step in (1, 2, 3)]


def my_index(stage, half):
    x, y, z, _ = place()
    return {"x": x, "y": y, "z": z}[ORDERS[half][stage]]


def rs_first(p, half, terms, got_0, got_1, send, recv):
    core = place()[3]
    core_copy(p, half, terms, got_0, send, recv).wait_recv()
    for a in range(4):
        terms[p, core, half, a] = terms[p, core, half, a] + got_0[p, half, a]
    for step in (2, 1, 3):
        stage_copy(p, 0, half, step, terms, got_1, send, recv).start()


def rs_next(p, half, stage, source, got, total, after, send, recv):
    for step in (1, 2, 3):
        stage_copy(p, stage, half, step, source, got, send, recv).wait_recv()
    index = (half, my_index(stage, half))
    mine = source[(p, place()[3]) + index if stage == 0 else (p,) + index].astype(F32)
    for i in range(3):
        mine = mine + got[p, half, i].astype(F32)
    total[p, half] = mine.astype(total.dtype)
    if after is not None:
        for step in (2, 1, 3):
            stage_copy(p, stage + 1, half, step, total, after, send, recv).start()


def rs_finish(p, terms, got_0, sums, gots, send, recv):
    for half in (0, 1):
        core_copy(p, half, terms, got_0, send, recv).wait_send()
    for stage in range(3):
        for half, step in STEPS:
            stage_copy(p, stage, half, step, sums[stage], gots[stage], send, recv).wait_send()


def write_grads(sum_3, grad_qkv, grad_out):
    scale = 1.0 / math.sqrt(LOCAL * 128)
    for p in range(CHUNKS):
        at = p * GROUP
        grad_qkv[:, at : at + GROUP] = sum_3[p, 0, :8, :] * scale
        grad_qkv[:, D + at : D + at + GROUP] = sum_3[p, 0, 8:, :] * scale
        grad_qkv[:, 2 * D + at : 2 * D + at + GROUP] = sum_3[p, 1, :8, :] * scale
        grad_out[:, at : at + GROUP] = sum_3[p, 1, 8:, :] * scale


def scatter_scratch():
    unit = (16, GROUP)
    return [
        pltpu.VMEM((CHUNKS, 2, 4, 4, 4) + unit, BF16),
        pltpu.VMEM((CHUNKS, 2, 3, 4, 4) + unit, BF16),
        pltpu.VMEM((CHUNKS, 2, 4, 4) + unit, BF16),
        pltpu.VMEM((CHUNKS, 2, 3, 4) + unit, BF16),
        pltpu.VMEM((CHUNKS, 2, 4) + unit, BF16),
        pltpu.VMEM((CHUNKS, 2, 3) + unit, BF16),
        pltpu.SemaphoreType.DMA((CHUNKS, 4, 6)),
        pltpu.SemaphoreType.DMA((CHUNKS, 4, 6)),
    ]


def on_device(tokens, cotangent, w_qkv, w_out, row_valid):
    flat = (LOCAL, D)
    d_tokens, grad_qkv, grad_out = place_call(
        *window_call(tokens.reshape(flat), cotangent.reshape(flat), w_qkv, w_out, row_valid)
    )
    return (d_tokens.reshape(tokens.shape), grad_qkv, grad_out)


def solution(mesh):
    placed = (P("lat", "lon", None), P("lat", "lon", None), P(), P(), P())
    return jax.shard_map(
        on_device,
        mesh=mesh,
        in_specs=placed,
        out_specs=(P("lat", "lon", None), P(("lon", "lat"), None), P(("lon", "lat"), None)),
        check_vma=False,
    )
```

```python
import math

import jax
import jax.numpy as jnp
from jax import lax
from jax.experimental import pallas as pl
from jax.experimental.pallas import tpu as pltpu
from jax.sharding import PartitionSpec as P

D = 1024
HEADS = 16
WIN = 6
HEAD_DIM = 64
HALF = 3
ROWS = 36
COLS = 24
LOCAL = ROWS * COLS
STRIPS = ROWS // WIN
STRIP = WIN * COLS
GROUP = 256
CHUNKS = D // GROUP
GROUP_HEADS = GROUP // HEAD_DIM
STACK = GROUP_HEADS * STRIP
EDGE = 112
EDGES = 128
BAND = 80
PLACED = 2
EARLY = STRIP * (STRIPS - 1)

SHARP = 10.0
LOG2E = math.log2(math.e)
EPSILON = 1e-06
BLOCKED = -1e30

F32 = jnp.float32
BF16 = jnp.bfloat16
MESH = pl.DeviceIdType.MESH
NN = (((1,), (0,)), ((), ()))
NT = (((1,), (1,)), ((), ()))
TN = (((0,), (0,)), ((), ()))


def dot(a, b, dims=NN):
    return lax.dot_general(a, b, dims, preferred_element_type=F32)


def head_sums(a, b, ones):
    both = dot(jnp.concatenate([a, b], axis=0), ones)
    return both[:STRIP], both[STRIP:]


def by_head(t):
    lane = lax.broadcasted_iota(jnp.int32, t.shape, 1) // HEAD_DIM
    zero = jnp.zeros_like(t)
    return jnp.concatenate([jnp.where(lane == h, t, zero) for h in range(GROUP_HEADS)], axis=0)


def pick_heads(t):
    lane = lax.broadcasted_iota(jnp.int32, (STRIP, GROUP), 1) // HEAD_DIM
    out = t[:STRIP]
    for h in range(1, GROUP_HEADS):
        out = jnp.where(lane == h, t[h * STRIP : (h + 1) * STRIP], out)
    return out


def shift_rows(ext, s):
    return ext[pl.ds(pl.multiple_of(s * STRIP + 64, 16), STRIP + 16), :].astype(F32)[8 : 8 + STRIP]


def edge_pick():
    at = lax.broadcasted_iota(jnp.int32, (EDGE, LOCAL), 0)
    token = lax.broadcasted_iota(jnp.int32, (EDGE, LOCAL), 1)
    return jnp.where(token == at // HALF * COLS + at % HALF, 1.0, 0.0).astype(BF16)


def corner_pick():
    at = lax.broadcasted_iota(jnp.int32, (16, STRIP), 0) - HALF
    token = lax.broadcasted_iota(jnp.int32, (16, STRIP), 1)
    source = (HALF + (at + HALF) // HALF - 1) * COLS + (at + HALF) % HALF
    return jnp.where((at >= 0) & (at < HALF * HALF) & (token == source), 1.0, 0.0).astype(BF16)


def edge_spread(s, near, far, width=EDGES):
    token = lax.broadcasted_iota(jnp.int32, (STRIP, width), 0)
    at = lax.broadcasted_iota(jnp.int32, (STRIP, width), 1)
    row, col = s * WIN + token // COLS, token % COLS
    source = jnp.where(near(row), far[0] + HALF * row + col, far[1] + HALF * row + col)
    return jnp.where((col < HALF) & (at == source), 1.0, 0.0).astype(BF16)


def normalize(strips, width, x_ext, cot_ext, edges, x, cot, normed, inv_rms):
    is_edge = lax.broadcasted_iota(jnp.int32, (STRIP, 1), 0) % COLS < HALF

    def norm_strip(s, _):
        rows = pl.ds(pl.multiple_of(s * STRIP, 16), STRIP)
        spread = edge_spread(s, lambda row: row < ROWS - HALF, (HALF * HALF, EDGE - HALF * (ROWS - HALF)), width)
        cot[rows, :] = jnp.where(is_edge, dot(spread, edges[1, 0:width, :]), shift_rows(cot_ext, s)).astype(BF16)
        xf = jnp.where(is_edge, dot(spread, edges[0, 0:width, :]), shift_rows(x_ext, s))
        x[rows, :] = xf.astype(BF16)
        inv = lax.rsqrt(jnp.mean(xf * xf, axis=-1, keepdims=True) + EPSILON)
        inv_rms[rows, :] = inv
        normed[rows, :] = (xf * inv).astype(BF16)
        return 0

    lax.fori_loop(*strips, norm_strip, 0)


def turn(blocks, cot, normed, normed_t, cot_t):
    for block in blocks:
        at = block * 128
        end = min(at + 128, LOCAL)
        normed_t[:, at:end] = normed[at:end, :].T
        cot_t[:, at:end] = cot[at:end, :].T


def project(p, start, size, cot, w_qkv, w_out, normed, qb, kb, vb, dab):
    rows = pl.ds(start, size)
    base = pl.multiple_of(p * GROUP, GROUP)
    n = normed[rows, :]
    qb[rows, :] = dot(n, w_qkv[:, pl.ds(base, GROUP)]).astype(BF16)
    kb[rows, :] = dot(n, w_qkv[:, pl.ds(base + D, GROUP)]).astype(BF16)
    vb[rows, :] = dot(n, w_qkv[:, pl.ds(base + 2 * D, GROUP)]).astype(BF16)
    dab[rows, :] = dot(cot[rows, :], w_out[pl.ds(base, GROUP), :], NT).astype(BF16)


def attend(p, strips, unroll, bias, qb, kb, vb, dab, ob, d_qkv):
    row_head = lax.broadcasted_iota(jnp.int32, (GROUP, GROUP), 0) // HEAD_DIM
    col_head = lax.broadcasted_iota(jnp.int32, (GROUP, GROUP), 1) // HEAD_DIM
    ones = jnp.where(row_head == col_head, 1.0, 0.0).astype(BF16)

    def strip(s, _):
        rows = pl.ds(pl.multiple_of(s * STRIP, 16), STRIP)
        base = pl.multiple_of(p * GROUP, GROUP)
        q, k = qb[rows, :], kb[rows, :]
        q_squares, k_squares = head_sums(q * q, k * k, ones)
        inv_q = lax.rsqrt(q_squares + EPSILON)
        inv_k = lax.rsqrt(k_squares + EPSILON)
        q_unit = q * inv_q
        k_unit = k * inv_k
        q_heads = by_head(q_unit.astype(BF16))
        k_round = k_unit.astype(BF16)
        v = vb[rows, :]
        da_heads = by_head(dab[rows, :])
        scores = dot(q_heads, k_round, NT).reshape(GROUP_HEADS, STRIP, STRIP)
        weights = jnp.exp2(scores * (SHARP * LOG2E) + bias[s][None])
        total = jnp.sum(weights, axis=-1, keepdims=True)
        probs = weights * (1.0 / total)
        prob_round = probs.astype(BF16).reshape(STACK, STRIP)
        d_probs = dot(da_heads, v, NT).reshape(GROUP_HEADS, STRIP, STRIP)
        mixed = jnp.sum(probs * d_probs, axis=-1, keepdims=True)
        ds_round = (probs * (d_probs - mixed)).astype(BF16).reshape(STACK, STRIP)
        ob[rows, :] = pick_heads(dot(prob_round, v)).astype(BF16)
        d_qkv[rows, pl.ds(base + 2 * D, GROUP)] = dot(prob_round, da_heads, TN).astype(BF16)
        dq_unit = SHARP * pick_heads(dot(ds_round, k_round))
        dk_unit = SHARP * dot(ds_round, q_heads, TN)
        q_along, k_along = head_sums((q_unit * dq_unit).astype(BF16), (k_unit * dk_unit).astype(BF16), ones)
        d_q = inv_q * (dq_unit - q_unit * q_along)
        d_k = inv_k * (dk_unit - k_unit * k_along)
        d_qkv[rows, pl.ds(base, GROUP)] = d_q.astype(BF16)
        d_qkv[rows, pl.ds(base + D, GROUP)] = d_k.astype(BF16)
        return 0

    lax.fori_loop(*strips, strip, 0, unroll=unroll)


def weight_terms(p, half, normed_t, cot_t, d_qkv, ob, terms):
    base = pl.multiple_of(p * GROUP, GROUP)
    for top in range(0, D, 512):
        n = normed_t[top : top + 512, :]
        if half == 0:
            upper = dot(n, d_qkv[:, pl.ds(base, GROUP)])
            lower = dot(n, d_qkv[:, pl.ds(base + D, GROUP)])
        else:
            upper = dot(n, d_qkv[:, pl.ds(base + 2 * D, GROUP)])
            lower = dot(cot_t[top : top + 512, :], ob[...])
        for at in range(0, 512, 8):
            unit = (top + at) // 8
            z, y_lo, core, x, y_hi = unit // 32, unit // 16 % 2, unit // 8 % 2, unit // 2 % 4, unit % 2
            y = y_hi * 2 + y_lo
            both = jnp.concatenate([upper[at : at + 8], lower[at : at + 8]], axis=0).astype(BF16)
            terms[(p, core, half) + ((x, y, z) if half == 0 else (z, y, x))] = both


def normed_grad(start, size, n, w_qkv, d_qkv, d_normed):
    cols = pl.ds(pl.multiple_of(n * 256, 256), 256)
    d_normed[start : start + size, cols] = dot(d_qkv[start : start + size, :], w_qkv[cols, :], NT)


def token_grad(strips, x, inv_rms, d_normed, d_ext):
    def strip(s, _):
        rows = pl.ds(pl.multiple_of(s * STRIP, 16), STRIP)
        xf = x[rows, :].astype(F32)
        dn = d_normed[rows, :]
        inv = inv_rms[rows, :]
        pull = jnp.mean(dn * xf, axis=-1, keepdims=True) * (inv * inv * inv)
        d_ext[pl.ds(pl.multiple_of(s * STRIP + BAND, 16), STRIP), :] = (inv * dn - xf * pull).astype(BF16)
        return 0

    lax.fori_loop(*strips, strip, 0)


def assemble(d_ext, d_next, d_edges, d_tokens):
    is_edge = lax.broadcasted_iota(jnp.int32, (STRIP, 1), 0) % COLS < HALF
    held = jnp.concatenate([d_ext[...].astype(F32), d_next[...].astype(F32)], axis=0)
    for i in range(PLACED):
        s = pl.program_id(0) * PLACED + i
        spread = edge_spread(s, lambda row: row >= HALF, (-HALF * HALF, EDGE + HALF))
        own = held[i * STRIP + 8 : (i + 1) * STRIP + 8]
        d_tokens[i * STRIP : (i + 1) * STRIP, :] = jnp.where(is_edge, dot(spread, d_edges[...]), own).astype(BF16)


def pair_bias(row_valid, bias):
    query = lax.broadcasted_iota(jnp.int32, (STRIP, STRIP), 0)
    key = lax.broadcasted_iota(jnp.int32, (STRIP, STRIP), 1)
    window = lambda t: (t % COLS + COLS - HALF) % COLS // WIN
    half = lambda t: t // (HALF * COLS)
    same_window = window(query) == window(key)
    same_half = half(query) == half(key)
    lat, bands = lax.axis_index("lat"), lax.axis_size("lat")
    open_bias = jnp.where(same_window, -SHARP * LOG2E, BLOCKED)
    seam_bias = jnp.where(same_window & same_half, -SHARP * LOG2E, BLOCKED)
    others = jnp.where(query == key, 0.0, BLOCKED)
    key_row = lax.broadcasted_iota(jnp.int32, (1, STRIP), 1) // COLS
    for s in range(STRIPS):
        base = open_bias if s < STRIPS - 1 else jnp.where(lat == bands - 1, seam_bias, open_bias)
        invalid = jnp.zeros((1, STRIP), F32)
        for i in range(WIN):
            flag = 1.0 - row_valid[(lat * ROWS + s * WIN + i + HALF) % (ROWS * bands)].astype(F32)
            invalid = jnp.where(key_row == i, flag, invalid)
        bias[s] = base + others * invalid


def neighbour(lat_step, lon_step):
    lon, lons = lax.axis_index("lon"), lax.axis_size("lon")
    lat, lats = lax.axis_index("lat"), lax.axis_size("lat")
    return {"lon": (lon + lon_step + lons) % lons, "lat": (lat + lat_step + lats) % lats}


def remote(source, target, send, recv, slot, peer):
    return pltpu.make_async_remote_copy(
        src_ref=source, dst_ref=target, send_sem=send.at[slot], recv_sem=recv.at[slot], device_id=peer, device_id_type=MESH
    )


def window_kernel(
    tokens, cotangent, w_qkv_hbm, w_out_hbm, row_valid, d_ext_hbm, d_edges_hbm, sum_3,
    x_ext, cot_ext, w_qkv, w_out, edge_out, edges, d_ext, d_edge_out, d_corner_out, d_edges,
    bias, x, cot, normed, normed_t, cot_t, inv_rms, qb, kb, vb, dab, ob, d_qkv, d_normed, terms,
    got_0, got_1, sum_1, got_2, sum_2, got_3, send, recv, halo_send, halo_recv, load,
):
    greet()
    loads = [
        pltpu.make_async_copy(tokens, x_ext.at[0:LOCAL], load.at[0]),
        pltpu.make_async_copy(cotangent, cot_ext.at[0:LOCAL], load.at[1]),
        pltpu.make_async_copy(w_qkv_hbm, w_qkv, load.at[2]),
        pltpu.make_async_copy(w_out_hbm, w_out, load.at[3]),
    ]
    for copy in loads:
        copy.start()
    pair_bias(row_valid, bias)
    pick = edge_pick()
    for copy in loads[:2]:
        copy.wait()
    edge_out[0] = dot(pick, x_ext[0:LOCAL, :]).astype(BF16)
    edge_out[1] = dot(pick, cot_ext[0:LOCAL, :]).astype(BF16)
    met()
    up, left, corner = neighbour(-1, 0), neighbour(0, -1), neighbour(-1, -1)
    halos = [
        remote(x_ext.at[0:BAND], x_ext.at[LOCAL : LOCAL + BAND], halo_send, halo_recv, 0, up),
        remote(cot_ext.at[0:BAND], cot_ext.at[LOCAL : LOCAL + BAND], halo_send, halo_recv, 1, up),
        remote(edge_out, edges.at[:, 0:EDGE], halo_send, halo_recv, 2, left),
        remote(edge_out.at[:, 0:16], edges.at[:, EDGE:EDGES], halo_send, halo_recv, 3, corner),
    ]
    halos[2].start()
    halos[3].start()
    halos[0].start()
    halos[1].start()
    halos[2].wait_recv()
    early, late = (0, STRIPS - 1), (STRIPS - 1, STRIPS)
    normalize(early, EDGE, x_ext, cot_ext, edges, x, cot, normed, inv_rms)
    turn(range(5), cot, normed, normed_t, cot_t)
    for copy in loads[2:]:
        copy.wait()
    first = lambda p, half: rs_first(p, half, terms, got_0, got_1, send, recv)
    second = lambda p, half: rs_next(p, half, 0, terms, got_1, sum_1, got_2, send, recv)
    third = lambda p, half: rs_next(p, half, 1, sum_1, got_2, sum_2, got_3, send, recv)
    last = lambda p, half: rs_next(p, half, 2, sum_2, got_3, sum_3, None, send, recv)

    def finish_halo():
        for i in (0, 1, 3):
            halos[i].wait_recv()
        normalize(late, EDGES, x_ext, cot_ext, edges, x, cot, normed, inv_rms)
        turn(range(5, 7), cot, normed, normed_t, cot_t)

    def both_thirds(p):
        third(p, 1)
        third(p, 0)

    def parts(p):
        project(p, 0, EARLY, cot, w_qkv, w_out, normed, qb, kb, vb, dab)
        attend(p, early, 5, bias, qb, kb, vb, dab, ob, d_qkv)
        finish_halo()
        project(p, EARLY, STRIP, cot, w_qkv, w_out, normed, qb, kb, vb, dab)
        attend(p, late, 1, bias, qb, kb, vb, dab, ob, d_qkv)

    def whole(p):
        project(p, 0, LOCAL, cot, w_qkv, w_out, normed, qb, kb, vb, dab)
        first(p - 1, 0)
        attend(p, (0, STRIPS), 6, bias, qb, kb, vb, dab, ob, d_qkv)
        second(p - 1, 1)
        pl.when(p > 1)(lambda: both_thirds(p - 2))

    def chunk(p, _):
        pl.when(p == 0)(lambda: parts(p))
        pl.when(p > 0)(lambda: whole(p))
        weight_terms(p, 1, normed_t, cot_t, d_qkv, ob, terms)
        core_copy(p, 1, terms, got_0, send, recv).start()
        weight_terms(p, 0, normed_t, cot_t, d_qkv, ob, terms)
        core_copy(p, 0, terms, got_0, send, recv).start()
        pl.when(p > 0)(lambda: second(p - 1, 0))
        first(p, 1)
        return 0

    lax.fori_loop(0, CHUNKS, chunk, 0)
    end = CHUNKS - 1
    down, right, far_corner = neighbour(1, 0), neighbour(0, 1), neighbour(1, 1)
    returns = [
        remote(d_ext.at[LOCAL : LOCAL + BAND], d_ext.at[0:BAND], halo_send, halo_recv, 4, down),
        remote(d_edge_out, d_edges.at[0:EDGE], halo_send, halo_recv, 5, right),
        remote(d_corner_out, d_edges.at[EDGE:EDGES], halo_send, halo_recv, 6, far_corner),
    ]
    lax.fori_loop(0, D // 256, lambda n, _: (normed_grad(EARLY, STRIP, n, w_qkv, d_qkv, d_normed), 0)[1], 0)
    first(end, 0)
    token_grad(late, x, inv_rms, d_normed, d_ext)
    d_corner_out[...] = dot(corner_pick(), d_ext[BAND + EARLY : BAND + LOCAL, :]).astype(BF16)
    returns[2].start()
    returns[0].start()
    lax.fori_loop(0, D // 256, lambda n, _: (normed_grad(0, EARLY, n, w_qkv, d_qkv, d_normed), 0)[1], 0)
    both_thirds(end - 1)
    token_grad(early, x, inv_rms, d_normed, d_ext)
    second(end, 1)
    d_edge_out[...] = dot(edge_pick(), d_ext[BAND : BAND + LOCAL, :]).astype(BF16)
    returns[1].start()
    stores = [
        pltpu.make_async_copy(d_ext.at[BAND : BAND + LOCAL], d_ext_hbm.at[BAND : BAND + LOCAL], load.at[0]),
        pltpu.make_async_copy(d_ext.at[0:BAND], d_ext_hbm.at[0:BAND], load.at[1]),
        pltpu.make_async_copy(d_edges, d_edges_hbm, load.at[2]),
    ]
    stores[0].start()
    second(end, 0)

    def settle(p, _):
        last(p, 1)
        last(p, 0)
        rs_finish(p, terms, got_0, (terms, sum_1, sum_2), (got_1, got_2, got_3), send, recv)
        return 0

    lax.fori_loop(0, end, settle, 0)
    third(end, 1)
    for copy in returns:
        copy.wait_recv()
    stores[1].start()
    stores[2].start()
    third(end, 0)
    for copy in halos + returns:
        copy.wait_send()
    settle(end, 0)
    for copy in stores:
        copy.wait()


def place_kernel(d_ext, d_next, d_edges, sum_3, d_tokens, grad_qkv, grad_out):
    assemble(d_ext, d_next, d_edges, d_tokens)
    pl.when(pl.program_id(0) == 0)(lambda: write_grads(sum_3, grad_qkv, grad_out))


def place_call(d_ext, d_edges, sum_3):
    rows = PLACED * STRIP
    return pl.pallas_call(
        place_kernel,
        grid=(STRIPS // PLACED,),
        out_shape=(
            jax.ShapeDtypeStruct((LOCAL, D), BF16),
            jax.ShapeDtypeStruct((8, 3 * D), F32),
            jax.ShapeDtypeStruct((8, D), F32),
        ),
        in_specs=[
            pl.BlockSpec((rows, D), lambda k: (k, 0)),
            pl.BlockSpec((16, D), lambda k: ((k + 1) * (rows // 16), 0)),
            pl.BlockSpec((EDGES, D), lambda k: (0, 0)),
            pl.BlockSpec((CHUNKS, 2, 16, GROUP), lambda k: (0, 0, 0, 0)),
        ],
        out_specs=(
            pl.BlockSpec((rows, D), lambda k: (k, 0)),
            pl.BlockSpec((8, 3 * D), lambda k: (0, 0)),
            pl.BlockSpec((8, D), lambda k: (0, 0)),
        ),
        compiler_params=pltpu.CompilerParams(vmem_limit_bytes=62 * 1024 * 1024),
        name="assembly",
    )(d_ext, d_ext, d_edges, sum_3)


TERMS = (CHUNKS, 2, 2, 4, 4, 4, 16, GROUP)


def window_call(tokens, cotangent, w_qkv, w_out, row_valid):
    vmem = pl.BlockSpec(memory_space=pltpu.VMEM)
    anywhere = pl.BlockSpec(memory_space=pl.ANY)
    return pl.pallas_call(
        window_kernel,
        out_shape=(
            jax.ShapeDtypeStruct((BAND + LOCAL, D), BF16),
            jax.ShapeDtypeStruct((EDGES, D), BF16),
            jax.ShapeDtypeStruct((CHUNKS, 2, 16, GROUP), F32),
        ),
        in_specs=[anywhere] * 4 + [pl.BlockSpec(memory_space=pltpu.SMEM)],
        out_specs=(anywhere, anywhere, vmem),
        scratch_shapes=[
            pltpu.VMEM((LOCAL + BAND, D), BF16),
            pltpu.VMEM((LOCAL + BAND, D), BF16),
            pltpu.VMEM((D, 3 * D), BF16),
            pltpu.VMEM((D, D), BF16),
            pltpu.VMEM((2, EDGE, D), BF16),
            pltpu.VMEM((2, EDGES, D), BF16),
            pltpu.VMEM((BAND + LOCAL, D), BF16),
            pltpu.VMEM((EDGE, D), BF16),
            pltpu.VMEM((16, D), BF16),
            pltpu.VMEM((EDGES, D), BF16),
            pltpu.VMEM((STRIPS, STRIP, STRIP), F32),
            pltpu.VMEM((LOCAL, D), BF16),
            pltpu.VMEM((LOCAL, D), BF16),
            pltpu.VMEM((LOCAL, D), BF16),
            pltpu.VMEM((D, LOCAL), BF16),
            pltpu.VMEM((D, LOCAL), BF16),
            pltpu.VMEM((LOCAL, 1), F32),
            pltpu.VMEM((LOCAL, GROUP), BF16),
            pltpu.VMEM((LOCAL, GROUP), BF16),
            pltpu.VMEM((LOCAL, GROUP), BF16),
            pltpu.VMEM((LOCAL, GROUP), BF16),
            pltpu.VMEM((LOCAL, GROUP), BF16),
            pltpu.VMEM((LOCAL, 3 * D), BF16),
            pltpu.VMEM((LOCAL, D), F32),
            pltpu.VMEM(TERMS, BF16),
        ]
        + scatter_scratch()
        + [pltpu.SemaphoreType.DMA((7,)), pltpu.SemaphoreType.DMA((7,)), pltpu.SemaphoreType.DMA((4,))],
        compiler_params=pltpu.CompilerParams(
            collective_id=0, has_side_effects=True, vmem_limit_bytes=62 * 1024 * 1024
        ),
        name="windows",
    )(tokens, cotangent, w_qkv, w_out, row_valid)


def place():
    lon, lat = lax.axis_index("lon"), lax.axis_index("lat")
    z, y_lo, core = lon // 4, lon // 2 % 2, lon % 2
    x, y_hi = lat // 2, lat % 2
    return x, y_hi * 2 + y_lo, z, core


def device(x, y, z, core):
    return {"lon": z * 4 + y % 2 * 2 + core, "lat": x * 2 + y // 2}


def axis_peer(axis, step):
    x, y, z, core = place()
    if axis == "x":
        at = (x + step) % 4
        return at, device(at, y, z, core)
    if axis == "y":
        at = (y + step) % 4
        return at, device(x, at, z, core)
    at = (z + step) % 4
    return at, device(x, y, at, core)


ORDERS = (("x", "y", "z"), ("z", "y", "x"))


AROUND = ((-1, 0), (0, -1), (-1, -1), (1, 0), (0, 1), (1, 1))


def greet():
    x, y, z, core = place()
    peers = [device(x, y, z, 1 - core)]
    peers += [axis_peer(axis, step)[1] for axis in "xyz" for step in (1, 2, 3)]
    peers += [neighbour(*step) for step in AROUND]
    for peer in peers:
        pl.semaphore_signal(pltpu.get_barrier_semaphore(), inc=1, device_id=peer, device_id_type=MESH)


def met():
    pl.semaphore_wait(pltpu.get_barrier_semaphore(), 10 + len(AROUND))


def core_copy(p, half, terms, got_0, send, recv):
    x, y, z, core = place()
    return pltpu.make_async_remote_copy(
        src_ref=terms.at[p, 1 - core, half],
        dst_ref=got_0.at[p, half],
        send_sem=send.at[p, 0, half],
        recv_sem=recv.at[p, 0, half],
        device_id=device(x, y, z, 1 - core),
        device_id_type=MESH,
    )


def stage_copy(p, stage, half, step, source, target, send, recv):
    at, peer = axis_peer(ORDERS[half][stage], step)
    slot = 3 * half + step - 1
    return pltpu.make_async_remote_copy(
        src_ref=source.at[p, place()[3], half, at] if stage == 0 else source.at[p, half, at],
        dst_ref=target.at[p, half, step - 1],
        send_sem=send.at[p, 1 + stage, slot],
        recv_sem=recv.at[p, 1 + stage, slot],
        device_id=peer,
        device_id_type=MESH,
    )


STEPS = [(half, step) for half in (0, 1) for step in (1, 2, 3)]


def my_index(stage, half):
    x, y, z, _ = place()
    return {"x": x, "y": y, "z": z}[ORDERS[half][stage]]


def rs_first(p, half, terms, got_0, got_1, send, recv):
    core = place()[3]
    core_copy(p, half, terms, got_0, send, recv).wait_recv()
    for a in range(4):
        terms[p, core, half, a] = terms[p, core, half, a] + got_0[p, half, a]
    for step in (2, 1, 3):
        stage_copy(p, 0, half, step, terms, got_1, send, recv).start()


def rs_next(p, half, stage, source, got, total, after, send, recv):
    for step in (1, 2, 3):
        stage_copy(p, stage, half, step, source, got, send, recv).wait_recv()
    index = (half, my_index(stage, half))
    mine = source[(p, place()[3]) + index if stage == 0 else (p,) + index].astype(F32)
    for i in range(3):
        mine = mine + got[p, half, i].astype(F32)
    total[p, half] = mine.astype(total.dtype)
    if after is not None:
        for step in (2, 1, 3):
            stage_copy(p, stage + 1, half, step, total, after, send, recv).start()


def rs_finish(p, terms, got_0, sums, gots, send, recv):
    for half in (0, 1):
        core_copy(p, half, terms, got_0, send, recv).wait_send()
    for stage in range(3):
        for half, step in STEPS:
            stage_copy(p, stage, half, step, sums[stage], gots[stage], send, recv).wait_send()


def write_grads(sum_3, grad_qkv, grad_out):
    scale = 1.0 / math.sqrt(LOCAL * 128)
    for p in range(CHUNKS):
        at = p * GROUP
        grad_qkv[:, at : at + GROUP] = sum_3[p, 0, :8, :] * scale
        grad_qkv[:, D + at : D + at + GROUP] = sum_3[p, 0, 8:, :] * scale
        grad_qkv[:, 2 * D + at : 2 * D + at + GROUP] = sum_3[p, 1, :8, :] * scale
        grad_out[:, at : at + GROUP] = sum_3[p, 1, 8:, :] * scale


def scatter_scratch():
    unit = (16, GROUP)
    return [
        pltpu.VMEM((CHUNKS, 2, 4, 4, 4) + unit, BF16),
        pltpu.VMEM((CHUNKS, 2, 3, 4, 4) + unit, BF16),
        pltpu.VMEM((CHUNKS, 2, 4, 4) + unit, BF16),
        pltpu.VMEM((CHUNKS, 2, 3, 4) + unit, BF16),
        pltpu.VMEM((CHUNKS, 2, 4) + unit, BF16),
        pltpu.VMEM((CHUNKS, 2, 3) + unit, BF16),
        pltpu.SemaphoreType.DMA((CHUNKS, 4, 6)),
        pltpu.SemaphoreType.DMA((CHUNKS, 4, 6)),
    ]


def on_device(tokens, cotangent, w_qkv, w_out, row_valid):
    flat = (LOCAL, D)
    d_tokens, grad_qkv, grad_out = place_call(
        *window_call(tokens.reshape(flat), cotangent.reshape(flat), w_qkv, w_out, row_valid)
    )
    return (d_tokens.reshape(tokens.shape), grad_qkv, grad_out)


def solution(mesh):
    placed = (P("lat", "lon", None), P("lat", "lon", None), P(), P(), P())
    return jax.shard_map(
        on_device,
        mesh=mesh,
        in_specs=placed,
        out_specs=(P("lat", "lon", None), P(("lon", "lat"), None), P(("lon", "lat"), None)),
        check_vma=False,
    )
```

```python
import math

import jax
import jax.numpy as jnp
from jax import lax
from jax.experimental import pallas as pl
from jax.experimental.pallas import tpu as pltpu
from jax.sharding import PartitionSpec as P

D = 1024
HEADS = 16
WIN = 6
HEAD_DIM = 64
HALF = 3
ROWS = 36
COLS = 24
LOCAL = ROWS * COLS
STRIPS = ROWS // WIN
STRIP = WIN * COLS
GROUP = 256
CHUNKS = D // GROUP
GROUP_HEADS = GROUP // HEAD_DIM
STACK = GROUP_HEADS * STRIP
EDGE = 112
EDGES = 128
BAND = 80
PLACED = 2
EARLY = STRIP * (STRIPS - 1)

SHARP = 10.0
LOG2E = math.log2(math.e)
EPSILON = 1e-06
BLOCKED = -1e30

F32 = jnp.float32
BF16 = jnp.bfloat16
MESH = pl.DeviceIdType.MESH
NN = (((1,), (0,)), ((), ()))
NT = (((1,), (1,)), ((), ()))
TN = (((0,), (0,)), ((), ()))


def dot(a, b, dims=NN):
    return lax.dot_general(a, b, dims, preferred_element_type=F32)


def head_sums(a, b, ones):
    both = dot(jnp.concatenate([a, b], axis=0), ones)
    return both[:STRIP], both[STRIP:]


def by_head(t):
    lane = lax.broadcasted_iota(jnp.int32, t.shape, 1) // HEAD_DIM
    zero = jnp.zeros_like(t)
    return jnp.concatenate([jnp.where(lane == h, t, zero) for h in range(GROUP_HEADS)], axis=0)


def pick_heads(t):
    lane = lax.broadcasted_iota(jnp.int32, (STRIP, GROUP), 1) // HEAD_DIM
    out = t[:STRIP]
    for h in range(1, GROUP_HEADS):
        out = jnp.where(lane == h, t[h * STRIP : (h + 1) * STRIP], out)
    return out


def shift_rows(ext, s):
    return ext[pl.ds(pl.multiple_of(s * STRIP + 64, 16), STRIP + 16), :].astype(F32)[8 : 8 + STRIP]


def edge_pick():
    at = lax.broadcasted_iota(jnp.int32, (EDGE, LOCAL), 0)
    token = lax.broadcasted_iota(jnp.int32, (EDGE, LOCAL), 1)
    return jnp.where(token == at // HALF * COLS + at % HALF, 1.0, 0.0).astype(BF16)


def corner_pick():
    at = lax.broadcasted_iota(jnp.int32, (16, STRIP), 0) - HALF
    token = lax.broadcasted_iota(jnp.int32, (16, STRIP), 1)
    source = (HALF + (at + HALF) // HALF - 1) * COLS + (at + HALF) % HALF
    return jnp.where((at >= 0) & (at < HALF * HALF) & (token == source), 1.0, 0.0).astype(BF16)


def edge_spread(s, near, far, width=EDGES):
    token = lax.broadcasted_iota(jnp.int32, (STRIP, width), 0)
    at = lax.broadcasted_iota(jnp.int32, (STRIP, width), 1)
    row, col = s * WIN + token // COLS, token % COLS
    source = jnp.where(near(row), far[0] + HALF * row + col, far[1] + HALF * row + col)
    return jnp.where((col < HALF) & (at == source), 1.0, 0.0).astype(BF16)


def normalize(strips, width, x_ext, cot_ext, edges, x, cot, normed, inv_rms):
    is_edge = lax.broadcasted_iota(jnp.int32, (STRIP, 1), 0) % COLS < HALF

    def norm_strip(s, _):
        rows = pl.ds(pl.multiple_of(s * STRIP, 16), STRIP)
        spread = edge_spread(s, lambda row: row < ROWS - HALF, (HALF * HALF, EDGE - HALF * (ROWS - HALF)), width)
        cot[rows, :] = jnp.where(is_edge, dot(spread, edges[1, 0:width, :]), shift_rows(cot_ext, s)).astype(BF16)
        xf = jnp.where(is_edge, dot(spread, edges[0, 0:width, :]), shift_rows(x_ext, s))
        x[rows, :] = xf.astype(BF16)
        inv = lax.rsqrt(jnp.mean(xf * xf, axis=-1, keepdims=True) + EPSILON)
        inv_rms[rows, :] = inv
        normed[rows, :] = (xf * inv).astype(BF16)
        return 0

    lax.fori_loop(*strips, norm_strip, 0)


def turn(blocks, cot, normed, normed_t, cot_t):
    for block in blocks:
        at = block * 128
        end = min(at + 128, LOCAL)
        normed_t[:, at:end] = normed[at:end, :].T
        cot_t[:, at:end] = cot[at:end, :].T


def project(p, start, size, cot, w_qkv, w_out, normed, qb, kb, vb, dab):
    rows = pl.ds(start, size)
    base = pl.multiple_of(p * GROUP, GROUP)
    n = normed[rows, :]
    qb[rows, :] = dot(n, w_qkv[:, pl.ds(base, GROUP)]).astype(BF16)
    kb[rows, :] = dot(n, w_qkv[:, pl.ds(base + D, GROUP)]).astype(BF16)
    vb[rows, :] = dot(n, w_qkv[:, pl.ds(base + 2 * D, GROUP)]).astype(BF16)
    dab[rows, :] = dot(cot[rows, :], w_out[pl.ds(base, GROUP), :], NT).astype(BF16)


def attend(p, strips, unroll, bias, qb, kb, vb, dab, ob, d_qkv):
    row_head = lax.broadcasted_iota(jnp.int32, (GROUP, GROUP), 0) // HEAD_DIM
    col_head = lax.broadcasted_iota(jnp.int32, (GROUP, GROUP), 1) // HEAD_DIM
    ones = jnp.where(row_head == col_head, 1.0, 0.0).astype(BF16)

    def strip(s, _):
        rows = pl.ds(pl.multiple_of(s * STRIP, 16), STRIP)
        base = pl.multiple_of(p * GROUP, GROUP)
        q, k = qb[rows, :], kb[rows, :]
        q_squares, k_squares = head_sums(q * q, k * k, ones)
        inv_q = lax.rsqrt(q_squares + EPSILON)
        inv_k = lax.rsqrt(k_squares + EPSILON)
        q_unit = q * inv_q
        k_unit = k * inv_k
        q_heads = by_head(q_unit.astype(BF16))
        k_round = k_unit.astype(BF16)
        v = vb[rows, :]
        da_heads = by_head(dab[rows, :])
        scores = dot(q_heads, k_round, NT).reshape(GROUP_HEADS, STRIP, STRIP)
        weights = jnp.exp2(scores * (SHARP * LOG2E) + bias[s][None])
        total = jnp.sum(weights, axis=-1, keepdims=True)
        probs = weights * (1.0 / total)
        prob_round = probs.astype(BF16).reshape(STACK, STRIP)
        d_probs = dot(da_heads, v, NT).reshape(GROUP_HEADS, STRIP, STRIP)
        mixed = jnp.sum(probs * d_probs, axis=-1, keepdims=True)
        ds_round = (probs * (d_probs - mixed)).astype(BF16).reshape(STACK, STRIP)
        ob[rows, :] = pick_heads(dot(prob_round, v)).astype(BF16)
        d_qkv[rows, pl.ds(base + 2 * D, GROUP)] = dot(prob_round, da_heads, TN).astype(BF16)
        dq_unit = SHARP * pick_heads(dot(ds_round, k_round))
        dk_unit = SHARP * dot(ds_round, q_heads, TN)
        q_along, k_along = head_sums((q_unit * dq_unit).astype(BF16), (k_unit * dk_unit).astype(BF16), ones)
        d_q = inv_q * (dq_unit - q_unit * q_along)
        d_k = inv_k * (dk_unit - k_unit * k_along)
        d_qkv[rows, pl.ds(base, GROUP)] = d_q.astype(BF16)
        d_qkv[rows, pl.ds(base + D, GROUP)] = d_k.astype(BF16)
        return 0

    lax.fori_loop(*strips, strip, 0, unroll=unroll)


def weight_terms(p, half, normed_t, cot_t, d_qkv, ob, terms):
    base = pl.multiple_of(p * GROUP, GROUP)
    for top in range(0, D, 512):
        n = normed_t[top : top + 512, :]
        if half == 0:
            upper = dot(n, d_qkv[:, pl.ds(base, GROUP)])
            lower = dot(n, d_qkv[:, pl.ds(base + D, GROUP)])
        else:
            upper = dot(n, d_qkv[:, pl.ds(base + 2 * D, GROUP)])
            lower = dot(cot_t[top : top + 512, :], ob[...])
        for at in range(0, 512, 8):
            unit = (top + at) // 8
            z, y_lo, core, x, y_hi = unit // 32, unit // 16 % 2, unit // 8 % 2, unit // 2 % 4, unit % 2
            y = y_hi * 2 + y_lo
            both = jnp.concatenate([upper[at : at + 8], lower[at : at + 8]], axis=0).astype(BF16)
            terms[(p, core, half) + ((x, y, z) if half == 0 else (z, y, x))] = both


def normed_grad(start, size, n, w_qkv, d_qkv, d_normed):
    cols = pl.ds(pl.multiple_of(n * 256, 256), 256)
    d_normed[start : start + size, cols] = dot(d_qkv[start : start + size, :], w_qkv[cols, :], NT)


def token_grad(strips, x, inv_rms, d_normed, d_ext):
    def strip(s, _):
        rows = pl.ds(pl.multiple_of(s * STRIP, 16), STRIP)
        xf = x[rows, :].astype(F32)
        dn = d_normed[rows, :]
        inv = inv_rms[rows, :]
        pull = jnp.mean(dn * xf, axis=-1, keepdims=True) * (inv * inv * inv)
        d_ext[pl.ds(pl.multiple_of(s * STRIP + BAND, 16), STRIP), :] = (inv * dn - xf * pull).astype(BF16)
        return 0

    lax.fori_loop(*strips, strip, 0)


def assemble(d_ext, d_next, d_edges, d_tokens):
    is_edge = lax.broadcasted_iota(jnp.int32, (STRIP, 1), 0) % COLS < HALF
    held = jnp.concatenate([d_ext[...].astype(F32), d_next[...].astype(F32)], axis=0)
    for i in range(PLACED):
        s = pl.program_id(0) * PLACED + i
        spread = edge_spread(s, lambda row: row >= HALF, (-HALF * HALF, EDGE + HALF))
        own = held[i * STRIP + 8 : (i + 1) * STRIP + 8]
        d_tokens[i * STRIP : (i + 1) * STRIP, :] = jnp.where(is_edge, dot(spread, d_edges[...]), own).astype(BF16)


def pair_bias(row_valid, bias):
    query = lax.broadcasted_iota(jnp.int32, (STRIP, STRIP), 0)
    key = lax.broadcasted_iota(jnp.int32, (STRIP, STRIP), 1)
    window = lambda t: (t % COLS + COLS - HALF) % COLS // WIN
    half = lambda t: t // (HALF * COLS)
    same_window = window(query) == window(key)
    same_half = half(query) == half(key)
    lat, bands = lax.axis_index("lat"), lax.axis_size("lat")
    open_bias = jnp.where(same_window, -SHARP * LOG2E, BLOCKED)
    seam_bias = jnp.where(same_window & same_half, -SHARP * LOG2E, BLOCKED)
    others = jnp.where(query == key, 0.0, BLOCKED)
    key_row = lax.broadcasted_iota(jnp.int32, (1, STRIP), 1) // COLS
    for s in range(STRIPS):
        base = open_bias if s < STRIPS - 1 else jnp.where(lat == bands - 1, seam_bias, open_bias)
        invalid = jnp.zeros((1, STRIP), F32)
        for i in range(WIN):
            flag = 1.0 - row_valid[(lat * ROWS + s * WIN + i + HALF) % (ROWS * bands)].astype(F32)
            invalid = jnp.where(key_row == i, flag, invalid)
        bias[s] = base + others * invalid


def neighbour(lat_step, lon_step):
    lon, lons = lax.axis_index("lon"), lax.axis_size("lon")
    lat, lats = lax.axis_index("lat"), lax.axis_size("lat")
    return {"lon": (lon + lon_step + lons) % lons, "lat": (lat + lat_step + lats) % lats}


def remote(source, target, send, recv, slot, peer):
    return pltpu.make_async_remote_copy(
        src_ref=source, dst_ref=target, send_sem=send.at[slot], recv_sem=recv.at[slot], device_id=peer, device_id_type=MESH
    )


def window_kernel(
    tokens, cotangent, w_qkv_hbm, w_out_hbm, row_valid, d_ext_hbm, d_edges_hbm, sum_3,
    x_ext, cot_ext, w_qkv, w_out, edge_out, edges, d_ext, d_edge_out, d_corner_out, d_edges,
    bias, x, cot, normed, normed_t, cot_t, inv_rms, qb, kb, vb, dab, ob, d_qkv, d_normed, terms,
    got_0, got_1, sum_1, got_2, sum_2, got_3, send, recv, halo_send, halo_recv, load,
):
    greet()
    loads = [
        pltpu.make_async_copy(tokens, x_ext.at[0:LOCAL], load.at[0]),
        pltpu.make_async_copy(cotangent, cot_ext.at[0:LOCAL], load.at[1]),
        pltpu.make_async_copy(w_qkv_hbm, w_qkv, load.at[2]),
        pltpu.make_async_copy(w_out_hbm, w_out, load.at[3]),
    ]
    for copy in loads:
        copy.start()
    pair_bias(row_valid, bias)
    pick = edge_pick()
    for copy in loads[:2]:
        copy.wait()
    edge_out[0] = dot(pick, x_ext[0:LOCAL, :]).astype(BF16)
    edge_out[1] = dot(pick, cot_ext[0:LOCAL, :]).astype(BF16)
    met()
    up, left, corner = neighbour(-1, 0), neighbour(0, -1), neighbour(-1, -1)
    halos = [
        remote(x_ext.at[0:BAND], x_ext.at[LOCAL : LOCAL + BAND], halo_send, halo_recv, 0, up),
        remote(cot_ext.at[0:BAND], cot_ext.at[LOCAL : LOCAL + BAND], halo_send, halo_recv, 1, up),
        remote(edge_out, edges.at[:, 0:EDGE], halo_send, halo_recv, 2, left),
        remote(edge_out.at[:, 0:16], edges.at[:, EDGE:EDGES], halo_send, halo_recv, 3, corner),
    ]
    halos[2].start()
    halos[3].start()
    halos[0].start()
    halos[1].start()
    halos[2].wait_recv()
    early, late = (0, STRIPS - 1), (STRIPS - 1, STRIPS)
    normalize(early, EDGE, x_ext, cot_ext, edges, x, cot, normed, inv_rms)
    turn(range(5), cot, normed, normed_t, cot_t)
    for copy in loads[2:]:
        copy.wait()
    first = lambda p, half: rs_first(p, half, terms, got_0, got_1, send, recv)
    second = lambda p, half: rs_next(p, half, 0, terms, got_1, sum_1, got_2, send, recv)
    third = lambda p, half: rs_next(p, half, 1, sum_1, got_2, sum_2, got_3, send, recv)
    last = lambda p, half: rs_next(p, half, 2, sum_2, got_3, sum_3, None, send, recv)

    def finish_halo():
        for i in (0, 1, 3):
            halos[i].wait_recv()
        normalize(late, EDGES, x_ext, cot_ext, edges, x, cot, normed, inv_rms)
        turn(range(5, 7), cot, normed, normed_t, cot_t)

    def both_thirds(p):
        third(p, 1)
        third(p, 0)

    def parts(p):
        project(p, 0, EARLY, cot, w_qkv, w_out, normed, qb, kb, vb, dab)
        attend(p, early, 5, bias, qb, kb, vb, dab, ob, d_qkv)
        finish_halo()
        project(p, EARLY, STRIP, cot, w_qkv, w_out, normed, qb, kb, vb, dab)
        attend(p, late, 1, bias, qb, kb, vb, dab, ob, d_qkv)

    def whole(p):
        project(p, 0, LOCAL, cot, w_qkv, w_out, normed, qb, kb, vb, dab)
        first(p - 1, 0)
        attend(p, (0, STRIPS), 6, bias, qb, kb, vb, dab, ob, d_qkv)
        second(p - 1, 1)
        pl.when(p > 1)(lambda: both_thirds(p - 2))

    def chunk(p, _):
        pl.when(p == 0)(lambda: parts(p))
        pl.when(p > 0)(lambda: whole(p))
        weight_terms(p, 1, normed_t, cot_t, d_qkv, ob, terms)
        core_copy(p, 1, terms, got_0, send, recv).start()
        weight_terms(p, 0, normed_t, cot_t, d_qkv, ob, terms)
        core_copy(p, 0, terms, got_0, send, recv).start()
        pl.when(p > 0)(lambda: second(p - 1, 0))
        first(p, 1)
        return 0

    lax.fori_loop(0, CHUNKS, chunk, 0)
    end = CHUNKS - 1
    down, right, far_corner = neighbour(1, 0), neighbour(0, 1), neighbour(1, 1)
    returns = [
        remote(d_ext.at[LOCAL : LOCAL + BAND], d_ext.at[0:BAND], halo_send, halo_recv, 4, down),
        remote(d_edge_out, d_edges.at[0:EDGE], halo_send, halo_recv, 5, right),
        remote(d_corner_out, d_edges.at[EDGE:EDGES], halo_send, halo_recv, 6, far_corner),
    ]
    lax.fori_loop(0, D // 256, lambda n, _: (normed_grad(EARLY, STRIP, n, w_qkv, d_qkv, d_normed), 0)[1], 0)
    first(end, 0)
    token_grad(late, x, inv_rms, d_normed, d_ext)
    d_corner_out[...] = dot(corner_pick(), d_ext[BAND + EARLY : BAND + LOCAL, :]).astype(BF16)
    returns[2].start()
    returns[0].start()
    lax.fori_loop(0, D // 256, lambda n, _: (normed_grad(0, EARLY, n, w_qkv, d_qkv, d_normed), 0)[1], 0)
    both_thirds(end - 1)
    second(end, 1)
    token_grad(early, x, inv_rms, d_normed, d_ext)
    d_edge_out[...] = dot(edge_pick(), d_ext[BAND : BAND + LOCAL, :]).astype(BF16)
    returns[1].start()
    stores = [
        pltpu.make_async_copy(d_ext.at[BAND : BAND + LOCAL], d_ext_hbm.at[BAND : BAND + LOCAL], load.at[0]),
        pltpu.make_async_copy(d_ext.at[0:BAND], d_ext_hbm.at[0:BAND], load.at[1]),
        pltpu.make_async_copy(d_edges, d_edges_hbm, load.at[2]),
    ]
    stores[0].start()
    second(end, 0)

    def settle(p, _):
        last(p, 1)
        last(p, 0)
        rs_finish(p, terms, got_0, (terms, sum_1, sum_2), (got_1, got_2, got_3), send, recv)
        return 0

    lax.fori_loop(0, end, settle, 0)
    third(end, 1)
    for copy in returns:
        copy.wait_recv()
    stores[1].start()
    stores[2].start()
    third(end, 0)
    for copy in halos + returns:
        copy.wait_send()
    settle(end, 0)
    for copy in stores:
        copy.wait()


def place_kernel(d_ext, d_next, d_edges, sum_3, d_tokens, grad_qkv, grad_out):
    assemble(d_ext, d_next, d_edges, d_tokens)
    pl.when(pl.program_id(0) == 0)(lambda: write_grads(sum_3, grad_qkv, grad_out))


def place_call(d_ext, d_edges, sum_3):
    rows = PLACED * STRIP
    return pl.pallas_call(
        place_kernel,
        grid=(STRIPS // PLACED,),
        out_shape=(
            jax.ShapeDtypeStruct((LOCAL, D), BF16),
            jax.ShapeDtypeStruct((8, 3 * D), F32),
            jax.ShapeDtypeStruct((8, D), F32),
        ),
        in_specs=[
            pl.BlockSpec((rows, D), lambda k: (k, 0)),
            pl.BlockSpec((16, D), lambda k: ((k + 1) * (rows // 16), 0)),
            pl.BlockSpec((EDGES, D), lambda k: (0, 0)),
            pl.BlockSpec((CHUNKS, 2, 16, GROUP), lambda k: (0, 0, 0, 0)),
        ],
        out_specs=(
            pl.BlockSpec((rows, D), lambda k: (k, 0)),
            pl.BlockSpec((8, 3 * D), lambda k: (0, 0)),
            pl.BlockSpec((8, D), lambda k: (0, 0)),
        ),
        compiler_params=pltpu.CompilerParams(vmem_limit_bytes=62 * 1024 * 1024),
        name="assembly",
    )(d_ext, d_ext, d_edges, sum_3)


TERMS = (CHUNKS, 2, 2, 4, 4, 4, 16, GROUP)


def window_call(tokens, cotangent, w_qkv, w_out, row_valid):
    vmem = pl.BlockSpec(memory_space=pltpu.VMEM)
    anywhere = pl.BlockSpec(memory_space=pl.ANY)
    return pl.pallas_call(
        window_kernel,
        out_shape=(
            jax.ShapeDtypeStruct((BAND + LOCAL, D), BF16),
            jax.ShapeDtypeStruct((EDGES, D), BF16),
            jax.ShapeDtypeStruct((CHUNKS, 2, 16, GROUP), F32),
        ),
        in_specs=[anywhere] * 4 + [pl.BlockSpec(memory_space=pltpu.SMEM)],
        out_specs=(anywhere, anywhere, vmem),
        scratch_shapes=[
            pltpu.VMEM((LOCAL + BAND, D), BF16),
            pltpu.VMEM((LOCAL + BAND, D), BF16),
            pltpu.VMEM((D, 3 * D), BF16),
            pltpu.VMEM((D, D), BF16),
            pltpu.VMEM((2, EDGE, D), BF16),
            pltpu.VMEM((2, EDGES, D), BF16),
            pltpu.VMEM((BAND + LOCAL, D), BF16),
            pltpu.VMEM((EDGE, D), BF16),
            pltpu.VMEM((16, D), BF16),
            pltpu.VMEM((EDGES, D), BF16),
            pltpu.VMEM((STRIPS, STRIP, STRIP), F32),
            pltpu.VMEM((LOCAL, D), BF16),
            pltpu.VMEM((LOCAL, D), BF16),
            pltpu.VMEM((LOCAL, D), BF16),
            pltpu.VMEM((D, LOCAL), BF16),
            pltpu.VMEM((D, LOCAL), BF16),
            pltpu.VMEM((LOCAL, 1), F32),
            pltpu.VMEM((LOCAL, GROUP), BF16),
            pltpu.VMEM((LOCAL, GROUP), BF16),
            pltpu.VMEM((LOCAL, GROUP), BF16),
            pltpu.VMEM((LOCAL, GROUP), BF16),
            pltpu.VMEM((LOCAL, GROUP), BF16),
            pltpu.VMEM((LOCAL, 3 * D), BF16),
            pltpu.VMEM((LOCAL, D), F32),
            pltpu.VMEM(TERMS, BF16),
        ]
        + scatter_scratch()
        + [pltpu.SemaphoreType.DMA((7,)), pltpu.SemaphoreType.DMA((7,)), pltpu.SemaphoreType.DMA((4,))],
        compiler_params=pltpu.CompilerParams(
            collective_id=0, has_side_effects=True, vmem_limit_bytes=62 * 1024 * 1024
        ),
        name="windows",
    )(tokens, cotangent, w_qkv, w_out, row_valid)


def place():
    lon, lat = lax.axis_index("lon"), lax.axis_index("lat")
    z, y_lo, core = lon // 4, lon // 2 % 2, lon % 2
    x, y_hi = lat // 2, lat % 2
    return x, y_hi * 2 + y_lo, z, core


def device(x, y, z, core):
    return {"lon": z * 4 + y % 2 * 2 + core, "lat": x * 2 + y // 2}


def axis_peer(axis, step):
    x, y, z, core = place()
    if axis == "x":
        at = (x + step) % 4
        return at, device(at, y, z, core)
    if axis == "y":
        at = (y + step) % 4
        return at, device(x, at, z, core)
    at = (z + step) % 4
    return at, device(x, y, at, core)


ORDERS = (("x", "y", "z"), ("z", "y", "x"))


AROUND = ((-1, 0), (0, -1), (-1, -1), (1, 0), (0, 1), (1, 1))


def greet():
    x, y, z, core = place()
    peers = [device(x, y, z, 1 - core)]
    peers += [axis_peer(axis, step)[1] for axis in "xyz" for step in (1, 2, 3)]
    peers += [neighbour(*step) for step in AROUND]
    for peer in peers:
        pl.semaphore_signal(pltpu.get_barrier_semaphore(), inc=1, device_id=peer, device_id_type=MESH)


def met():
    pl.semaphore_wait(pltpu.get_barrier_semaphore(), 10 + len(AROUND))


def core_copy(p, half, terms, got_0, send, recv):
    x, y, z, core = place()
    return pltpu.make_async_remote_copy(
        src_ref=terms.at[p, 1 - core, half],
        dst_ref=got_0.at[p, half],
        send_sem=send.at[p, 0, half],
        recv_sem=recv.at[p, 0, half],
        device_id=device(x, y, z, 1 - core),
        device_id_type=MESH,
    )


def stage_copy(p, stage, half, step, source, target, send, recv):
    at, peer = axis_peer(ORDERS[half][stage], step)
    slot = 3 * half + step - 1
    return pltpu.make_async_remote_copy(
        src_ref=source.at[p, place()[3], half, at] if stage == 0 else source.at[p, half, at],
        dst_ref=target.at[p, half, step - 1],
        send_sem=send.at[p, 1 + stage, slot],
        recv_sem=recv.at[p, 1 + stage, slot],
        device_id=peer,
        device_id_type=MESH,
    )


STEPS = [(half, step) for half in (0, 1) for step in (1, 2, 3)]


def my_index(stage, half):
    x, y, z, _ = place()
    return {"x": x, "y": y, "z": z}[ORDERS[half][stage]]


def rs_first(p, half, terms, got_0, got_1, send, recv):
    core = place()[3]
    core_copy(p, half, terms, got_0, send, recv).wait_recv()
    for a in range(4):
        terms[p, core, half, a] = terms[p, core, half, a] + got_0[p, half, a]
    for step in (2, 1, 3):
        stage_copy(p, 0, half, step, terms, got_1, send, recv).start()


def rs_next(p, half, stage, source, got, total, after, send, recv):
    for step in (1, 2, 3):
        stage_copy(p, stage, half, step, source, got, send, recv).wait_recv()
    index = (half, my_index(stage, half))
    mine = source[(p, place()[3]) + index if stage == 0 else (p,) + index].astype(F32)
    for i in range(3):
        mine = mine + got[p, half, i].astype(F32)
    total[p, half] = mine.astype(total.dtype)
    if after is not None:
        for step in (2, 1, 3):
            stage_copy(p, stage + 1, half, step, total, after, send, recv).start()


def rs_finish(p, terms, got_0, sums, gots, send, recv):
    for half in (0, 1):
        core_copy(p, half, terms, got_0, send, recv).wait_send()
    for stage in range(3):
        for half, step in STEPS:
            stage_copy(p, stage, half, step, sums[stage], gots[stage], send, recv).wait_send()


def write_grads(sum_3, grad_qkv, grad_out):
    scale = 1.0 / math.sqrt(LOCAL * 128)
    for p in range(CHUNKS):
        at = p * GROUP
        grad_qkv[:, at : at + GROUP] = sum_3[p, 0, :8, :] * scale
        grad_qkv[:, D + at : D + at + GROUP] = sum_3[p, 0, 8:, :] * scale
        grad_qkv[:, 2 * D + at : 2 * D + at + GROUP] = sum_3[p, 1, :8, :] * scale
        grad_out[:, at : at + GROUP] = sum_3[p, 1, 8:, :] * scale


def scatter_scratch():
    unit = (16, GROUP)
    return [
        pltpu.VMEM((CHUNKS, 2, 4, 4, 4) + unit, BF16),
        pltpu.VMEM((CHUNKS, 2, 3, 4, 4) + unit, BF16),
        pltpu.VMEM((CHUNKS, 2, 4, 4) + unit, BF16),
        pltpu.VMEM((CHUNKS, 2, 3, 4) + unit, BF16),
        pltpu.VMEM((CHUNKS, 2, 4) + unit, BF16),
        pltpu.VMEM((CHUNKS, 2, 3) + unit, BF16),
        pltpu.SemaphoreType.DMA((CHUNKS, 4, 6)),
        pltpu.SemaphoreType.DMA((CHUNKS, 4, 6)),
    ]


def on_device(tokens, cotangent, w_qkv, w_out, row_valid):
    flat = (LOCAL, D)
    d_tokens, grad_qkv, grad_out = place_call(
        *window_call(tokens.reshape(flat), cotangent.reshape(flat), w_qkv, w_out, row_valid)
    )
    return (d_tokens.reshape(tokens.shape), grad_qkv, grad_out)


def solution(mesh):
    placed = (P("lat", "lon", None), P("lat", "lon", None), P(), P(), P())
    return jax.shard_map(
        on_device,
        mesh=mesh,
        in_specs=placed,
        out_specs=(P("lat", "lon", None), P(("lon", "lat"), None), P(("lon", "lat"), None)),
        check_vma=False,
    )
```
